32 devices in a mesh: lat: 4 (over x, core), lon: 8 (over z, y).
Axes of the slice: x: 2, y: 2, z: 4, core: 2. Of those that a mesh axis runs over, the one named last changes fastest.
Arguments:
- queries: bfloat16 [64, 128, 1280], P('lat', 'lon'), may hold values from -8 to 8
- key_field: bfloat16 [64, 128, 1280], P('lat', 'lon'), may hold values from -8 to 8
- value_field: bfloat16 [64, 128, 1280], P('lat', 'lon'), may hold values from -6 to 6
- out_grad: bfloat16 [64, 128, 1280], P('lat', 'lon'), may hold values from -6 to 6
Outputs:
- grad_query: bfloat16 [64, 128, 1280], P('lat', 'lon')
- grad_key: bfloat16 [64, 128, 1280], P('lat', 'lon')
- grad_value: bfloat16 [64, 128, 1280], P('lat', 'lon')
The draws below stay inside these ranges and needn't reach their ends.
All inputs are finite; a program needn't handle non-finite values.
Results may differ from the reference program's by a relative error of at most 0.012.
Values may be sent and summed in bfloat16 or wider, within the bound.
No kernel may reach another device: no remote copies, remote signals or barrier semaphores. Data moves between devices by JAX's collectives and lax.ppermute only.
A program may use at most 128 MiB of HBM per device.

```python
import math
import jax
import jax.numpy as jnp
from jax import lax

HEADS = 10
HEAD_DIM = 128
WINDOW = 13
NLAT = 64
NLON = 128


def draw_queries(key, part):
    values = jax.random.truncated_normal(jax.random.fold_in(key, 1), -6.0, 6.0, (NLAT, NLON, HEADS * HEAD_DIM), jnp.float32)
    return values.astype(jnp.bfloat16)


def draw_key_field(key, part):
    values = jax.random.truncated_normal(jax.random.fold_in(key, 2), -6.0, 6.0, (NLAT, NLON, HEADS * HEAD_DIM), jnp.float32)
    return values.astype(jnp.bfloat16)


def level_of(own_key, extent, split, least, largest):
    def one(position, blocks):
        steps = jax.random.uniform(jax.random.fold_in(jax.random.fold_in(own_key, 6), position), (blocks,), jnp.float32, least / len(split), largest / len(split))
        return jnp.repeat(jnp.exp(steps), extent[position] // blocks).reshape((-1,) + (1,) * (len(extent) - position - 1))

    level = one(*split[0])
    for cut in split[1:]:
        level = level * one(*cut)
    return level


def centred(own_key, dims, scale, limit, pieces=(), kind=jnp.bfloat16):
    entries = jax.random.normal(own_key, dims, jnp.float32) * scale
    if len(pieces) > 0:
        entries = level_of(own_key, dims, pieces, -0.22, 0.18) * entries
    return jnp.clip(entries, min=-limit, max=limit).astype(kind)


def setup_inputs(seed: int = 0) -> dict:
    arg_keys = jax.random.split(jax.random.key(seed), 5)
    return {
        "queries": draw_queries(jax.random.fold_in(arg_keys[4], 71), 0),
        "key_field": draw_key_field(jax.random.fold_in(arg_keys[4], 71), 0),
        "value_field": centred(arg_keys[2], (NLAT, NLON, HEADS * HEAD_DIM), 1.0, 6.0, ((0, 4), (1, 8))),
        "out_grad": centred(arg_keys[3], (NLAT, NLON, HEADS * HEAD_DIM), 1.0, 6.0, ((0, 4), (1, 8))),
    }


def by_heads(tensor):
    return tensor.astype(jnp.float32).reshape(tensor.shape[:-1] + (HEADS, HEAD_DIM))

def wrap_band(tensor, radius):
    return jnp.concatenate([tensor[:, NLON - radius:], tensor, tensor[:, :radius]], axis=1)

def fold_band(band, radius):
    middle = band[:, radius:radius + NLON]
    middle = middle.at[:, NLON - radius:].add(band[:, :radius])
    middle = middle.at[:, :radius].add(band[:, NLON + radius:])
    return middle.reshape((WINDOW, NLON, HEADS * HEAD_DIM))

def low_copy(tensor):
    return lax.optimization_barrier(tensor.astype(jnp.bfloat16)).astype(jnp.float32)

def reference(queries, key_field, value_field, out_grad):
    radius = WINDOW // 2
    score_scale = 1.0 / math.sqrt(HEAD_DIM)
    feat_width = HEADS * HEAD_DIM

    def row_step(running, row_now):
        key_acc, value_acc = running
        first_row = jnp.clip(row_now - radius, 0, NLAT - WINDOW).astype(jnp.int32)
        query_row = by_heads(lax.dynamic_index_in_dim(queries, row_now, 0, keepdims=False))
        grad_row = by_heads(lax.dynamic_index_in_dim(out_grad, row_now, 0, keepdims=False))
        key_band = wrap_band(by_heads(lax.dynamic_slice_in_dim(key_field, first_row, WINDOW, 0)), radius)
        value_band = wrap_band(by_heads(lax.dynamic_slice_in_dim(value_field, first_row, WINDOW, 0)), radius)
        scores = jnp.stack([jnp.einsum('chd,wchd->wch', query_row, key_band[:, column:column + NLON]) for column in range(WINDOW)], axis=1) * score_scale
        row_peak = lax.optimization_barrier(jnp.max(scores, axis=(0, 1)))
        log_total = row_peak + jnp.log(lax.optimization_barrier(jnp.sum(jnp.exp(scores - row_peak), axis=(0, 1))))
        weights = jnp.exp(scores - log_total)
        low_weights = low_copy(weights)
        attended = jnp.zeros((NLON, HEADS, HEAD_DIM), jnp.float32)
        for column in range(WINDOW):
            attended = attended + jnp.einsum('wch,wchd->chd', low_weights[:, column], value_band[:, column:column + NLON])
        row_delta = lax.optimization_barrier(jnp.sum(grad_row * attended, axis=-1))
        weight_grad = jnp.stack([jnp.einsum('chd,wchd->wch', grad_row, value_band[:, column:column + NLON]) for column in range(WINDOW)], axis=1)
        score_grad = low_copy(weights * (weight_grad - row_delta))
        query_grad = jnp.zeros((NLON, HEADS, HEAD_DIM), jnp.float32)
        key_part = jnp.zeros((WINDOW, NLON + 2 * radius, HEADS, HEAD_DIM), jnp.float32)
        value_part = jnp.zeros((WINDOW, NLON + 2 * radius, HEADS, HEAD_DIM), jnp.float32)
        for column in range(WINDOW):
            query_grad = query_grad + jnp.einsum('wch,wchd->chd', score_grad[:, column], key_band[:, column:column + NLON])
            key_part = key_part.at[:, column:column + NLON].add(jnp.einsum('wch,chd->wchd', score_grad[:, column], query_row))
            value_part = value_part.at[:, column:column + NLON].add(jnp.einsum('wch,chd->wchd', low_weights[:, column], grad_row))
        query_grad = (query_grad * score_scale).reshape((NLON, feat_width)).astype(jnp.bfloat16)
        key_now = lax.dynamic_slice_in_dim(key_acc, first_row, WINDOW, 0) + fold_band(key_part, radius) * score_scale
        key_acc = lax.dynamic_update_slice_in_dim(key_acc, key_now, first_row, 0)
        value_now = lax.dynamic_slice_in_dim(value_acc, first_row, WINDOW, 0) + fold_band(value_part, radius)
        value_acc = lax.dynamic_update_slice_in_dim(value_acc, value_now, first_row, 0)
        return ((key_acc, value_acc), query_grad)
    zeroed = jnp.zeros((NLAT, NLON, feat_width), jnp.float32)
    (key_acc, value_acc), grad_query = lax.scan(row_step, (zeroed, zeroed), jnp.arange(NLAT, dtype=jnp.int32))
    return (grad_query, key_acc.astype(jnp.bfloat16), value_acc.astype(jnp.bfloat16))
```

```python
import functools
import math

import jax
import jax.numpy as jnp
from jax import lax
from jax.experimental import pallas as pl
from jax.experimental.pallas import tpu as pltpu
from jax.sharding import PartitionSpec as P

HEAD_DIM = 128
WINDOW = 13
RADIUS = WINDOW // 2
CHUNKS = (10,)
LANES = 128
MASKED = -1e30
LOG2E = math.log2(math.e)
VMEM_BYTES = 40 * 1024 * 1024


def split(index, width):
    if width & (width - 1) == 0:
        whole = index >> (width.bit_length() - 1)
    else:
        whole = (index * ((1 << 12) // width + 1)) >> 12
    return whole, index - whole * width


def odd(axis):
    return lax.axis_index(axis) & 1


def slot_side(axis, slot):
    parity = odd(axis)
    return 1 - parity if slot == 0 else parity


def own_query_cell(position, rows, cols):
    edge = rows * RADIUS
    group = position >> 7
    place = position & (LANES - 1)
    side = jnp.where(group == 0, slot_side("lon", 0), slot_side("lon", 1))
    row_a, col_a = split(place, RADIUS)
    inner = cols - 2 * RADIUS
    row_b, col_b = split(place - edge + (LANES - edge) * group, inner)
    at_edge = place < edge
    row = jnp.where(at_edge, row_a, row_b)
    col = jnp.where(at_edge, side * (cols - RADIUS) + col_a, RADIUS + col_b)
    return row, col


def halo_query_cell(position, rows, cols):
    edge = rows * RADIUS
    group = position >> 7
    place = position & (LANES - 1)
    side = jnp.where(group == 0, slot_side("lon", 0), slot_side("lon", 1))
    row, col = split(place, RADIUS)
    col = jnp.where(side == 1, cols, -RADIUS) + col
    col = jnp.where(place < edge, col, 1 << 12)
    return row, col


def key_cell(position, rows, cols):
    own = rows * cols
    edge = RADIUS * cols
    row, col = split(position, cols)
    row_0 = row - rows + jnp.where(slot_side("lat", 0) == 1, rows, -RADIUS)
    row_1 = row - rows - RADIUS + jnp.where(slot_side("lat", 1) == 1, rows, -RADIUS)
    row = jnp.where(position < own, row, jnp.where(position < own + edge, row_0, row_1))
    return row, col


def bias_of(kind, rows, cols):
    total_rows = rows * lax.axis_size("lat")
    first = rows * lax.axis_index("lat")
    keys = rows * cols + 2 * RADIUS * cols
    key_row, key_col = key_cell(lax.broadcasted_iota(jnp.int32, (keys, 1), 0), rows, cols)
    query_row, query_col = kind(lax.broadcasted_iota(jnp.int32, (1, 2 * LANES), 1), rows, cols)
    start = jnp.clip(first + query_row - RADIUS, 0, total_rows - WINDOW)
    from_start = first + key_row - start
    inside = (from_start >= 0) & (from_start < WINDOW)
    inside = inside & (jnp.abs(key_col - query_col) <= RADIUS)
    return jnp.where(inside, 0.0, MASKED)


def dot(a, b, contract):
    return lax.dot_general(a, b, ((contract[:1], contract[1:]), ((), ())), preferred_element_type=jnp.float32)


def call(kernel, name, grid, ins, outs, out_shapes, scratch=(), flops=0, aliases=None):
    return pl.pallas_call(
        kernel,
        name=name,
        grid=(grid,),
        in_specs=ins,
        out_specs=outs,
        out_shape=out_shapes,
        scratch_shapes=scratch,
        input_output_aliases=aliases or {},
        compiler_params=pltpu.CompilerParams(
            dimension_semantics=("arbitrary",), vmem_limit_bytes=VMEM_BYTES
        ),
        cost_estimate=pl.CostEstimate(flops=flops, bytes_accessed=1 << 20, transcendentals=0),
    )


def heads_of(rows, first=0):
    return pl.BlockSpec((rows, HEAD_DIM), lambda i: (0, first + i))


def whole(shape):
    return pl.BlockSpec(shape, lambda i: (0,) * len(shape))


def pack_queries(queries, out_grad, rows, cols, first, count):
    own, edge = rows * cols, rows * RADIUS

    def kernel(q_ref, g_ref, qp_ref, gp_ref, send_0, send_1, order):
        @pl.when(pl.program_id(0) == 0)
        def _():
            row, col = own_query_cell(lax.broadcasted_iota(jnp.int32, (own, 1), 0), rows, cols)
            source = lax.broadcasted_iota(jnp.int32, (own, own), 1)
            order[...] = jnp.where(source == row * cols + col, 1.0, 0.0).astype(jnp.bfloat16)

        for place, (src, dst) in enumerate(((q_ref, qp_ref), (g_ref, gp_ref))):
            moved = dot(order[...], src[...], (1, 0)).astype(jnp.bfloat16)
            dst[...] = moved
            for group, send in enumerate((send_0, send_1)):
                send[place * edge : (place + 1) * edge, :] = moved[group * LANES : group * LANES + edge]

    width = count * HEAD_DIM
    shape = lambda n: jax.ShapeDtypeStruct((n, width), jnp.bfloat16)
    return call(
        kernel, "pack_queries", count,
        [heads_of(own, first)] * 2,
        [heads_of(own)] * 2 + [heads_of(2 * edge)] * 2,
        [shape(own)] * 2 + [shape(2 * edge)] * 2,
        [pltpu.VMEM((own, own), jnp.bfloat16)],
        flops=1 << 28,
    )(queries, out_grad)


def pack_keys(key_field, value_field, rows, cols):
    own, edge = rows * cols, RADIUS * cols

    def kernel(k_ref, v_ref, send_0, send_1):
        for slot, send in enumerate((send_0, send_1)):
            start = pl.multiple_of(slot_side("lat", slot) * (own - edge), 16)
            send[:edge, :] = k_ref[pl.ds(start, edge), :]
            send[edge:, :] = v_ref[pl.ds(start, edge), :]

    width = key_field.shape[1]
    block = 2 * HEAD_DIM
    spec = lambda n: pl.BlockSpec((n, block), lambda i: (0, i))
    return call(
        kernel, "pack_keys", width // block,
        [spec(own)] * 2, [spec(2 * edge)] * 2,
        [jax.ShapeDtypeStruct((2 * edge, width), jnp.bfloat16)] * 2,
        flops=1 << 28,
    )(key_field, value_field)


def padded(first, second, edge):
    gap = jnp.zeros((LANES - edge, HEAD_DIM), jnp.bfloat16)
    return jnp.concatenate([first, gap, second, gap], axis=0)


def halo_heads(ref_0, ref_1, edge, part):
    piece = slice(part * edge, (part + 1) * edge)
    return padded(ref_0[piece, :], ref_1[piece, :], edge)


def key_heads(own_ref, ref_0, ref_1, edge, part):
    piece = slice(part * edge, (part + 1) * edge)
    return jnp.concatenate([own_ref[...], ref_0[piece, :], ref_1[piece, :]], axis=0)


SCORE_SCALE = 1.0 / math.sqrt(HEAD_DIM)


def part_stats(keys, values, queries, grads, bias):
    scores = dot(keys, queries, (1, 1)) * (SCORE_SCALE * LOG2E) + bias
    peak = jnp.max(scores, axis=0, keepdims=True)
    weights = jnp.exp2(scores - peak)
    total = jnp.sum(weights, axis=0, keepdims=True)
    weight_grad = dot(values, grads, (1, 1))
    dotted = jnp.sum(weights * weight_grad, axis=0, keepdims=True)
    return peak + jnp.log(total) * LOG2E, dotted / total


def put_row(ref, lanes, row, value):
    here = lax.broadcasted_iota(jnp.int32, (ref.shape[0], 1), 0) == row
    ref[:, lanes] = jnp.where(here, value, ref[:, lanes])


def stat_rows(count):
    return -(-2 * count // 8) * 8


def own_stats(qp, gp, keys, values, lat_0, lat_1, rows, cols, first, count):
    own, edge = rows * cols, RADIUS * cols

    def kernel(q_ref, g_ref, k_ref, v_ref, lat_0, lat_1, out, bias):
        head = pl.program_id(0)

        @pl.when(head == 0)
        def _():
            bias[...] = bias_of(own_query_cell, rows, cols)
            out[...] = jnp.zeros_like(out)

        log_total, delta = part_stats(
            key_heads(k_ref, lat_0, lat_1, edge, 0), key_heads(v_ref, lat_0, lat_1, edge, 1),
            q_ref[...], g_ref[...], bias[...],
        )
        put_row(out, slice(None), head, log_total)
        put_row(out, slice(None), count + head, delta)

    shape = (stat_rows(count), own)
    return call(
        kernel, "own_stats", count,
        [heads_of(own)] * 2 + [heads_of(own, first)] * 2 + [heads_of(2 * edge, first)] * 2,
        whole(shape), jax.ShapeDtypeStruct(shape, jnp.float32),
        [pltpu.VMEM((own + 2 * edge, own), jnp.float32)],
        flops=1 << 30,
    )(qp, gp, keys, values, lat_0, lat_1)


def halo_stats(halo_0, halo_1, own_stat, keys, values, lat_0, lat_1, rows, cols, first, count):
    own, edge = rows * cols, RADIUS * cols
    lon_edge = RADIUS * rows

    def kernel(h_0, h_1, stat, k_ref, v_ref, lat_0, lat_1, out_0, out_1, bias):
        head = pl.program_id(0)

        @pl.when(head == 0)
        def _():
            bias[...] = bias_of(halo_query_cell, rows, cols)
            for group, out in enumerate((out_0, out_1)):
                out[:, :LANES] = stat[:, group * LANES : (group + 1) * LANES]
                out[:, LANES:] = jnp.zeros((out.shape[0], LANES), jnp.float32)

        log_total, delta = part_stats(
            key_heads(k_ref, lat_0, lat_1, edge, 0), key_heads(v_ref, lat_0, lat_1, edge, 1),
            halo_heads(h_0, h_1, lon_edge, 0), halo_heads(h_0, h_1, lon_edge, 1), bias[...],
        )
        for group, out in enumerate((out_0, out_1)):
            lanes = slice(group * LANES, (group + 1) * LANES)
            put_row(out, slice(LANES, None), head, log_total[:, lanes])
            put_row(out, slice(LANES, None), count + head, delta[:, lanes])

    shape = (stat_rows(count), 2 * LANES)
    return call(
        kernel, "halo_stats", count,
        [heads_of(2 * lon_edge)] * 2 + [whole(own_stat.shape)] + [heads_of(own, first)] * 2
        + [heads_of(2 * edge, first)] * 2,
        [whole(shape)] * 2, [jax.ShapeDtypeStruct(shape, jnp.float32)] * 2,
        [pltpu.VMEM((own + 2 * edge, 2 * LANES), jnp.float32)],
        flops=1 << 30,
    )(halo_0, halo_1, own_stat, keys, values, lat_0, lat_1)


def combined(mine, theirs, count):
    a, b = mine[:count], theirs[:count]
    peak = jnp.maximum(a, b)
    part_a, part_b = jnp.exp2(a - peak), jnp.exp2(b - peak)
    total = part_a + part_b
    delta = (part_a * mine[count : 2 * count] + part_b * theirs[count : 2 * count]) / total
    return peak + jnp.log(total) * LOG2E, delta


def fill_combined(mine, theirs, mine_half, log_ref, delta_ref, at, count):
    for group, (a, b) in enumerate(zip(mine, theirs)):
        low, high = slice(0, LANES), slice(LANES, 2 * LANES)
        own_half, other_half = (low, high) if mine_half == 0 else (high, low)
        log_total, delta = combined(a[:, own_half], b[:, other_half], count)
        lanes = slice(at + group * LANES, at + (group + 1) * LANES)
        log_ref[:count, lanes] = log_total
        delta_ref[:count, lanes] = delta


def gradients(keys, values, queries, grads, bias, log_total, delta):
    scores = dot(keys, queries, (1, 1)) * (SCORE_SCALE * LOG2E) + bias
    weights = jnp.exp2(scores - log_total)
    weight_grad = dot(values, grads, (1, 1))
    low_grad = (weights * (weight_grad - delta)).astype(jnp.bfloat16)
    return weights.astype(jnp.bfloat16), low_grad


def halo_query_grad(halo_0, halo_1, mine, theirs, keys, values, lat_0, lat_1, rows, cols, first, count):
    own, edge = rows * cols, RADIUS * cols
    lon_edge = RADIUS * rows

    def kernel(h_0, h_1, m_0, m_1, t_0, t_1, k_ref, v_ref, lat_0, lat_1, out_0, out_1, bias, logs, deltas):
        head = pl.program_id(0)

        @pl.when(head == 0)
        def _():
            bias[...] = bias_of(halo_query_cell, rows, cols)
            fill_combined((m_0, m_1), (t_0, t_1), 1, logs, deltas, 0, count)

        key_all = key_heads(k_ref, lat_0, lat_1, edge, 0)
        _, low_grad = gradients(
            key_all, key_heads(v_ref, lat_0, lat_1, edge, 1),
            halo_heads(h_0, h_1, lon_edge, 0), halo_heads(h_0, h_1, lon_edge, 1),
            bias[...], logs[pl.ds(head, 1), :], deltas[pl.ds(head, 1), :],
        )
        grad = (dot(low_grad, key_all, (0, 0)) * SCORE_SCALE).astype(jnp.bfloat16)
        out_0[...] = grad[:lon_edge]
        out_1[...] = grad[LANES : LANES + lon_edge]

    return call(
        kernel, "halo_query_grad", count,
        [heads_of(2 * lon_edge)] * 2 + [whole(mine[0].shape)] * 4 + [heads_of(own, first)] * 2
        + [heads_of(2 * edge, first)] * 2,
        [heads_of(lon_edge)] * 2,
        [jax.ShapeDtypeStruct((lon_edge, count * HEAD_DIM), jnp.bfloat16)] * 2,
        [pltpu.VMEM((own + 2 * edge, 2 * LANES), jnp.float32)]
        + [pltpu.VMEM((-(-count // 8) * 8, 2 * LANES), jnp.float32)] * 2,
        flops=1 << 30,
    )(halo_0, halo_1, *mine, *theirs, keys, values, lat_0, lat_1)


def own_grads(qp, gp, halo_0, halo_1, mine, theirs, keys, values, lat_0, lat_1, rows, cols, first, count):
    own, edge = rows * cols, RADIUS * cols
    lon_edge = RADIUS * rows
    every = own + 2 * LANES

    def kernel(
        q_ref, g_ref, h_0, h_1, m_0, m_1, t_0, t_1, k_ref, v_ref, lat_0, lat_1,
        dq_ref, dk_ref, dv_ref, out_0, out_1, bias, logs, deltas,
    ):
        head = pl.program_id(0)

        @pl.when(head == 0)
        def _():
            bias[:, :own] = bias_of(own_query_cell, rows, cols)
            bias[:, own:] = bias_of(halo_query_cell, rows, cols)
            fill_combined((m_0, m_1), (t_0, t_1), 0, logs, deltas, 0, count)
            fill_combined((m_0, m_1), (t_0, t_1), 1, logs, deltas, own, count)

        key_all = key_heads(k_ref, lat_0, lat_1, edge, 0)
        queries = jnp.concatenate([q_ref[...], halo_heads(h_0, h_1, lon_edge, 0)], axis=0)
        grads = jnp.concatenate([g_ref[...], halo_heads(h_0, h_1, lon_edge, 1)], axis=0)
        low_weights, low_grad = gradients(
            key_all, key_heads(v_ref, lat_0, lat_1, edge, 1), queries, grads,
            bias[...], logs[pl.ds(head, 1), :], deltas[pl.ds(head, 1), :],
        )
        dq_ref[...] = dot(low_grad[:, :own], key_all, (0, 0)) * SCORE_SCALE
        key_grad = dot(low_grad, queries, (1, 0)) * SCORE_SCALE
        value_grad = dot(low_weights, grads, (1, 0))
        dk_ref[...] = key_grad[:own]
        dv_ref[...] = value_grad[:own]
        for slot, out in enumerate((out_0, out_1)):
            piece = slice(own + slot * edge, own + (slot + 1) * edge)
            out[:edge, :] = key_grad[piece].astype(jnp.bfloat16)
            out[edge:, :] = value_grad[piece].astype(jnp.bfloat16)

    width = count * HEAD_DIM
    return call(
        kernel, "own_grads", count,
        [heads_of(own)] * 2 + [heads_of(2 * lon_edge)] * 2 + [whole(mine[0].shape)] * 4
        + [heads_of(own, first)] * 2 + [heads_of(2 * edge, first)] * 2,
        [heads_of(own)] * 3 + [heads_of(2 * edge)] * 2,
        [jax.ShapeDtypeStruct((own, width), jnp.float32)] * 3
        + [jax.ShapeDtypeStruct((2 * edge, width), jnp.bfloat16)] * 2,
        [pltpu.VMEM((own + 2 * edge, every), jnp.float32)]
        + [pltpu.VMEM((-(-count // 8) * 8, every), jnp.float32)] * 2,
        flops=1 << 31,
    )(qp, gp, halo_0, halo_1, *mine, *theirs, keys, values, lat_0, lat_1)


def finish_queries(grad, back_0, back_1, result, rows, cols, first, count, width):
    own, edge = rows * cols, rows * RADIUS

    def kernel(g_ref, b_0, b_1, *rest):
        out, order, total = rest[-3:]

        @pl.when(pl.program_id(0) == 0)
        def _():
            row, col = own_query_cell(lax.broadcasted_iota(jnp.int32, (1, own), 1), rows, cols)
            target = lax.broadcasted_iota(jnp.int32, (own, own), 0)
            order[...] = jnp.where(target == row * cols + col, 1.0, 0.0).astype(jnp.bfloat16)

        total[...] = g_ref[...].astype(jnp.bfloat16)
        for group, back in enumerate((b_0, b_1)):
            piece = slice(group * LANES, group * LANES + edge)
            total[piece, :] = (g_ref[piece, :] + back[...].astype(jnp.float32)).astype(jnp.bfloat16)
        out[...] = dot(order[...], total[...], (1, 0)).astype(jnp.bfloat16)

    extra = [] if result is None else [result]
    return call(
        kernel, "finish_queries", count,
        [heads_of(own)] + [heads_of(edge)] * 2 + [pl.BlockSpec(memory_space=pl.ANY)] * len(extra),
        heads_of(own, first),
        jax.ShapeDtypeStruct((own, width), jnp.bfloat16),
        [pltpu.VMEM((own, own), jnp.bfloat16), pltpu.VMEM((own, HEAD_DIM), jnp.bfloat16)],
        flops=1 << 28, aliases={3: 0} if extra else None,
    )(grad, back_0, back_1, *extra)


def finish_keys(key_grad, value_grad, back_0, back_1, results, rows, cols, first, count, width):
    own, edge = rows * cols, RADIUS * cols

    def kernel(dk_ref, dv_ref, b_0, b_1, *rest):
        outs = rest[-2:]
        for part, (grad, out) in enumerate(zip((dk_ref, dv_ref), outs)):
            middle = slice(edge, own - edge)
            out[middle, :] = grad[middle, :].astype(jnp.bfloat16)
            for slot, back in enumerate((b_0, b_1)):
                start = pl.multiple_of(slot_side("lat", slot) * (own - edge), 16)
                arrived = back[part * edge : (part + 1) * edge, :].astype(jnp.float32)
                out[pl.ds(start, edge), :] = (grad[pl.ds(start, edge), :] + arrived).astype(jnp.bfloat16)

    extra = [] if results is None else list(results)
    return call(
        kernel, "finish_keys", count,
        [heads_of(own)] * 2 + [heads_of(2 * edge)] * 2 + [pl.BlockSpec(memory_space=pl.ANY)] * len(extra),
        [heads_of(own, first)] * 2,
        [jax.ShapeDtypeStruct((own, width), jnp.bfloat16)] * 2,
        flops=1 << 28, aliases={4: 0, 5: 1} if extra else None,
    )(key_grad, value_grad, back_0, back_1, *extra)


def swap(axis, slot, wrap, array):
    count = lax.axis_size(axis)
    pairs = []
    for low in range(slot, count if wrap else count - 1, 2):
        high = (low + 1) % count
        pairs += [(low, high), (high, low)]
    return lax.ppermute(array, axis, pairs)


def swap_lon(arrays):
    return [swap("lon", slot, True, array) for slot, array in enumerate(arrays)]


def swap_lat(arrays):
    return [swap("lat", slot, False, array) for slot, array in enumerate(arrays)]


def shards(queries, key_field, value_field, out_grad):
    rows, cols, width = queries.shape
    own = rows * cols
    heads = width // HEAD_DIM
    flat = lambda x: x.reshape(own, width)
    queries, key_field, value_field, out_grad = map(flat, (queries, key_field, value_field, out_grad))
    starts = [sum(CHUNKS[:i]) for i in range(len(CHUNKS))]
    assert sum(CHUNKS) == heads
    size = (rows, cols)

    packs = [pack_queries(queries, out_grad, *size, f, n) for f, n in zip(starts, CHUNKS)]
    halos = [swap_lon(pack[2:]) for pack in packs]
    lat = swap_lat(pack_keys(key_field, value_field, *size))
    keyed = (key_field, value_field, *lat)
    grad_query, key_value = None, None
    for (f, n), pack, halo in zip(zip(starts, CHUNKS), packs, halos):
        qp, gp = pack[:2]
        own_stat = own_stats(qp, gp, *keyed, *size, f, n)
        mine = halo_stats(*halo, own_stat, *keyed, *size, f, n)
        theirs = swap_lon(mine)
        back = swap_lon(halo_query_grad(*halo, mine, theirs, *keyed, *size, f, n))
        dq, dk, dv, *lat_back = own_grads(qp, gp, *halo, mine, theirs, *keyed, *size, f, n)
        lat_back = swap_lat(lat_back)
        grad_query = finish_queries(dq, *back, grad_query, *size, f, n, width)
        key_value = finish_keys(dk, dv, *lat_back, key_value, *size, f, n, width)
    shape = (rows, cols, width)
    return tuple(x.reshape(shape) for x in (grad_query, *key_value))


def solution(mesh):
    spec = P("lat", "lon", None)
    return jax.shard_map(
        shards, mesh=mesh, in_specs=(spec,) * 4, out_specs=(spec,) * 3, check_vma=False
    )
```

```python
import math

import jax
import jax.numpy as jnp
from jax import lax
from jax.experimental import pallas as pl
from jax.experimental.pallas import tpu as pltpu
from jax.sharding import PartitionSpec as P

HEAD_DIM = 128
WINDOW = 13
RADIUS = WINDOW // 2
LANES = 128
MASKED = -1e30
LOG2E = math.log2(math.e)
VMEM_BYTES = 24 * 1024 * 1024


def split(index, width):
    if width & (width - 1) == 0:
        whole = index >> (width.bit_length() - 1)
    else:
        whole = (index * ((1 << 12) // width + 1)) >> 12
    return whole, index - whole * width


def odd(axis):
    return lax.axis_index(axis) & 1


def slot_side(axis, slot):
    parity = odd(axis)
    return 1 - parity if slot == 0 else parity


def own_query_cell(position, rows, cols):
    edge = rows * RADIUS
    group = position >> 7
    place = position & (LANES - 1)
    side = jnp.where(group == 0, slot_side("lon", 0), slot_side("lon", 1))
    row_a, col_a = split(place, RADIUS)
    inner = cols - 2 * RADIUS
    row_b, col_b = split(place - edge + (LANES - edge) * group, inner)
    at_edge = place < edge
    row = jnp.where(at_edge, row_a, row_b)
    col = jnp.where(at_edge, side * (cols - RADIUS) + col_a, RADIUS + col_b)
    return row, col


def halo_query_cell(position, rows, cols):
    edge = rows * RADIUS
    group = position >> 7
    place = position & (LANES - 1)
    side = jnp.where(group == 0, slot_side("lon", 0), slot_side("lon", 1))
    row, col = split(place, RADIUS)
    col = jnp.where(side == 1, cols, -RADIUS) + col
    col = jnp.where(place < edge, col, 1 << 12)
    return row, col


def edge_key_cell(slot, position, rows, cols):
    near = LANES * 3 // 8
    inner = cols - 2 * RADIUS
    group = jnp.where(position >= near, 1, 0)
    side = jnp.where(group == 0, slot_side("lon", 0), slot_side("lon", 1))
    row_a, col_a = split(position - near * group, RADIUS)
    row_b, col_b = split(jnp.maximum(position - 2 * near, 0), inner)
    in_middle = position >= 2 * near
    row = jnp.where(in_middle, row_b, row_a)
    col = jnp.where(in_middle, RADIUS + col_b, side * (cols - RADIUS) + col_a)
    return jnp.where(row < RADIUS, row, -1), col


def band_edge(slot, rows):
    return slot_side("lat", slot) * (rows - RADIUS)


NEAR = 192
KEYS = 512


def near_key_cell(group, position, rows, cols):
    edge = rows * RADIUS
    half = LANES * 3 // 8
    side = slot_side("lon", group)
    row_a, col_a = split(position, RADIUS)
    row, col = row_a, col_a
    for slot in (0, 1):
        place = position - edge - half * slot
        row_b, col_b = split(jnp.maximum(place, 0), RADIUS)
        outside = jnp.where(slot_side("lat", slot) == 1, rows, -RADIUS)
        row_b = jnp.where(row_b < RADIUS, row_b + outside, -(1 << 12))
        row = jnp.where(place >= 0, row_b, row)
        col = jnp.where(place >= 0, col_b, col)
    return row, side * (cols - RADIUS) + col


def middle_key_cell(position, rows, cols):
    inner = cols - 2 * RADIUS
    edge = rows * inner
    row, col = split(position, inner)
    for slot in (0, 1):
        place = position - edge - 32 * slot
        row_b, col_b = split(jnp.maximum(place, 0), inner)
        outside = jnp.where(slot_side("lat", slot) == 1, rows, -RADIUS)
        row_b = jnp.where(row_b < RADIUS, row_b + outside, -(1 << 12))
        row = jnp.where(place >= 0, row_b, row)
        col = jnp.where(place >= 0, col_b, col)
    return row, RADIUS + col


def bias_of(key_cells, query_cells, rows):
    total_rows = rows * lax.axis_size("lat")
    first = rows * lax.axis_index("lat")
    key_row, key_col = key_cells
    query_row, query_col = query_cells
    start = jnp.clip(first + query_row - RADIUS, 0, total_rows - WINDOW)
    from_start = first + key_row - start
    inside = (from_start >= 0) & (from_start < WINDOW)
    inside = inside & (jnp.abs(key_col - query_col) <= RADIUS)
    return jnp.where(inside, 0.0, MASKED)


def down(count):
    return lax.broadcasted_iota(jnp.int32, (count, 1), 0)


def across(count, start=0):
    return lax.broadcasted_iota(jnp.int32, (1, count), 1) + start


def dot(a, b, contract):
    return lax.dot_general(a, b, ((contract[:1], contract[1:]), ((), ())), preferred_element_type=jnp.float32)


def call(kernel, name, operands, out_shapes, scratch=(), flops=0, aliases=None, outs=None, ins=None):
    spec = pl.BlockSpec(memory_space=pltpu.VMEM)
    return pl.pallas_call(
        kernel,
        name=name,
        in_specs=ins or [spec] * len(operands),
        out_specs=outs or [spec] * len(out_shapes),
        out_shape=out_shapes,
        scratch_shapes=scratch,
        input_output_aliases=aliases or {},
        compiler_params=pltpu.CompilerParams(vmem_limit_bytes=VMEM_BYTES),
        cost_estimate=pl.CostEstimate(flops=flops, bytes_accessed=1 << 20, transcendentals=0),
    )(*operands)


def low(*shape):
    return jax.ShapeDtypeStruct(shape, jnp.bfloat16)


def full(*shape):
    return jax.ShapeDtypeStruct(shape, jnp.float32)


def lanes_of(head, count=1):
    return slice(head * HEAD_DIM, (head + count) * HEAD_DIM)


def selection(row, col, rows, cols):
    source = across(rows * cols)
    return jnp.where(source == row * cols + col, 1.0, 0.0).astype(jnp.bfloat16)


def pack_queries(queries, out_grad, rows, cols, first, count):
    own, edge = rows * cols, rows * RADIUS

    def kernel(q_ref, g_ref, qp_ref, gp_ref, send_0, send_1):
        order = selection(*own_query_cell(down(own), rows, cols), rows, cols)
        for place, (src, dst) in enumerate(((q_ref, qp_ref), (g_ref, gp_ref))):
            for at in range(0, count, 2):
                here = lanes_of(at, min(2, count - at))
                moved = dot(order, src[:, lanes_of(first + at, min(2, count - at))], (1, 0)).astype(jnp.bfloat16)
                dst[:, here] = moved
                for group, send in enumerate((send_0, send_1)):
                    send[place * edge : (place + 1) * edge, here] = moved[group * LANES : group * LANES + edge]

    width = count * HEAD_DIM
    return call(
        kernel, "pack_queries", (queries, out_grad),
        [low(own, width)] * 2 + [low(2 * edge, width)] * 2, flops=1 << 28,
    )


def pack_keys(key_field, value_field, rows, cols):
    own = rows * cols
    width = key_field.shape[1]

    def kernel(k_ref, v_ref, kp_ref, vp_ref, send_0, send_1):
        order = selection(*own_query_cell(down(own), rows, cols), rows, cols)
        picks = []
        for slot in (0, 1):
            row, col = edge_key_cell(slot, down(LANES), rows, cols)
            row = jnp.where(row < 0, rows, row + band_edge(slot, rows))
            picks.append(selection(row, col, rows, cols))
        for part, (src, dst) in enumerate(((k_ref, kp_ref), (v_ref, vp_ref))):
            for at in range(0, width, 256):
                here = slice(at, at + 256)
                block = src[:, here]
                dst[:, here] = dot(order, block, (1, 0)).astype(jnp.bfloat16)
                for pick, send in zip(picks, (send_0, send_1)):
                    send[part * LANES : (part + 1) * LANES, here] = dot(pick, block, (1, 0)).astype(jnp.bfloat16)

    return call(
        kernel, "pack_keys", (key_field, value_field),
        [low(own, width)] * 2 + [low(2 * LANES, width)] * 2, flops=1 << 28,
    )


def halo_head(ref, edge, part, head):
    rows = ref[part * edge : (part + 1) * edge, lanes_of(head)]
    return jnp.concatenate([rows, jnp.zeros((LANES - edge, HEAD_DIM), jnp.bfloat16)], axis=0)


def near_keys(group, own_ref, lat_refs, part, head):
    lanes, half = lanes_of(head), LANES * 3 // 8
    edge = NEAR - 2 * half
    pieces = [own_ref[group * LANES : group * LANES + edge, lanes]]
    at = part * LANES + group * half
    pieces += [ref[at : at + half, lanes] for ref in lat_refs]
    return jnp.concatenate(pieces, axis=0)


def middle_keys(own_ref, lat_refs, part, head):
    lanes, half = lanes_of(head), LANES * 3 // 8
    edge = NEAR - 2 * half
    pieces = [own_ref[edge:LANES, lanes], own_ref[LANES + edge :, lanes]]
    at = part * LANES + 2 * half
    pieces += [ref[at : part * LANES + LANES, lanes] for ref in lat_refs]
    return jnp.concatenate(pieces, axis=0)


def every_key(own_ref, lat_refs, part, head):
    near = [near_keys(group, own_ref, lat_refs, part, head) for group in (0, 1)]
    return jnp.concatenate(near + [middle_keys(own_ref, lat_refs, part, head)], axis=0)


SCORE_SCALE = 1.0 / math.sqrt(HEAD_DIM)


def part_stats(scores, weight_grad):
    peak = jnp.max(scores, axis=0, keepdims=True)
    weights = jnp.exp2(scores - peak)
    total = jnp.sum(weights, axis=0, keepdims=True)
    dotted = jnp.sum(weights * weight_grad, axis=0, keepdims=True)
    return peak + jnp.log(total) * LOG2E, dotted / total


def stat_rows(count):
    return -(-2 * count // 8) * 8


def own_stats(qp, gp, kp, vp, lat, rows, cols, first, count):
    own = rows * cols

    def kernel(q_ref, g_ref, k_ref, v_ref, lat_0, lat_1, out, s_ref, d_ref, bias):
        lat_refs = (lat_0, lat_1)
        queries = own_query_cell(across(own), rows, cols)
        for group in (0, 1):
            bias[group * NEAR : (group + 1) * NEAR, :] = bias_of(
                near_key_cell(group, down(NEAR), rows, cols), queries, rows
            )
        bias[2 * NEAR :, :] = bias_of(middle_key_cell(down(LANES), rows, cols), queries, rows)
        out[...] = jnp.zeros_like(out)
        for head in range(count):
            key = every_key(k_ref, lat_refs, 0, first + head)
            value = every_key(v_ref, lat_refs, 1, first + head)
            scores = dot(key, q_ref[:, lanes_of(head)], (1, 1)) * (SCORE_SCALE * LOG2E) + bias[...]
            weight_grad = dot(value, g_ref[:, lanes_of(head)], (1, 1))
            s_ref[head] = scores
            d_ref[head] = weight_grad
            log_total, delta = part_stats(scores, weight_grad)
            out[head : head + 1, :] = log_total
            out[count + head : count + head + 1, :] = delta

    return call(
        kernel, "own_stats", (qp, gp, kp, vp, *lat),
        [full(stat_rows(count), own)] + [full(count, KEYS, own)] * 2,
        [pltpu.VMEM((KEYS, own), jnp.float32)], flops=1 << 30,
    )


def halo_stats(halo, own_stat, kp, vp, lat, rows, cols, first, count):
    edge = RADIUS * rows

    def kernel(h_0, h_1, stat, k_ref, v_ref, lat_0, lat_1, out_0, out_1, s_ref, d_ref, bias):
        lat_refs = (lat_0, lat_1)
        for group, (halo_ref, out) in enumerate(zip((h_0, h_1), (out_0, out_1))):
            lanes = slice(group * LANES, (group + 1) * LANES)
            bias[...] = bias_of(
                near_key_cell(group, down(NEAR), rows, cols),
                halo_query_cell(across(LANES, group * LANES), rows, cols), rows,
            )
            out[:, :LANES] = stat[:, lanes]
            out[:, LANES:] = jnp.zeros((out.shape[0], LANES), jnp.float32)
            for head in range(count):
                key = near_keys(group, k_ref, lat_refs, 0, first + head)
                value = near_keys(group, v_ref, lat_refs, 1, first + head)
                scores = dot(key, halo_head(halo_ref, edge, 0, head), (1, 1)) * (SCORE_SCALE * LOG2E) + bias[...]
                weight_grad = dot(value, halo_head(halo_ref, edge, 1, head), (1, 1))
                s_ref[head, :, lanes] = scores
                d_ref[head, :, lanes] = weight_grad
                log_total, delta = part_stats(scores, weight_grad)
                out[head : head + 1, LANES:] = log_total
                out[count + head : count + head + 1, LANES:] = delta

    return call(
        kernel, "halo_stats", (*halo, own_stat, kp, vp, *lat),
        [full(stat_rows(count), 2 * LANES)] * 2 + [full(count, NEAR, 2 * LANES)] * 2,
        [pltpu.VMEM((NEAR, LANES), jnp.float32)], flops=1 << 30,
    )


def combined(mine, theirs, count):
    a, b = mine[:count], theirs[:count]
    peak = jnp.maximum(a, b)
    part_a, part_b = jnp.exp2(a - peak), jnp.exp2(b - peak)
    total = part_a + part_b
    delta = (part_a * mine[count : 2 * count] + part_b * theirs[count : 2 * count]) / total
    return peak + jnp.log(total) * LOG2E, delta


LOW, HIGH = slice(0, LANES), slice(LANES, 2 * LANES)


def gradients(scores, weight_grad, log_total, delta):
    weights = jnp.exp2(scores - log_total)
    return weights.astype(jnp.bfloat16), (weights * (weight_grad - delta)).astype(jnp.bfloat16)


def halo_query_grad(mine, theirs, scores, weight_grad, kp, lat, rows, cols, first, count):
    edge = RADIUS * rows

    def kernel(m_0, m_1, t_0, t_1, s_ref, d_ref, k_ref, lat_0, lat_1, out_0, out_1, p_ref, g_ref):
        for group, (m, t, out) in enumerate(((m_0, t_0, out_0), (m_1, t_1, out_1))):
            lanes = slice(group * LANES, (group + 1) * LANES)
            log_total, delta = combined(m[:, HIGH], t[:, LOW], count)
            for head in range(count):
                here = slice(head, head + 1)
                weights, grad = gradients(
                    s_ref[head, :, lanes], d_ref[head, :, lanes], log_total[here], delta[here]
                )
                p_ref[head, :, lanes] = weights
                g_ref[head, :, lanes] = grad
                key = near_keys(group, k_ref, (lat_0, lat_1), 0, first + head)
                query_grad = dot(grad, key, (0, 0)) * SCORE_SCALE
                out[:, lanes_of(head)] = query_grad[:edge].astype(jnp.bfloat16)

    return call(
        kernel, "halo_query_grad", (*mine, *theirs, scores, weight_grad, kp, *lat),
        [low(edge, count * HEAD_DIM)] * 2 + [low(count, NEAR, 2 * LANES)] * 2, flops=1 << 30,
    )


def own_grads(qp, gp, halo, mine, theirs, scores, weight_grad, low_weights, low_grad, kp, lat, rows, cols, first, count):
    own, edge = rows * cols, RADIUS * rows
    half = LANES * 3 // 8

    def kernel(
        q_ref, g_ref, h_0, h_1, m_0, m_1, t_0, t_1, s_ref, d_ref, p_ref, l_ref, k_ref, lat_0, lat_1,
        dq_ref, dk_ref, dv_ref, out_0, out_1, total,
    ):
        combos = [combined(m[:, LOW], t[:, HIGH], count) for m, t in ((m_0, t_0), (m_1, t_1))]
        logs, deltas = (jnp.concatenate([c[i] for c in combos], axis=1) for i in (0, 1))
        for head in range(count):
            here, lanes = slice(head, head + 1), lanes_of(head)
            weights, grad = gradients(s_ref[head], d_ref[head], logs[here], deltas[here])
            key = every_key(k_ref, (lat_0, lat_1), 0, first + head)
            dq_ref[:, lanes] = dot(grad, key, (0, 0)) * SCORE_SCALE
            sides = (
                (grad, l_ref, q_ref, 0, dk_ref, SCORE_SCALE),
                (weights, p_ref, g_ref, 1, dv_ref, None),
            )
            for mine_low, halo_low, own_ref, part, result, scale in sides:
                total[...] = dot(mine_low, own_ref[:, lanes], (1, 0))
                for group, halo_ref in enumerate((h_0, h_1)):
                    near = slice(group * NEAR, (group + 1) * NEAR)
                    total[near, :] += dot(
                        halo_low[head, :, group * LANES : (group + 1) * LANES],
                        halo_head(halo_ref, edge, part, head), (1, 0),
                    )
                scaled = (lambda x: x) if scale is None else (lambda x: x * scale)
                middle = 2 * NEAR
                for group in (0, 1):
                    at = group * LANES
                    result[at : at + edge, lanes] = scaled(total[group * NEAR : group * NEAR + edge, :])
                    rest = LANES - edge
                    result[at + edge : at + LANES, lanes] = scaled(
                        total[middle + group * rest : middle + (group + 1) * rest, :]
                    )
                for slot, out in enumerate((out_0, out_1)):
                    base = part * LANES
                    for group in (0, 1):
                        at = group * NEAR + edge + slot * half
                        out[base + group * half : base + (group + 1) * half, lanes] = scaled(
                            total[at : at + half, :]
                        ).astype(jnp.bfloat16)
                    at = middle + 2 * (LANES - edge) + slot * 32
                    out[base + 2 * half : base + LANES, lanes] = scaled(total[at : at + 32, :]).astype(jnp.bfloat16)

    width = count * HEAD_DIM
    return call(
        kernel, "own_grads",
        (qp, gp, *halo, *mine, *theirs, scores, weight_grad, low_weights, low_grad, kp, *lat),
        [full(own, width)] * 3 + [low(2 * LANES, width)] * 2,
        [pltpu.VMEM((KEYS, HEAD_DIM), jnp.float32)], flops=1 << 31,
    )


def restore(rows, cols):
    own = rows * cols
    row, col = own_query_cell(across(own), rows, cols)
    return jnp.where(down(own) == row * cols + col, 1.0, 0.0).astype(jnp.bfloat16)


def finish_queries(grad, back, result, rows, cols, first, count, width):
    own, edge = rows * cols, rows * RADIUS

    def kernel(g_ref, b_0, b_1, *rest):
        out, total = rest[-2:]
        order = restore(rows, cols)
        total[...] = g_ref[...].astype(jnp.bfloat16)
        for group, back_ref in enumerate((b_0, b_1)):
            piece = slice(group * LANES, group * LANES + edge)
            total[piece, :] = (g_ref[piece, :] + back_ref[...].astype(jnp.float32)).astype(jnp.bfloat16)
        for at in range(0, count, 2):
            n = min(2, count - at)
            out[:, lanes_of(first + at, n)] = dot(order, total[:, lanes_of(at, n)], (1, 0)).astype(jnp.bfloat16)

    return call(
        kernel, "finish_queries", (grad, *back), [low(own, width)],
        [pltpu.VMEM((own, count * HEAD_DIM), jnp.bfloat16)], flops=1 << 28,
    )[0]


def finish_keys(key_grad, value_grad, back, rows, cols, first, count, width):
    own = rows * cols

    def kernel(dk_ref, dv_ref, b_0, b_1, out_k, out_v):
        order = restore(rows, cols)
        own_row, own_col = own_query_cell(down(own), rows, cols)
        spread = []
        for slot in (0, 1):
            row, col = edge_key_cell(slot, across(LANES), rows, cols)
            cell = jnp.where(row < 0, -1, (row + band_edge(slot, rows)) * cols + col)
            spread.append(jnp.where(own_row * cols + own_col == cell, 1.0, 0.0).astype(jnp.bfloat16))
        spread = jnp.concatenate(spread, axis=1)
        for part, (grad, out) in enumerate(((dk_ref, out_k), (dv_ref, out_v))):
            for at in range(0, count, 2):
                n = min(2, count - at)
                lanes = lanes_of(at, n)
                piece = slice(part * LANES, (part + 1) * LANES)
                arrived = jnp.concatenate([b_0[piece, lanes], b_1[piece, lanes]], axis=0)
                total = (grad[:, lanes] + dot(spread, arrived, (1, 0))).astype(jnp.bfloat16)
                out[:, lanes_of(first + at, n)] = dot(order, total, (1, 0)).astype(jnp.bfloat16)

    return call(kernel, "finish_keys", (key_grad, value_grad, *back), [low(own, width)] * 2, flops=1 << 28)


def swap(axis, slot, wrap, array):
    count = lax.axis_size(axis)
    pairs = []
    for lower in range(slot, count if wrap else count - 1, 2):
        upper = (lower + 1) % count
        pairs += [(lower, upper), (upper, lower)]
    return lax.ppermute(array, axis, pairs)


def swap_lon(arrays):
    second = swap("lon", 1, True, arrays[1])
    return [swap("lon", 0, True, arrays[0]), second]


def swap_lat(arrays):
    return [swap("lat", slot, False, array) for slot, array in enumerate(arrays)]


def after(value, *earlier):
    return lax.optimization_barrier((value, *earlier))[0]


def shards(queries, key_field, value_field, out_grad):
    rows, cols, width = queries.shape
    own = rows * cols
    flat = lambda x: x.reshape(own, width)
    queries, key_field, value_field, out_grad = map(flat, (queries, key_field, value_field, out_grad))
    size = (rows, cols)
    f, n = 0, width // HEAD_DIM

    qp, gp, *sends = pack_queries(queries, out_grad, *size, f, n)
    halo = swap_lon(sends)
    kp, vp, *sends = pack_keys(key_field, value_field, *size)
    lat = swap_lat(sends)
    own_stat, own_s, own_d = own_stats(qp, gp, kp, vp, lat, *size, f, n)
    *mine, halo_s, halo_d = halo_stats(halo, own_stat, kp, vp, lat, *size, f, n)
    theirs = swap_lon(mine)
    *back, low_weights, low_grad = halo_query_grad(mine, theirs, halo_s, halo_d, kp, lat, *size, f, n)
    back = swap_lon(back)
    dq, dk, dv, *lat_back = own_grads(
        qp, gp, halo, mine, theirs, own_s, own_d, low_weights, low_grad, kp, lat, *size, f, n
    )
    lat_back = swap_lat(lat_back)
    grad_query = finish_queries(dq, back, None, *size, f, n, width)
    grad_key, grad_value = finish_keys(dk, dv, lat_back, *size, f, n, width)
    shape = (rows, cols, width)
    return tuple(x.reshape(shape) for x in (grad_query, grad_key, grad_value))


def solution(mesh):
    spec = P("lat", "lon", None)
    return jax.shard_map(
        shards, mesh=mesh, in_specs=(spec,) * 4, out_specs=(spec,) * 3, check_vma=False
    )
```

```python
import math

import jax
import jax.numpy as jnp
from jax import lax
from jax.experimental import pallas as pl
from jax.experimental.pallas import tpu as pltpu
from jax.sharding import PartitionSpec as P

HEAD_DIM = 128
WINDOW = 13
RADIUS = WINDOW // 2
LANES = 128
FIRST = 0
MASKED = -1e30
LOG2E = math.log2(math.e)
VMEM_BYTES = 24 * 1024 * 1024


def split(index, width):
    if width & (width - 1) == 0:
        whole = index >> (width.bit_length() - 1)
    else:
        whole = (index * ((1 << 12) // width + 1)) >> 12
    return whole, index - whole * width


def odd(axis):
    return lax.axis_index(axis) & 1


def slot_side(axis, slot):
    parity = odd(axis)
    return parity if slot == 0 else 1 - parity


def own_query_cell(position, rows, cols):
    edge = rows * RADIUS
    group = position >> 7
    place = position & (LANES - 1)
    side = jnp.where(group == 0, slot_side("lon", 0), slot_side("lon", 1))
    row_a, col_a = split(place, RADIUS)
    inner = cols - 2 * RADIUS
    row_b, col_b = split(place - edge + (LANES - edge) * group, inner)
    at_edge = place < edge
    row = jnp.where(at_edge, row_a, row_b)
    col = jnp.where(at_edge, side * (cols - RADIUS) + col_a, RADIUS + col_b)
    return row, col


def halo_query_cell(position, rows, cols):
    edge = rows * RADIUS
    group = position >> 7
    place = position & (LANES - 1)
    side = jnp.where(group == 0, slot_side("lon", 0), slot_side("lon", 1))
    row, col = split(place, RADIUS)
    col = jnp.where(side == 1, cols, -RADIUS) + col
    col = jnp.where(place < edge, col, 1 << 12)
    return row, col


def lat_key_cell(slot, position, rows, cols):
    row, col = split(position, cols)
    return row + jnp.where(slot_side("lat", slot) == 1, rows, -RADIUS), col


def bias_of(key_cells, query_cells, rows):
    total_rows = rows * lax.axis_size("lat")
    first = rows * lax.axis_index("lat")
    key_row, key_col = key_cells
    query_row, query_col = query_cells
    start = jnp.clip(first + query_row - RADIUS, 0, total_rows - WINDOW)
    from_start = first + key_row - start
    inside = (from_start >= 0) & (from_start < WINDOW)
    inside = inside & (jnp.abs(key_col - query_col) <= RADIUS)
    return jnp.where(inside, 0.0, MASKED)


def down(count):
    return lax.broadcasted_iota(jnp.int32, (count, 1), 0)


def across(count, start=0):
    return lax.broadcasted_iota(jnp.int32, (1, count), 1) + start


def dot(a, b, contract):
    return lax.dot_general(a, b, ((contract[:1], contract[1:]), ((), ())), preferred_element_type=jnp.float32)


def call(kernel, name, operands, out_shapes, scratch=(), flops=0, aliases=None, outs=None, ins=None):
    return pl.pallas_call(
        kernel,
        name=name,
        in_specs=ins or [VMEM_SPEC] * len(operands),
        out_specs=outs or [VMEM_SPEC] * len(out_shapes),
        out_shape=out_shapes,
        scratch_shapes=scratch,
        input_output_aliases=aliases or {},
        compiler_params=pltpu.CompilerParams(vmem_limit_bytes=VMEM_BYTES),
        cost_estimate=pl.CostEstimate(flops=flops, bytes_accessed=0, transcendentals=0),
    )(*operands)


def low(*shape):
    return jax.ShapeDtypeStruct(shape, jnp.bfloat16)


def full(*shape):
    return jax.ShapeDtypeStruct(shape, jnp.float32)


def lanes_of(head, count=1):
    return slice(head * HEAD_DIM, (head + count) * HEAD_DIM)


def selection(row, col, rows, cols):
    source = across(rows * cols)
    return jnp.where(source == row * cols + col, 1.0, 0.0).astype(jnp.bfloat16)


HBM_SPEC, VMEM_SPEC = pl.BlockSpec(memory_space=pltpu.HBM), pl.BlockSpec(memory_space=pltpu.VMEM)
BLOCK = 2 * HEAD_DIM


def pack_queries(queries, out_grad, key_field, value_field, rows, cols, count):
    own, edge, width = rows * cols, rows * RADIUS, count * HEAD_DIM

    def kernel(q_hbm, g_hbm, k_hbm, v_hbm, qp_ref, gp_ref, send_0, send_1, k_ref, v_ref, q_ref, g_ref, sems):
        copies = [
            pltpu.make_async_copy(src, dst, sems.at[i])
            for i, (src, dst) in enumerate(
                ((q_hbm, q_ref), (g_hbm, g_ref), (k_hbm, k_ref), (v_hbm, v_ref))
            )
        ]
        for copy in copies:
            copy.start()
        order = selection(*own_query_cell(down(own), rows, cols), rows, cols)
        for place, (src, dst) in enumerate(((q_ref, qp_ref), (g_ref, gp_ref))):
            copies[place].wait()
            for at in range(0, width, BLOCK):
                here = slice(at, at + BLOCK)
                moved = dot(order, src[:, here], (1, 0)).astype(jnp.bfloat16)
                dst[:, here] = moved
                for group, send in enumerate((send_0, send_1)):
                    send[place * edge : (place + 1) * edge, here] = moved[group * LANES : group * LANES + edge]
        copies[2].wait()
        copies[3].wait()

    operands = [
        pltpu.with_memory_space_constraint(x, pltpu.HBM) for x in (queries, out_grad, key_field, value_field)
    ]
    return call(
        kernel, "pack_queries", operands,
        [low(own, width)] * 2 + [low(2 * edge, width)] * 2 + [low(own, width)] * 2,
        [pltpu.VMEM((own, width), jnp.bfloat16)] * 2 + [pltpu.SemaphoreType.DMA((4,))],
        ins=[HBM_SPEC] * 4,
    )


def pack_keys(key_field, value_field, rows, cols):
    own, edge = rows * cols, RADIUS * cols
    width = key_field.shape[1]

    def kernel(k_ref, v_ref, kp_ref, vp_ref, k_0, k_1, v_0, v_1):
        order = selection(*own_query_cell(down(own), rows, cols), rows, cols)
        for src, dst, sends in zip((k_ref, v_ref), (kp_ref, vp_ref), ((k_0, k_1), (v_0, v_1))):
            for slot, send in enumerate(sends):
                start = pl.multiple_of(slot_side("lat", slot) * (own - edge), 16)
                send[...] = src[pl.ds(start, edge), :]
            for at in range(0, width, BLOCK):
                here = slice(at, at + BLOCK)
                dst[:, here] = dot(order, src[:, here], (1, 0)).astype(jnp.bfloat16)

    return call(
        kernel, "pack_keys", (key_field, value_field),
        [low(own, width)] * 2 + [low(edge, width)] * 4,
    )


def halo_head(ref, edge, part, head):
    rows = ref[part * edge : (part + 1) * edge, lanes_of(head)]
    return jnp.concatenate([rows, jnp.zeros((LANES - edge, HEAD_DIM), jnp.bfloat16)], axis=0)


def near_keys(group, own_ref, lat_refs, head):
    lanes, edge = lanes_of(head), lat_refs[0].shape[0]
    pieces = [own_ref[group * LANES : group * LANES + edge, lanes]]
    return jnp.concatenate(pieces + [ref[:, lanes] for ref in lat_refs], axis=0)


def every_key(own_ref, lat_refs, head):
    lanes = lanes_of(head)
    return jnp.concatenate([ref[:, lanes] for ref in (own_ref, *lat_refs)], axis=0)


def fill_bias(bias, own_position, queries, rows, cols):
    at, edge = own_position.shape[0], RADIUS * cols
    bias[:at, :] = bias_of(own_query_cell(own_position, rows, cols), queries, rows)
    for slot in (0, 1):
        here = slice(at + slot * edge, at + (slot + 1) * edge)
        bias[here, :] = bias_of(lat_key_cell(slot, down(edge), rows, cols), queries, rows)


LOW, HIGH = slice(0, LANES), slice(LANES, 2 * LANES)
SCORE_SCALE = 1.0 / math.sqrt(HEAD_DIM)


def part_stats(scores, weight_grad):
    peak = jnp.max(scores, axis=0, keepdims=True)
    weights = jnp.exp2(scores - peak)
    total = jnp.sum(weights, axis=0, keepdims=True)
    dotted = jnp.sum(weights * weight_grad, axis=0, keepdims=True)
    return peak + jnp.log(total) * LOG2E, dotted / total


def stat_rows(count):
    return -(-2 * count // 8) * 8


def own_stats(qp, gp, kp, vp, lat, rows, cols, count):
    own, keys = rows * cols, (rows + 2 * RADIUS) * cols

    def kernel(q_ref, g_ref, k_ref, v_ref, k_0, k_1, v_0, v_1, out, s_ref, d_ref, bias):
        fill_bias(bias, down(own), own_query_cell(across(own), rows, cols), rows, cols)
        out[...] = jnp.zeros_like(out)
        for head in range(count):
            key = every_key(k_ref, (k_0, k_1), head)
            value = every_key(v_ref, (v_0, v_1), head)
            scores = dot(key, q_ref[:, lanes_of(head)], (1, 1)) * (SCORE_SCALE * LOG2E) + bias[...]
            weight_grad = dot(value, g_ref[:, lanes_of(head)], (1, 1))
            s_ref[head] = scores
            d_ref[head] = weight_grad
            log_total, delta = part_stats(scores, weight_grad)
            out[head : head + 1, :] = log_total
            out[count + head : count + head + 1, :] = delta

    return call(
        kernel, "own_stats", (qp, gp, kp, vp, *lat),
        [full(stat_rows(count), own)] + [full(count, keys, own)] * 2,
        [pltpu.VMEM((keys, own), jnp.float32)],
    )


def halo_stats(group, halo, own_stat, kp, vp, lat, rows, cols, count):
    edge = RADIUS * rows
    near = edge + 2 * RADIUS * cols

    def kernel(halo_ref, stat, k_ref, v_ref, k_0, k_1, v_0, v_1, out, s_ref, d_ref, bias):
        queries = halo_query_cell(across(LANES, group * LANES), rows, cols)
        fill_bias(bias, down(edge) + group * LANES, queries, rows, cols)
        out[:, LOW] = stat[:, group * LANES : (group + 1) * LANES]
        out[:, HIGH] = jnp.zeros((out.shape[0], LANES), jnp.float32)
        for head in range(count):
            key = near_keys(group, k_ref, (k_0, k_1), head)
            value = near_keys(group, v_ref, (v_0, v_1), head)
            scores = dot(key, halo_head(halo_ref, edge, 0, head), (1, 1)) * (SCORE_SCALE * LOG2E) + bias[...]
            weight_grad = dot(value, halo_head(halo_ref, edge, 1, head), (1, 1))
            s_ref[head] = scores
            d_ref[head] = weight_grad
            log_total, delta = part_stats(scores, weight_grad)
            out[head : head + 1, HIGH] = log_total
            out[count + head : count + head + 1, HIGH] = delta

    return call(
        kernel, f"halo_stats_{group}", (halo, own_stat, kp, vp, *lat),
        [full(stat_rows(count), 2 * LANES)] + [full(count, near, LANES)] * 2,
        [pltpu.VMEM((near, LANES), jnp.float32)],
    )


def combined(mine, theirs, count):
    a, b = mine[:count], theirs[:count]
    peak = jnp.maximum(a, b)
    part_a, part_b = jnp.exp2(a - peak), jnp.exp2(b - peak)
    total = part_a + part_b
    delta = (part_a * mine[count : 2 * count] + part_b * theirs[count : 2 * count]) / total
    return peak + jnp.log(total) * LOG2E, delta


def gradients(scores, weight_grad, log_total, delta):
    weights = jnp.exp2(scores - log_total)
    return weights.astype(jnp.bfloat16), (weights * (weight_grad - delta)).astype(jnp.bfloat16)


def halo_query_grad(group, mine, theirs, scores, weight_grad, kp, lat, rows, cols, count):
    edge = RADIUS * rows

    def kernel(m, t, s_ref, d_ref, k_ref, lat_0, lat_1, out, p_ref, g_ref):
        log_total, delta = combined(m[:, HIGH], t[:, LOW], count)
        for head in range(count):
            here = slice(head, head + 1)
            p_ref[head], grad = gradients(s_ref[head], d_ref[head], log_total[here], delta[here])
            g_ref[head] = grad
            key = near_keys(group, k_ref, (lat_0, lat_1), head)
            query_grad = dot(grad, key, (0, 0)) * SCORE_SCALE
            out[:, lanes_of(head)] = query_grad[:edge].astype(jnp.bfloat16)

    return call(
        kernel, f"halo_query_grad_{group}", (mine, theirs, scores, weight_grad, kp, *lat),
        [low(edge, count * HEAD_DIM)] + [low(count, *scores.shape[1:])] * 2,
    )


def group_grads(group, refs, dq_ref, use, rows, cols, count):
    q_ref, g_ref, halo_ref, m, t, s_ref, d_ref, p_ref, l_ref, k_ref, *lat_refs = refs
    own, edge = rows * cols, RADIUS * rows
    here = slice(group * LANES, (group + 1) * LANES)
    near = slice(group * LANES, group * LANES + edge)
    logs, deltas = combined(m[:, LOW], t[:, HIGH], count)
    for head in range(count):
        row, lanes = slice(head, head + 1), lanes_of(head)
        weights, grad = gradients(s_ref[head, :, here], d_ref[head, :, here], logs[row], deltas[row])
        dq_ref[:, lanes] = dot(grad, every_key(k_ref, lat_refs, head), (0, 0)) * SCORE_SCALE
        for part, (own_low, halo_low, own_ref) in enumerate(((grad, l_ref, q_ref), (weights, p_ref, g_ref))):
            own_rows = own_ref[here, lanes]
            both = jnp.concatenate([own_rows, halo_head(halo_ref, edge, part, head)], axis=0)
            met = jnp.concatenate([own_low[near], own_low[own:]], axis=0)
            met = dot(jnp.concatenate([met, halo_low[head]], axis=1), both, (1, 0))
            apart = [] if group == 0 else [dot(own_low[: group * LANES], own_rows, (1, 0))]
            apart.append(dot(own_low[near.stop : own], own_rows, (1, 0)))
            use(part, head, lanes, jnp.concatenate(apart[:-1] + [met[:edge], apart[-1]], axis=0), met[edge:])


def first_grads(group, operands, rows, cols, count):
    own, keys, width = rows * cols, (rows + 2 * RADIUS) * cols, count * HEAD_DIM

    def kernel(*refs):
        *refs, dq_ref, dk_ref, dv_ref = refs

        def use(part, head, lanes, inside, outside):
            result = (dk_ref, dv_ref)[part]
            result[:own, lanes] = inside
            result[own:, lanes] = outside

        group_grads(group, refs, dq_ref, use, rows, cols, count)

    return call(kernel, "first_grads", operands, [full(LANES, width)] + [full(keys, width)] * 2)


def second_grads(group, operands, key_part, value_part, rows, cols, count):
    own, width, edge = rows * cols, count * HEAD_DIM, RADIUS * cols

    def kernel(*refs):
        *refs, kpart, vpart, dq_ref, dk_ref, dv_ref, out_0, out_1 = refs

        def use(part, head, lanes, inside, outside):
            before, result, scale = ((kpart, dk_ref, SCORE_SCALE), (vpart, dv_ref, 1.0))[part]
            result[:, lanes] = (inside + before[:own, lanes]) * scale
            outside = (outside + before[own:, lanes]) * scale
            for slot, out in enumerate((out_0, out_1)):
                out[part * edge : (part + 1) * edge, lanes] = outside[
                    slot * edge : (slot + 1) * edge
                ].astype(jnp.bfloat16)

        group_grads(group, refs, dq_ref, use, rows, cols, count)

    return call(
        kernel, "second_grads", (*operands, key_part, value_part),
        [full(LANES, width)] + [full(own, width)] * 2 + [low(2 * edge, width)] * 2,
    )


def restore(rows, cols):
    own = rows * cols
    row, col = own_query_cell(across(own), rows, cols)
    return jnp.where(down(own) == row * cols + col, 1.0, 0.0).astype(jnp.bfloat16)


def finish_queries(grads, back, rows, cols, count):
    own, edge, width = rows * cols, rows * RADIUS, count * HEAD_DIM

    def kernel(g_0, g_1, b_0, b_1, out, total):
        order = restore(rows, cols)
        for group, (grad, arrived) in enumerate(((g_0, b_0), (g_1, b_1))):
            at = group * LANES
            total[at : at + edge, :] = (grad[:edge, :] + arrived[...].astype(jnp.float32)).astype(jnp.bfloat16)
            total[at + edge : at + LANES, :] = grad[edge:, :].astype(jnp.bfloat16)
        for at in range(0, width, 256):
            lanes = slice(at, at + 256)
            out[:, lanes] = dot(order, total[:, lanes], (1, 0)).astype(jnp.bfloat16)

    return call(
        kernel, "finish_queries", (*grads, *back), [low(own, width)],
        [pltpu.VMEM((own, width), jnp.bfloat16)], flops=1 << 36,
    )[0]


def finish_keys(key_grad, value_grad, back, rows, cols, count):
    own, width, edge = rows * cols, count * HEAD_DIM, RADIUS * cols

    def kernel(dk_ref, dv_ref, b_0, b_1, out_k, out_v):
        order = restore(rows, cols)
        row, col = own_query_cell(down(own), rows, cols)
        position = across(2 * edge)
        starts = [slot_side("lat", slot) * (own - edge) for slot in (0, 1)]
        cell = jnp.where(position < edge, position + starts[0], position - edge + starts[1])
        spread = jnp.where(row * cols + col == cell, 1.0, 0.0).astype(jnp.bfloat16)
        for part, (grad, out) in enumerate(((dk_ref, out_k), (dv_ref, out_v))):
            piece = slice(part * edge, (part + 1) * edge)
            for at in range(0, width, BLOCK):
                lanes = slice(at, at + BLOCK)
                arrived = jnp.concatenate([b_0[piece, lanes], b_1[piece, lanes]], axis=0)
                total = (grad[:, lanes] + dot(spread, arrived, (1, 0))).astype(jnp.bfloat16)
                out[:, lanes] = dot(order, total, (1, 0)).astype(jnp.bfloat16)

    return call(kernel, "finish_keys", (key_grad, value_grad, *back), [low(own, width)] * 2)


def swap(axis, slot, wrap, array):
    count = lax.axis_size(axis)
    pairs = []
    for lower in range(slot, count if wrap else count - 1, 2):
        upper = (lower + 1) % count
        pairs += [(lower, upper), (upper, lower)]
    return lax.ppermute(array, axis, pairs)


def swap_lon(slot, array):
    return swap("lon", 1 - slot, True, array)


def swap_lat(slot, array):
    return swap("lat", 1 - slot, False, array)


def after(value, *earlier):
    return lax.optimization_barrier((value, *earlier))[0]


def held(value, flops=1 << 36):
    spec = pl.BlockSpec(memory_space=pl.ANY)
    return call(
        lambda src, dst: None, "held", (value,), [jax.ShapeDtypeStruct(value.shape, value.dtype)],
        flops=flops, aliases={0: 0}, ins=[spec], outs=[spec],
    )[0]


def shards(queries, key_field, value_field, out_grad):
    rows, cols, width = queries.shape
    own = rows * cols
    flat = lambda x: x.reshape(own, width)
    queries, key_field, value_field, out_grad = map(flat, (queries, key_field, value_field, out_grad))
    size = (rows, cols, width // HEAD_DIM)

    qp, gp, *sends, key_field, value_field = pack_queries(queries, out_grad, key_field, value_field, *size)
    halo = [swap_lon(slot, send) for slot, send in enumerate(sends)]
    kp, vp, *sends = pack_keys(key_field, value_field, rows, cols)
    lat = [swap_lat(place & 1, send) for place, send in enumerate(sends)]
    own_stat, own_s, own_d = own_stats(qp, gp, kp, vp, lat, *size)

    def stats(group):
        mine, s, d = halo_stats(group, halo[group], own_stat, kp, vp, lat, *size)
        return mine, swap_lon(group, mine), s, d

    def query_grad(group, mine, theirs, s, d):
        return halo_query_grad(group, mine, theirs, s, d, kp, lat[:2], *size)

    def operands(group, mine, theirs, low_weights, low_grad):
        return (qp, gp, halo[group], mine, theirs, own_s, own_d, low_weights, low_grad, kp, *lat[:2])

    first, second = FIRST, 1 - FIRST
    dq, back = [None, None], [None, None]
    halo[first] = held(after(halo[first], own_stat))
    mine_a, theirs_a, s, d = stats(first)
    result, *lows_a = query_grad(first, mine_a, theirs_a, s, d)
    back[first] = held(swap_lon(first, result))
    halo[second] = held(after(halo[second], result))
    mine_b, theirs_b, s, d = stats(second)
    dq[first], key_part, value_part = first_grads(first, operands(first, mine_a, theirs_a, *lows_a), *size)
    result, *lows_b = query_grad(second, mine_b, after(theirs_b, key_part), s, d)
    back[second] = swap_lon(second, result)
    dq[second], dk, dv, *lat_back = second_grads(
        second, operands(second, mine_b, theirs_b, *lows_b), after(key_part, back[first]), value_part, *size
    )
    lat_back = [swap_lat(slot, send) for slot, send in enumerate(lat_back)]
    grad_query = finish_queries(dq, back, *size)
    grad_key, grad_value = finish_keys(dk, dv, lat_back, *size)
    shape = (rows, cols, width)
    return tuple(x.reshape(shape) for x in (grad_query, grad_key, grad_value))


def solution(mesh):
    spec = P("lat", "lon", None)
    return jax.shard_map(
        shards, mesh=mesh, in_specs=(spec,) * 4, out_specs=(spec,) * 3, check_vma=False
    )
```

```python
import math

import jax
import jax.numpy as jnp
from jax import lax
from jax.experimental import pallas as pl
from jax.experimental.pallas import tpu as pltpu
from jax.sharding import PartitionSpec as P

HEAD_DIM = 128
WINDOW = 13
RADIUS = WINDOW // 2
LANES = 128
FIRST = 0
MASKED = -1e30
LOG2E = math.log2(math.e)
VMEM_BYTES = 24 * 1024 * 1024


def split(index, width):
    if width & (width - 1) == 0:
        whole = index >> (width.bit_length() - 1)
    else:
        whole = (index * ((1 << 12) // width + 1)) >> 12
    return whole, index - whole * width


def odd(axis):
    return lax.axis_index(axis) & 1


def slot_side(axis, slot):
    parity = odd(axis)
    return parity if slot == 0 else 1 - parity


def own_query_cell(position, rows, cols):
    edge = rows * RADIUS
    group = position >> 7
    place = position & (LANES - 1)
    side = jnp.where(group == 0, slot_side("lon", 0), slot_side("lon", 1))
    row_a, col_a = split(place, RADIUS)
    inner = cols - 2 * RADIUS
    row_b, col_b = split(place - edge + (LANES - edge) * group, inner)
    at_edge = place < edge
    row = jnp.where(at_edge, row_a, row_b)
    col = jnp.where(at_edge, side * (cols - RADIUS) + col_a, RADIUS + col_b)
    return row, col


def halo_query_cell(position, rows, cols):
    edge = rows * RADIUS
    group = position >> 7
    place = position & (LANES - 1)
    side = jnp.where(group == 0, slot_side("lon", 0), slot_side("lon", 1))
    row, col = split(place, RADIUS)
    col = jnp.where(side == 1, cols, -RADIUS) + col
    col = jnp.where(place < edge, col, 1 << 12)
    return row, col


def lat_key_cell(slot, position, rows, cols):
    row, col = split(position, cols)
    return row + jnp.where(slot_side("lat", slot) == 1, rows, -RADIUS), col


def bias_of(key_cells, query_cells, rows):
    total_rows = rows * lax.axis_size("lat")
    first = rows * lax.axis_index("lat")
    key_row, key_col = key_cells
    query_row, query_col = query_cells
    start = jnp.clip(first + query_row - RADIUS, 0, total_rows - WINDOW)
    from_start = first + key_row - start
    inside = (from_start >= 0) & (from_start < WINDOW)
    inside = inside & (jnp.abs(key_col - query_col) <= RADIUS)
    return jnp.where(inside, 0.0, MASKED)


def down(count):
    return lax.broadcasted_iota(jnp.int32, (count, 1), 0)


def across(count, start=0):
    return lax.broadcasted_iota(jnp.int32, (1, count), 1) + start


def dot(a, b, contract):
    return lax.dot_general(a, b, ((contract[:1], contract[1:]), ((), ())), preferred_element_type=jnp.float32)


def call(kernel, name, operands, out_shapes, scratch=(), flops=0, aliases=None, outs=None, ins=None):
    return pl.pallas_call(
        kernel,
        name=name,
        in_specs=ins or [VMEM_SPEC] * len(operands),
        out_specs=outs or [VMEM_SPEC] * len(out_shapes),
        out_shape=out_shapes,
        scratch_shapes=scratch,
        input_output_aliases=aliases or {},
        compiler_params=pltpu.CompilerParams(vmem_limit_bytes=VMEM_BYTES),
        cost_estimate=pl.CostEstimate(flops=flops, bytes_accessed=0, transcendentals=0),
    )(*operands)


def low(*shape):
    return jax.ShapeDtypeStruct(shape, jnp.bfloat16)


def full(*shape):
    return jax.ShapeDtypeStruct(shape, jnp.float32)


def lanes_of(head, count=1):
    return slice(head * HEAD_DIM, (head + count) * HEAD_DIM)


def selection(row, col, rows, cols):
    source = across(rows * cols)
    return jnp.where(source == row * cols + col, 1.0, 0.0).astype(jnp.bfloat16)


HBM_SPEC, VMEM_SPEC = pl.BlockSpec(memory_space=pltpu.HBM), pl.BlockSpec(memory_space=pltpu.VMEM)
BLOCK = 2 * HEAD_DIM


def pack_queries(queries, out_grad, key_field, value_field, rows, cols, count):
    own, edge, width = rows * cols, rows * RADIUS, count * HEAD_DIM

    def kernel(q_hbm, g_hbm, k_hbm, v_hbm, qp_ref, gp_ref, send_0, send_1, k_ref, v_ref, q_ref, g_ref, sems):
        copies = [
            pltpu.make_async_copy(src, dst, sems.at[i])
            for i, (src, dst) in enumerate(
                ((q_hbm, q_ref), (g_hbm, g_ref), (k_hbm, k_ref), (v_hbm, v_ref))
            )
        ]
        for copy in copies:
            copy.start()
        order = selection(*own_query_cell(down(own), rows, cols), rows, cols)
        for place, (src, dst) in enumerate(((q_ref, qp_ref), (g_ref, gp_ref))):
            copies[place].wait()
            for at in range(0, width, BLOCK):
                here = slice(at, at + BLOCK)
                moved = dot(order, src[:, here], (1, 0)).astype(jnp.bfloat16)
                dst[:, here] = moved
                for group, send in enumerate((send_0, send_1)):
                    send[place * edge : (place + 1) * edge, here] = moved[group * LANES : group * LANES + edge]
        copies[2].wait()
        copies[3].wait()

    operands = [
        pltpu.with_memory_space_constraint(x, pltpu.HBM) for x in (queries, out_grad, key_field, value_field)
    ]
    return call(
        kernel, "pack_queries", operands,
        [low(own, width)] * 2 + [low(2 * edge, width)] * 2 + [low(own, width)] * 2,
        [pltpu.VMEM((own, width), jnp.bfloat16)] * 2 + [pltpu.SemaphoreType.DMA((4,))],
        ins=[HBM_SPEC] * 4,
    )


def pack_keys(key_field, value_field, rows, cols):
    own, edge = rows * cols, RADIUS * cols
    width = key_field.shape[1]

    def kernel(k_ref, v_ref, kp_ref, vp_ref, k_0, k_1, v_0, v_1):
        order = selection(*own_query_cell(down(own), rows, cols), rows, cols)
        for src, dst, sends in zip((k_ref, v_ref), (kp_ref, vp_ref), ((k_0, k_1), (v_0, v_1))):
            for slot, send in enumerate(sends):
                start = pl.multiple_of(slot_side("lat", slot) * (own - edge), 16)
                send[...] = src[pl.ds(start, edge), :]
            for at in range(0, width, BLOCK):
                here = slice(at, at + BLOCK)
                dst[:, here] = dot(order, src[:, here], (1, 0)).astype(jnp.bfloat16)

    return call(
        kernel, "pack_keys", (key_field, value_field),
        [low(own, width)] * 2 + [low(edge, width)] * 4,
    )


def halo_head(ref, edge, part, head):
    rows = ref[part * edge : (part + 1) * edge, lanes_of(head)]
    return jnp.concatenate([rows, jnp.zeros((LANES - edge, HEAD_DIM), jnp.bfloat16)], axis=0)


def near_keys(group, own_ref, lat_refs, head):
    lanes, edge = lanes_of(head), lat_refs[0].shape[0]
    pieces = [own_ref[group * LANES : group * LANES + edge, lanes]]
    return jnp.concatenate(pieces + [ref[:, lanes] for ref in lat_refs], axis=0)


def every_key(own_ref, lat_refs, head):
    lanes = lanes_of(head)
    return jnp.concatenate([ref[:, lanes] for ref in (own_ref, *lat_refs)], axis=0)


def fill_bias(bias, own_position, queries, rows, cols):
    at, edge = own_position.shape[0], RADIUS * cols
    bias[:at, :] = bias_of(own_query_cell(own_position, rows, cols), queries, rows)
    for slot in (0, 1):
        here = slice(at + slot * edge, at + (slot + 1) * edge)
        bias[here, :] = bias_of(lat_key_cell(slot, down(edge), rows, cols), queries, rows)


LOW, HIGH = slice(0, LANES), slice(LANES, 2 * LANES)
SCORE_SCALE = 1.0 / math.sqrt(HEAD_DIM)


def part_stats(scores, weight_grad):
    peak = jnp.max(scores, axis=0, keepdims=True)
    weights = jnp.exp2(scores - peak)
    total = jnp.sum(weights, axis=0, keepdims=True)
    dotted = jnp.sum(weights * weight_grad, axis=0, keepdims=True)
    return peak + jnp.log(total) * LOG2E, dotted / total


def stat_rows(count):
    return -(-2 * count // 8) * 8


def own_stats(qp, gp, kp, vp, lat, rows, cols, count):
    own, keys = rows * cols, (rows + 2 * RADIUS) * cols

    def kernel(q_ref, g_ref, k_ref, v_ref, k_0, k_1, v_0, v_1, out, s_ref, d_ref, bias):
        fill_bias(bias, down(own), own_query_cell(across(own), rows, cols), rows, cols)
        out[...] = jnp.zeros_like(out)
        for head in range(count):
            key = every_key(k_ref, (k_0, k_1), head)
            value = every_key(v_ref, (v_0, v_1), head)
            scores = dot(key, q_ref[:, lanes_of(head)], (1, 1)) * (SCORE_SCALE * LOG2E) + bias[...]
            weight_grad = dot(value, g_ref[:, lanes_of(head)], (1, 1))
            s_ref[head] = scores
            d_ref[head] = weight_grad
            log_total, delta = part_stats(scores, weight_grad)
            out[head : head + 1, :] = log_total
            out[count + head : count + head + 1, :] = delta

    return call(
        kernel, "own_stats", (qp, gp, kp, vp, *lat),
        [full(stat_rows(count), own)] + [full(count, keys, own)] * 2,
        [pltpu.VMEM((keys, own), jnp.float32)],
    )


def halo_stats(group, halo, own_stat, kp, vp, lat, rows, cols, count):
    edge = RADIUS * rows
    near = edge + 2 * RADIUS * cols

    def kernel(halo_ref, stat, k_ref, v_ref, k_0, k_1, v_0, v_1, out, s_ref, d_ref, bias):
        queries = halo_query_cell(across(LANES, group * LANES), rows, cols)
        fill_bias(bias, down(edge) + group * LANES, queries, rows, cols)
        out[:, LOW] = stat[:, group * LANES : (group + 1) * LANES]
        out[:, HIGH] = jnp.zeros((out.shape[0], LANES), jnp.float32)
        for head in range(count):
            key = near_keys(group, k_ref, (k_0, k_1), head)
            value = near_keys(group, v_ref, (v_0, v_1), head)
            scores = dot(key, halo_head(halo_ref, edge, 0, head), (1, 1)) * (SCORE_SCALE * LOG2E) + bias[...]
            weight_grad = dot(value, halo_head(halo_ref, edge, 1, head), (1, 1))
            s_ref[head] = scores
            d_ref[head] = weight_grad
            log_total, delta = part_stats(scores, weight_grad)
            out[head : head + 1, HIGH] = log_total
            out[count + head : count + head + 1, HIGH] = delta

    return call(
        kernel, f"halo_stats_{group}", (halo, own_stat, kp, vp, *lat),
        [full(stat_rows(count), 2 * LANES)] + [full(count, near, LANES)] * 2,
        [pltpu.VMEM((near, LANES), jnp.float32)],
    )


def combined(mine, theirs, count):
    a, b = mine[:count], theirs[:count]
    peak = jnp.maximum(a, b)
    part_a, part_b = jnp.exp2(a - peak), jnp.exp2(b - peak)
    total = part_a + part_b
    delta = (part_a * mine[count : 2 * count] + part_b * theirs[count : 2 * count]) / total
    return peak + jnp.log(total) * LOG2E, delta


def gradients(scores, weight_grad, log_total, delta):
    weights = jnp.exp2(scores - log_total)
    return weights.astype(jnp.bfloat16), (weights * (weight_grad - delta)).astype(jnp.bfloat16)


def halo_query_grad(group, mine, theirs, scores, weight_grad, kp, lat, rows, cols, count):
    edge = RADIUS * rows

    def kernel(m, t, s_ref, d_ref, k_ref, lat_0, lat_1, out, p_ref, g_ref):
        log_total, delta = combined(m[:, HIGH], t[:, LOW], count)
        for head in range(count):
            here = slice(head, head + 1)
            p_ref[head], grad = gradients(s_ref[head], d_ref[head], log_total[here], delta[here])
            g_ref[head] = grad
            key = near_keys(group, k_ref, (lat_0, lat_1), head)
            query_grad = dot(grad, key, (0, 0)) * SCORE_SCALE
            out[:, lanes_of(head)] = query_grad[:edge].astype(jnp.bfloat16)

    return call(
        kernel, f"halo_query_grad_{group}", (mine, theirs, scores, weight_grad, kp, *lat),
        [low(edge, count * HEAD_DIM)] + [low(count, *scores.shape[1:])] * 2,
    )


def group_grads(group, refs, dq_ref, use, rows, cols, count):
    q_ref, g_ref, halo_ref, m, t, s_ref, d_ref, p_ref, l_ref, k_ref, *lat_refs = refs
    own, edge = rows * cols, RADIUS * rows
    here = slice(group * LANES, (group + 1) * LANES)
    near = slice(group * LANES, group * LANES + edge)
    logs, deltas = combined(m[:, LOW], t[:, HIGH], count)
    for head in range(count):
        row, lanes = slice(head, head + 1), lanes_of(head)
        weights, grad = gradients(s_ref[head, :, here], d_ref[head, :, here], logs[row], deltas[row])
        dq_ref[:, lanes] = dot(grad, every_key(k_ref, lat_refs, head), (0, 0)) * SCORE_SCALE
        for part, (own_low, halo_low, own_ref) in enumerate(((grad, l_ref, q_ref), (weights, p_ref, g_ref))):
            own_rows = own_ref[here, lanes]
            both = jnp.concatenate([own_rows, halo_head(halo_ref, edge, part, head)], axis=0)
            met = jnp.concatenate([own_low[near], own_low[own:]], axis=0)
            met = dot(jnp.concatenate([met, halo_low[head]], axis=1), both, (1, 0))
            apart = [] if group == 0 else [dot(own_low[: group * LANES], own_rows, (1, 0))]
            apart.append(dot(own_low[near.stop : own], own_rows, (1, 0)))
            use(part, head, lanes, jnp.concatenate(apart[:-1] + [met[:edge], apart[-1]], axis=0), met[edge:])


def first_grads(group, operands, rows, cols, count):
    own, keys, width = rows * cols, (rows + 2 * RADIUS) * cols, count * HEAD_DIM

    def kernel(*refs):
        *refs, dq_ref, dk_ref, dv_ref = refs

        def use(part, head, lanes, inside, outside):
            result = (dk_ref, dv_ref)[part]
            result[:own, lanes] = inside
            result[own:, lanes] = outside

        group_grads(group, refs, dq_ref, use, rows, cols, count)

    return call(kernel, "first_grads", operands, [full(LANES, width)] + [full(keys, width)] * 2)


def second_grads(group, operands, key_part, value_part, rows, cols, count):
    own, width, edge = rows * cols, count * HEAD_DIM, RADIUS * cols

    def kernel(*refs):
        *refs, kpart, vpart, dq_ref, dk_ref, dv_ref, out_0, out_1 = refs

        def use(part, head, lanes, inside, outside):
            before, result, scale = ((kpart, dk_ref, SCORE_SCALE), (vpart, dv_ref, 1.0))[part]
            result[:, lanes] = (inside + before[:own, lanes]) * scale
            outside = (outside + before[own:, lanes]) * scale
            for slot, out in enumerate((out_0, out_1)):
                out[part * edge : (part + 1) * edge, lanes] = outside[
                    slot * edge : (slot + 1) * edge
                ].astype(jnp.bfloat16)

        group_grads(group, refs, dq_ref, use, rows, cols, count)

    return call(
        kernel, "second_grads", (*operands, key_part, value_part),
        [full(LANES, width)] + [full(own, width)] * 2 + [low(2 * edge, width)] * 2,
    )


def restore(rows, cols):
    own = rows * cols
    row, col = own_query_cell(across(own), rows, cols)
    return jnp.where(down(own) == row * cols + col, 1.0, 0.0).astype(jnp.bfloat16)


def finish_queries(grads, back, rows, cols, count):
    own, edge, width = rows * cols, rows * RADIUS, count * HEAD_DIM

    def kernel(g_0, g_1, b_0, b_1, out, total):
        order = restore(rows, cols)
        for group, (grad, arrived) in enumerate(((g_0, b_0), (g_1, b_1))):
            at = group * LANES
            total[at : at + edge, :] = (grad[:edge, :] + arrived[...].astype(jnp.float32)).astype(jnp.bfloat16)
            total[at + edge : at + LANES, :] = grad[edge:, :].astype(jnp.bfloat16)
        for at in range(0, width, 256):
            lanes = slice(at, at + 256)
            out[:, lanes] = dot(order, total[:, lanes], (1, 0)).astype(jnp.bfloat16)

    return call(
        kernel, "finish_queries", (*grads, *back), [low(own, width)],
        [pltpu.VMEM((own, width), jnp.bfloat16)], flops=1 << 36,
    )[0]


def finish_keys(key_grad, value_grad, back, rows, cols, count):
    own, width, edge = rows * cols, count * HEAD_DIM, RADIUS * cols

    def kernel(dk_ref, dv_ref, b_0, b_1, out_k, out_v):
        order = restore(rows, cols)
        row, col = own_query_cell(down(own), rows, cols)
        position = across(2 * edge)
        starts = [slot_side("lat", slot) * (own - edge) for slot in (0, 1)]
        cell = jnp.where(position < edge, position + starts[0], position - edge + starts[1])
        spread = jnp.where(row * cols + col == cell, 1.0, 0.0).astype(jnp.bfloat16)
        for part, (grad, out) in enumerate(((dk_ref, out_k), (dv_ref, out_v))):
            piece = slice(part * edge, (part + 1) * edge)
            for at in range(0, width, BLOCK):
                lanes = slice(at, at + BLOCK)
                arrived = jnp.concatenate([b_0[piece, lanes], b_1[piece, lanes]], axis=0)
                total = (grad[:, lanes] + dot(spread, arrived, (1, 0))).astype(jnp.bfloat16)
                out[:, lanes] = dot(order, total, (1, 0)).astype(jnp.bfloat16)

    return call(kernel, "finish_keys", (key_grad, value_grad, *back), [low(own, width)] * 2)


def swap(axis, slot, wrap, array):
    count = lax.axis_size(axis)
    pairs = []
    for lower in range(slot, count if wrap else count - 1, 2):
        upper = (lower + 1) % count
        pairs += [(lower, upper), (upper, lower)]
    return lax.ppermute(array, axis, pairs)


def swap_lon(slot, array):
    return swap("lon", 1 - slot, True, array)


def swap_lat(slot, array):
    return swap("lat", 1 - slot, False, array)


def after(value, *earlier):
    return lax.optimization_barrier((value, *earlier))[0]


def held(value, flops=1 << 36):
    spec = pl.BlockSpec(memory_space=pl.ANY)
    return call(
        lambda src, dst: None, "held", (value,), [jax.ShapeDtypeStruct(value.shape, value.dtype)],
        flops=flops, aliases={0: 0}, ins=[spec], outs=[spec],
    )[0]


def shards(queries, key_field, value_field, out_grad):
    rows, cols, width = queries.shape
    own = rows * cols
    flat = lambda x: x.reshape(own, width)
    queries, key_field, value_field, out_grad = map(flat, (queries, key_field, value_field, out_grad))
    size = (rows, cols, width // HEAD_DIM)

    qp, gp, *sends, key_field, value_field = pack_queries(queries, out_grad, key_field, value_field, *size)
    halo = [swap_lon(slot, send) for slot, send in enumerate(sends)]
    kp, vp, *sends = pack_keys(key_field, value_field, rows, cols)
    lat = [swap_lat(place & 1, send) for place, send in enumerate(sends)]
    own_stat, own_s, own_d = own_stats(qp, gp, kp, vp, lat, *size)

    def stats(group):
        mine, s, d = halo_stats(group, halo[group], own_stat, kp, vp, lat, *size)
        return mine, swap_lon(group, mine), s, d

    def query_grad(group, mine, theirs, s, d):
        return halo_query_grad(group, mine, theirs, s, d, kp, lat[:2], *size)

    def operands(group, mine, theirs, low_weights, low_grad):
        return (qp, gp, halo[group], mine, theirs, own_s, own_d, low_weights, low_grad, kp, *lat[:2])

    first, second = FIRST, 1 - FIRST
    dq, back = [None, None], [None, None]
    halo[first] = held(after(halo[first], own_stat))
    mine_a, theirs_a, s, d = stats(first)
    result, *lows_a = query_grad(first, mine_a, theirs_a, s, d)
    result_a = result
    halo[second] = held(after(halo[second], result_a))
    mine_b, theirs_b, s, d = stats(second)
    back[first] = swap_lon(first, after(result_a, mine_b))
    dq[first], key_part, value_part = first_grads(first, operands(first, mine_a, theirs_a, *lows_a), *size)
    theirs_b = held(after(theirs_b, key_part))
    result, *lows_b = query_grad(second, mine_b, theirs_b, s, d)
    back[second] = swap_lon(second, result)
    dq[second], dk, dv, *lat_back = second_grads(
        second, operands(second, mine_b, theirs_b, *lows_b), key_part, value_part, *size
    )
    lat_back = [swap_lat(slot, send) for slot, send in enumerate(lat_back)]
    grad_query = finish_queries(dq, back, *size)
    grad_key, grad_value = finish_keys(dk, dv, lat_back, *size)
    shape = (rows, cols, width)
    return tuple(x.reshape(shape) for x in (grad_query, grad_key, grad_value))


def solution(mesh):
    spec = P("lat", "lon", None)
    return jax.shard_map(
        shards, mesh=mesh, in_specs=(spec,) * 4, out_specs=(spec,) * 3, check_vma=False
    )
```

```python
import math

import jax
import jax.numpy as jnp
from jax import lax
from jax.experimental import pallas as pl
from jax.experimental.pallas import tpu as pltpu
from jax.sharding import PartitionSpec as P

HEAD_DIM = 128
WINDOW = 13
RADIUS = WINDOW // 2
LANES = 128
MASKED = -1e30
LOG2E = math.log2(math.e)
VMEM_BYTES = 16 * 1024 * 1024


def split(index, width):
    if width & (width - 1) == 0:
        whole = index >> (width.bit_length() - 1)
    else:
        whole = (index * ((1 << 12) // width + 1)) >> 12
    return whole, index - whole * width


def odd(axis):
    return lax.axis_index(axis) & 1


def slot_side(axis, slot):
    parity = odd(axis)
    return parity if slot == (0 if axis == "lon" else 1) else 1 - parity


def own_query_cell(position, rows, cols):
    edge = rows * RADIUS
    group = position >> 7
    place = position & (LANES - 1)
    side = jnp.where(group == 0, slot_side("lon", 0), slot_side("lon", 1))
    row_a, col_a = split(place, RADIUS)
    inner = cols - 2 * RADIUS
    row_b, col_b = split(place - edge + (LANES - edge) * group, inner)
    at_edge = place < edge
    row = jnp.where(at_edge, row_a, row_b)
    col = jnp.where(at_edge, side * (cols - RADIUS) + col_a, RADIUS + col_b)
    return row, col


def halo_query_cell(position, rows, cols):
    edge = rows * RADIUS
    group = position >> 7
    place = position & (LANES - 1)
    side = jnp.where(group == 0, slot_side("lon", 0), slot_side("lon", 1))
    row, col = split(place, RADIUS)
    col = jnp.where(side == 1, cols, -RADIUS) + col
    col = jnp.where(place < edge, col, 1 << 12)
    return row, col


def lat_key_cell(slot, position, rows, cols):
    row, col = split(position, cols)
    return row + jnp.where(slot_side("lat", slot) == 1, rows, -RADIUS), col


def bias_of(key_cells, query_cells, rows):
    total_rows = rows * lax.axis_size("lat")
    first = rows * lax.axis_index("lat")
    key_row, key_col = key_cells
    query_row, query_col = query_cells
    start = jnp.clip(first + query_row - RADIUS, 0, total_rows - WINDOW)
    from_start = first + key_row - start
    inside = (from_start >= 0) & (from_start < WINDOW)
    inside = inside & (jnp.abs(key_col - query_col) <= RADIUS)
    return jnp.where(inside, 0.0, MASKED)


def down(count):
    return lax.broadcasted_iota(jnp.int32, (count, 1), 0)


def across(count, start=0):
    return lax.broadcasted_iota(jnp.int32, (1, count), 1) + start


def dot(a, b, contract):
    return lax.dot_general(a, b, ((contract[:1], contract[1:]), ((), ())), preferred_element_type=jnp.float32)


def call(kernel, name, operands, out_shapes, scratch=(), flops=0, aliases=None, outs=None, ins=None):
    return pl.pallas_call(
        kernel,
        name=name,
        in_specs=ins or [VMEM_SPEC] * len(operands),
        out_specs=outs or [VMEM_SPEC] * len(out_shapes),
        out_shape=out_shapes,
        scratch_shapes=scratch,
        input_output_aliases=aliases or {},
        compiler_params=pltpu.CompilerParams(vmem_limit_bytes=VMEM_BYTES),
        cost_estimate=pl.CostEstimate(flops=flops, bytes_accessed=0, transcendentals=0),
    )(*operands)


def low(*shape):
    return jax.ShapeDtypeStruct(shape, jnp.bfloat16)


def full(*shape):
    return jax.ShapeDtypeStruct(shape, jnp.float32)


def lanes_of(head, count=1):
    return slice(head * HEAD_DIM, (head + count) * HEAD_DIM)


def selection(row, col, rows, cols):
    source = across(rows * cols)
    return jnp.where(source == row * cols + col, 1.0, 0.0).astype(jnp.bfloat16)


HBM_SPEC, VMEM_SPEC = pl.BlockSpec(memory_space=pltpu.HBM), pl.BlockSpec(memory_space=pltpu.VMEM)
BLOCK = 2 * HEAD_DIM


def pack_queries(queries, out_grad, key_field, value_field, rows, cols, count):
    own, edge, width = rows * cols, rows * RADIUS, count * HEAD_DIM
    lat_edge = RADIUS * cols

    def kernel(
        q_hbm, g_hbm, k_hbm, v_hbm, qp_ref, gp_ref, send_0, send_1, k_ref, v_ref, k_0, k_1, v_0, v_1, q_ref, g_ref, sems
    ):
        copies = [
            pltpu.make_async_copy(src, dst, sems.at[i])
            for i, (src, dst) in enumerate(
                ((q_hbm, q_ref), (g_hbm, g_ref), (k_hbm, k_ref), (v_hbm, v_ref))
            )
        ]
        for copy in copies:
            copy.start()
        order = selection(*own_query_cell(down(own), rows, cols), rows, cols)
        for place, (src, dst) in enumerate(((q_ref, qp_ref), (g_ref, gp_ref))):
            copies[place].wait()
            for at in range(0, width, BLOCK):
                here = slice(at, at + BLOCK)
                moved = dot(order, src[:, here], (1, 0)).astype(jnp.bfloat16)
                dst[:, here] = moved
                for group, send in enumerate((send_0, send_1)):
                    send[place * edge : (place + 1) * edge, here] = moved[group * LANES : group * LANES + edge]
        for copy, src, sends in zip(copies[2:], (k_ref, v_ref), ((k_0, k_1), (v_0, v_1))):
            copy.wait()
            for slot, send in enumerate(sends):
                start = pl.multiple_of(slot_side("lat", slot) * (own - lat_edge), 16)
                send[...] = src[pl.ds(start, lat_edge), :]

    operands = [
        pltpu.with_memory_space_constraint(x, pltpu.HBM) for x in (queries, out_grad, key_field, value_field)
    ]
    return call(
        kernel, "pack_queries", operands,
        [low(own, width)] * 2 + [low(2 * edge, width)] * 2 + [low(own, width)] * 2 + [low(lat_edge, width)] * 4,
        [pltpu.VMEM((own, width), jnp.bfloat16)] * 2 + [pltpu.SemaphoreType.DMA((4,))],
        ins=[HBM_SPEC] * 4,
    )


def own_scores(qp, gp, key_field, value_field, rows, cols, count):
    own, width = rows * cols, key_field.shape[1]

    def kernel(q_ref, g_ref, k_ref, v_ref, kp_ref, vp_ref, out_0, out_1, s_ref, d_ref, bias):
        order = selection(*own_query_cell(down(own), rows, cols), rows, cols)
        for src, dst in ((k_ref, kp_ref), (v_ref, vp_ref)):
            for at in range(0, width, BLOCK):
                here = slice(at, at + BLOCK)
                dst[:, here] = dot(order, src[:, here], (1, 0)).astype(jnp.bfloat16)
        bias[...] = bias_of(
            own_query_cell(down(own), rows, cols), own_query_cell(across(own), rows, cols), rows
        )
        for out in (out_0, out_1):
            out[...] = jnp.zeros_like(out)
        for head in range(count):
            lanes = lanes_of(head)
            s_ref[head] = dot(kp_ref[:, lanes], q_ref[:, lanes], (1, 1)) * (SCORE_SCALE * LOG2E) + bias[...]
            d_ref[head] = dot(vp_ref[:, lanes], g_ref[:, lanes], (1, 1))
            put_stats((out_0, out_1), head, part_stats(s_ref[head], d_ref[head]), count)

    return call(
        kernel, "own_scores", (qp, gp, key_field, value_field),
        [low(own, width)] * 2 + [full(stat_rows(count), LANES)] * 2 + [full(count, own, own)] * 2,
        [pltpu.VMEM((own, own), jnp.float32)],
    )


def put_stats(outs, head, stats, count):
    for out, half in zip(outs, (LOW, HIGH)):
        for at, stat in zip((head, count + head), stats):
            out[at : at + 1, :] = stat[:, half]


def halo_head(ref, edge, part, head):
    rows = ref[part * edge : (part + 1) * edge, lanes_of(head)]
    return jnp.concatenate([rows, jnp.zeros((LANES - edge, HEAD_DIM), jnp.bfloat16)], axis=0)


def near_keys(group, own_ref, lat_refs, head):
    lanes, edge = lanes_of(head), lat_refs[0].shape[0]
    pieces = [own_ref[group * LANES : group * LANES + edge, lanes]]
    return jnp.concatenate(pieces + [ref[:, lanes] for ref in lat_refs], axis=0)


def every_key(own_ref, lat_refs, head):
    lanes = lanes_of(head)
    return jnp.concatenate([ref[:, lanes] for ref in (own_ref, *lat_refs)], axis=0)


def fill_bias(bias, own_position, queries, rows, cols):
    at, edge = own_position.shape[0], RADIUS * cols
    bias[:at, :] = bias_of(own_query_cell(own_position, rows, cols), queries, rows)
    for slot in (0, 1):
        here = slice(at + slot * edge, at + (slot + 1) * edge)
        bias[here, :] = bias_of(lat_key_cell(slot, down(edge), rows, cols), queries, rows)


LOW, HIGH = slice(0, LANES), slice(LANES, 2 * LANES)
SCORE_SCALE = 1.0 / math.sqrt(HEAD_DIM)


def part_stats(scores, weight_grad):
    peak = jnp.max(scores, axis=0, keepdims=True)
    weights = jnp.exp2(scores - peak)
    total = jnp.sum(weights, axis=0, keepdims=True)
    dotted = jnp.sum(weights * weight_grad, axis=0, keepdims=True)
    return peak + jnp.log(total) * LOG2E, dotted / total


def stat_rows(count):
    return -(-2 * count // 8) * 8


def lat_scores(qp, gp, lat, stats, rows, cols, count):
    own, lat_edge = rows * cols, RADIUS * cols

    def kernel(q_ref, g_ref, k_0, k_1, v_0, v_1, before_0, before_1, out_0, out_1, s_ref, d_ref, bias, part_0, part_1):
        queries = own_query_cell(across(own), rows, cols)
        for slot in (0, 1):
            cells = lat_key_cell(slot, down(lat_edge), rows, cols)
            bias[slot * lat_edge : (slot + 1) * lat_edge, :] = bias_of(cells, queries, rows)
        for head in range(count):
            lanes = lanes_of(head)
            key, value = (
                jnp.concatenate([ref[:, lanes] for ref in pair], axis=0) for pair in ((k_0, k_1), (v_0, v_1))
            )
            s_ref[head] = dot(key, q_ref[:, lanes], (1, 1)) * (SCORE_SCALE * LOG2E) + bias[...]
            d_ref[head] = dot(value, g_ref[:, lanes], (1, 1))
            put_stats((part_0, part_1), head, part_stats(s_ref[head], d_ref[head]), count)
        for out, part, before in ((out_0, part_0, before_0), (out_1, part_1, before_1)):
            out[...] = jnp.zeros_like(out)
            out[:count, :], out[count : 2 * count, :] = stats_of(part, before, count)

    return call(
        kernel, "lat_scores", (qp, gp, *lat, *stats),
        [full(stat_rows(count), LANES)] * 2 + [full(count, 2 * lat_edge, own)] * 2,
        [pltpu.VMEM((2 * lat_edge, own), jnp.float32)] + [pltpu.VMEM((stat_rows(count), LANES), jnp.float32)] * 2,
    )


def combined(mine, theirs):
    (a, delta_a), (b, delta_b) = mine, theirs
    peak = jnp.maximum(a, b)
    part_a, part_b = jnp.exp2(a - peak), jnp.exp2(b - peak)
    total = part_a + part_b
    return peak + jnp.log(total) * LOG2E, (part_a * delta_a + part_b * delta_b) / total


def halo_grads(group, halo, theirs, kp, vp, lat, rows, cols, count, pad=0):
    edge = RADIUS * rows
    near = edge + 2 * RADIUS * cols

    def kernel(halo_ref, stat, k_ref, v_ref, k_0, k_1, v_0, v_1, out, mine, p_ref, g_ref, bias, s_ref, d_ref):
        queries = halo_query_cell(across(LANES, group * LANES), rows, cols)
        fill_bias(bias, down(edge) + group * LANES, queries, rows, cols)
        mine[...] = jnp.zeros_like(mine)
        for head in range(count):
            key = near_keys(group, k_ref, (k_0, k_1), head)
            value = near_keys(group, v_ref, (v_0, v_1), head)
            s_ref[head] = dot(key, halo_head(halo_ref, edge, 0, head), (1, 1)) * (SCORE_SCALE * LOG2E) + bias[...]
            d_ref[head] = dot(value, halo_head(halo_ref, edge, 1, head), (1, 1))
            log_total, delta = part_stats(s_ref[head], d_ref[head])
            mine[head : head + 1, :] = log_total
            mine[count + head : count + head + 1, :] = delta
        log_total, delta = combined(*((x[:count, :], x[count : 2 * count, :]) for x in (mine, stat)))
        for head in range(count):
            row = slice(head, head + 1)
            p_ref[head], grad = gradients(s_ref[head], d_ref[head], log_total[row], delta[row])
            g_ref[head] = grad
            query_grad = dot(grad, near_keys(group, k_ref, (k_0, k_1), head), (0, 0)) * SCORE_SCALE
            out[:, lanes_of(head)] = query_grad[:edge].astype(jnp.bfloat16)

    return call(
        kernel, f"halo_grads_{group}", (halo, theirs, kp, vp, *lat),
        [pltpu.VMEM((edge, count * HEAD_DIM), jnp.bfloat16), full(stat_rows(count) + pad, LANES)]
        + [low(count, near, LANES)] * 2,
        [pltpu.VMEM((near, LANES), jnp.float32)] + [pltpu.VMEM((count, near, LANES), jnp.float32)] * 2,
    )


def halo_scores(group, halo, own_stat, kp, vp, lat, rows, cols, count):
    edge = RADIUS * rows
    near = edge + 2 * RADIUS * cols

    def kernel(halo_ref, stat, k_ref, v_ref, k_0, k_1, v_0, v_1, out, s_ref, d_ref, bias):
        queries = halo_query_cell(across(LANES, group * LANES), rows, cols)
        fill_bias(bias, down(edge) + group * LANES, queries, rows, cols)
        out[:, LOW] = stat[...]
        out[:, HIGH] = jnp.zeros((out.shape[0], LANES), jnp.float32)
        for head in range(count):
            key = near_keys(group, k_ref, (k_0, k_1), head)
            value = near_keys(group, v_ref, (v_0, v_1), head)
            s_ref[head] = dot(key, halo_head(halo_ref, edge, 0, head), (1, 1)) * (SCORE_SCALE * LOG2E) + bias[...]
            d_ref[head] = dot(value, halo_head(halo_ref, edge, 1, head), (1, 1))
            log_total, delta = part_stats(s_ref[head], d_ref[head])
            out[head : head + 1, HIGH] = log_total
            out[count + head : count + head + 1, HIGH] = delta

    return call(
        kernel, f"halo_scores_{group}", (halo, own_stat, kp, vp, *lat),
        [full(stat_rows(count), 2 * LANES)] + [full(count, near, LANES)] * 2,
        [pltpu.VMEM((near, LANES), jnp.float32)],
    )


def halo_finish(group, mine, theirs, scores, weight_grad, kp, lat, rows, cols, count):
    edge = RADIUS * rows

    def kernel(m, t, s_ref, d_ref, k_ref, k_0, k_1, out, final, p_ref, g_ref):
        final[...] = jnp.zeros_like(final)
        logs, deltas = combined(*((x[:count, half], x[count : 2 * count, half]) for x, half in ((m, LOW), (t, HIGH))))
        final[:count, :] = logs
        final[count : 2 * count, :] = deltas
        logs, deltas = combined(*((x[:count, half], x[count : 2 * count, half]) for x, half in ((m, HIGH), (t, LOW))))
        for head in range(count):
            row = slice(head, head + 1)
            p_ref[head], grad = gradients(s_ref[head], d_ref[head], logs[row], deltas[row])
            g_ref[head] = grad
            query_grad = dot(grad, near_keys(group, k_ref, (k_0, k_1), head), (0, 0)) * SCORE_SCALE
            out[:, lanes_of(head)] = query_grad[:edge].astype(jnp.bfloat16)

    return call(
        kernel, f"halo_finish_{group}", (mine, theirs, scores, weight_grad, kp, *lat),
        [low(edge, count * HEAD_DIM), full(stat_rows(count), LANES)] + [low(count, *scores.shape[1:])] * 2,
    )


def gradients(scores, weight_grad, log_total, delta):
    weights = jnp.exp2(scores - log_total)
    return weights.astype(jnp.bfloat16), (weights * (weight_grad - delta)).astype(jnp.bfloat16)


def stats_of(mine, theirs, count):
    return combined(*((x[:count, :], x[count : 2 * count, :]) for x in (mine, theirs)))


def first_grads(qp, gp, halo, stats, scores, weight_grad, lows, kp, lat, rows, cols, count):
    own, width, edge = rows * cols, count * HEAD_DIM, RADIUS * rows
    keys = own + 2 * RADIUS * cols

    def kernel(
        q_ref, g_ref, h_ref, stat, s_own, s_lat, d_own, d_lat, p_ref, l_ref, k_ref, k_0, k_1, dq_ref, dk_ref, dv_ref
    ):
        for head in range(count):
            row, lanes = slice(head, head + 1), lanes_of(head)
            logs, deltas = stat[row, :], stat[count + head : count + head + 1, :]
            own_p, own_l = gradients(s_own[head, :, LOW], d_own[head, :, LOW], logs, deltas)
            lat_p, lat_l = gradients(s_lat[head, :, LOW], d_lat[head, :, LOW], logs, deltas)
            every = jnp.concatenate([own_l, lat_l], axis=0)
            dq_ref[:, lanes] = dot(every, every_key(k_ref, (k_0, k_1), head), (0, 0)) * SCORE_SCALE
            sides = ((own_l, lat_l, l_ref, q_ref, dk_ref), (own_p, lat_p, p_ref, g_ref, dv_ref))
            for part, (low_own, low_lat, low_halo, own_ref, result) in enumerate(sides):
                own_rows = own_ref[LOW, lanes]
                both = jnp.concatenate([own_rows, halo_head(h_ref, edge, part, head)], axis=0)
                met = jnp.concatenate([low_own[:edge], low_lat], axis=0)
                met = dot(jnp.concatenate([met, low_halo[head]], axis=1), both, (1, 0))
                result[:edge, lanes] = met[:edge]
                result[own:, lanes] = met[edge:]
                result[edge:own, lanes] = dot(low_own[edge:own], own_rows, (1, 0))

    return call(
        kernel, "first_grads", (qp, gp, halo, stats, *scores, *weight_grad, *lows, kp, *lat),
        [full(LANES, width)] + [full(keys, width)] * 2,
    )


def lat_grads(qp, gp, halo, mine, theirs, scores, weight_grad, lows, key_part, value_part, rows, cols, count):
    own, width, edge, lat_edge = rows * cols, count * HEAD_DIM, RADIUS * rows, RADIUS * cols

    def kernel(q_ref, g_ref, h_ref, m, t, s_ref, d_ref, p_ref, l_ref, kpart, vpart, out_0, out_1, final, lat_low):
        logs, deltas = stats_of(m, t, count)
        final[...] = jnp.zeros_like(final)
        final[:count, :], final[count : 2 * count, :] = logs, deltas
        for head in range(count):
            row, lanes = slice(head, head + 1), lanes_of(head)
            weights, grad = gradients(s_ref[head, :, HIGH], d_ref[head, :, HIGH], logs[row], deltas[row])
            lat_low[head] = grad
            sides = ((grad, l_ref, q_ref, kpart, SCORE_SCALE), (weights, p_ref, g_ref, vpart, 1.0))
            for part, (low_lat, low_halo, own_ref, before, scale) in enumerate(sides):
                both = jnp.concatenate([own_ref[HIGH, lanes], halo_head(h_ref, edge, part, head)], axis=0)
                met = jnp.concatenate([low_lat, low_halo[head, edge:, :]], axis=1)
                outside = ((dot(met, both, (1, 0)) + before[own:, lanes]) * scale).astype(jnp.bfloat16)
                for slot, out in enumerate((out_0, out_1)):
                    out[part * lat_edge : (part + 1) * lat_edge, lanes] = outside[
                        slot * lat_edge : (slot + 1) * lat_edge
                    ]

    return call(
        kernel, "lat_grads", (qp, gp, halo, mine, theirs, scores, weight_grad, *lows, key_part, value_part),
        [low(2 * lat_edge, width)] * 2 + [full(stat_rows(count), LANES), low(count, 2 * lat_edge, LANES)],
    )


def second_grads(qp, gp, halo, stats, lat_low, scores, weight_grad, lows, kp, lat, parts, rows, cols, count):
    own, width, edge = rows * cols, count * HEAD_DIM, RADIUS * rows

    def kernel(
        q_ref, g_ref, h_ref, stat, lat_ref, s_ref, d_ref, p_ref, l_ref, k_ref, k_0, k_1, dq_0, kpart, vpart,
        dq_ref, dk_ref, dv_ref, sums,
    ):
        near = slice(LANES, LANES + edge)
        order = restore(rows, cols)
        twice = jnp.concatenate([order, order], axis=1)

        for head in range(count):
            row, lanes = slice(head, head + 1), lanes_of(head)
            logs, deltas = stat[row, :], stat[count + head : count + head + 1, :]
            own_p, own_l = gradients(s_ref[head, :, HIGH], d_ref[head, :, HIGH], logs, deltas)
            every = jnp.concatenate([own_l, lat_ref[head]], axis=0)
            dq_1 = dot(every, every_key(k_ref, (k_0, k_1), head), (0, 0)) * SCORE_SCALE
            sums[0, :LANES, lanes], sums[0, LANES:, lanes] = dq_0[:, lanes], dq_1
            sides = ((own_l, l_ref, q_ref, kpart, SCORE_SCALE), (own_p, p_ref, g_ref, vpart, 1.0))
            for part, (low_own, low_halo, own_ref, before, scale) in enumerate(sides):
                own_rows = own_ref[HIGH, lanes]
                both = jnp.concatenate([own_rows, halo_head(h_ref, edge, part, head)], axis=0)
                met = jnp.concatenate([low_own[near], low_halo[head, :edge, :]], axis=1)
                pieces = (
                    (slice(0, LANES), dot(low_own[:LANES], own_rows, (1, 0))),
                    (near, dot(met, both, (1, 0))),
                    (slice(near.stop, own), dot(low_own[near.stop : own], own_rows, (1, 0))),
                )
                for here, piece in pieces:
                    sums[1 + part, here, lanes] = (piece + before[here, lanes]) * scale
        for place, result in enumerate((dq_ref, dk_ref, dv_ref)):
            for at in range(0, width, BLOCK):
                value = sums[place, :, at : at + BLOCK]
                high = value.astype(jnp.bfloat16)
                rest = (value - high.astype(jnp.float32)).astype(jnp.bfloat16)
                result[:, at : at + BLOCK] = dot(twice, jnp.concatenate([high, rest], axis=0), (1, 0))

    return call(
        kernel, "second_grads", (qp, gp, halo, stats, lat_low, scores, weight_grad, *lows, kp, *lat, *parts),
        [full(own, width)] * 3, [pltpu.VMEM((3, own, width), jnp.float32)],
    )


def restore(rows, cols):
    own = rows * cols
    row, col = own_query_cell(across(own), rows, cols)
    return jnp.where(down(own) == row * cols + col, 1.0, 0.0).astype(jnp.bfloat16)


def finish(query_grad, back, key_grad, value_grad, lat_back, rows, cols, count):
    own, width, edge, lat_edge = rows * cols, count * HEAD_DIM, RADIUS * rows, RADIUS * cols

    def kernel(dq_ref, b_0, b_1, dk_ref, dv_ref, a_1, a_0, out_q, out_k, out_v, done_q, done_k, done_v, sems):
        copies = []

        def write(done, out):
            copies.append(pltpu.make_async_copy(done, out, sems.at[len(copies)]))
            copies[-1].start()

        middle = slice(lat_edge, own - lat_edge)
        for part, (grad, done, out) in enumerate(((dk_ref, done_k, out_k), (dv_ref, done_v, out_v))):
            done[middle, :] = grad[middle, :].astype(jnp.bfloat16)
            for slot, arrived in enumerate((a_0, a_1)):
                start = pl.multiple_of(slot_side("lat", slot) * (own - lat_edge), 16)
                added = arrived[part * lat_edge : (part + 1) * lat_edge, :].astype(jnp.float32)
                done[pl.ds(start, lat_edge), :] = (grad[pl.ds(start, lat_edge), :] + added).astype(jnp.bfloat16)
            write(done, out)
        position = across(2 * edge)
        place = jnp.where(position < edge, position, position - edge + LANES)
        row, col = own_query_cell(place, rows, cols)
        spread = jnp.where(down(own) == row * cols + col, 1.0, 0.0).astype(jnp.bfloat16)
        for at in range(0, width, BLOCK):
            lanes = slice(at, at + BLOCK)
            arrived = jnp.concatenate([b_0[:, lanes], b_1[:, lanes]], axis=0)
            done_q[:, lanes] = (dq_ref[:, lanes] + dot(spread, arrived, (1, 0))).astype(jnp.bfloat16)
        write(done_q, out_q)
        for copy in copies:
            copy.wait()

    return call(
        kernel, "finish", (query_grad, *back, key_grad, value_grad, *lat_back), [low(own, width)] * 3,
        [pltpu.VMEM((own, width), jnp.bfloat16)] * 3 + [pltpu.SemaphoreType.DMA((3,))],
        outs=[HBM_SPEC] * 3,
    )


def swap(axis, slot, wrap, array):
    count = lax.axis_size(axis)
    pairs = []
    for lower in range(slot, count if wrap else count - 1, 2):
        upper = (lower + 1) % count
        pairs += [(lower, upper), (upper, lower)]
    return lax.ppermute(array, axis, pairs)


def swap_lon(slot, array):
    return swap("lon", 1 - slot, True, array)


def swap_lat(slot, array):
    return swap("lat", slot, False, array)


def after(value, *earlier):
    return lax.optimization_barrier((value, *earlier))[0]


def held(value, *earlier, flops=1 << 33):
    spec = pl.BlockSpec(memory_space=pl.ANY)
    return call(
        lambda *refs: None, "held", (value, *earlier), [jax.ShapeDtypeStruct(value.shape, value.dtype)],
        flops=flops, aliases={0: 0}, ins=[spec] * (1 + len(earlier)), outs=[spec],
    )[0]


def shards(queries, key_field, value_field, out_grad):
    rows, cols, width = queries.shape
    own = rows * cols
    flat = lambda x: x.reshape(own, width)
    queries, key_field, value_field, out_grad = map(flat, (queries, key_field, value_field, out_grad))
    size = (rows, cols, width // HEAD_DIM)

    qp, gp, *sends = pack_queries(queries, out_grad, key_field, value_field, *size)
    sends, (key_field, value_field), edges = sends[:2], sends[2:4], sends[4:]
    halo = [swap_lon(slot, send) for slot, send in enumerate(sends)]
    lat = [swap_lat(place & 1, edge) for place, edge in enumerate(edges)]
    kp, vp, *stats, own_s, own_d = own_scores(qp, gp, key_field, value_field, *size)
    *own_stat, lat_s, lat_d = lat_scores(qp, gp, lat, stats, *size)
    theirs_1 = swap_lon(1, own_stat[1])

    mine_0, *scores_0 = halo_scores(0, halo[0], own_stat[0], kp, vp, lat, *size)
    theirs_0 = swap_lon(0, mine_0)
    result_0, stats_0, *lows_0 = halo_finish(0, mine_0, theirs_0, *scores_0, kp, lat[:2], *size)
    dq_0, *parts = first_grads(
        qp, gp, halo[0], stats_0, (own_s, lat_s), (own_d, lat_d), lows_0, kp, lat[:2], *size
    )
    halo[1] = after(halo[1], parts[0])
    result_1, part_1, *lows_1 = halo_grads(1, halo[1], theirs_1, kp, vp, lat, *size)
    other_1 = swap_lon(1, part_1)
    result_1 = held(result_1, part_1, flops=1 << 29)
    result_0 = held(result_0, result_1, flops=1 << 29)
    back = [swap_lon(0, result_0), swap_lon(1, result_1)]
    other_1 = held(other_1)
    *lat_back, stats_1, lat_low = lat_grads(
        qp, gp, halo[1], own_stat[1], other_1, lat_s, lat_d, lows_1, *parts, *size
    )
    dq, dk, dv = second_grads(
        qp, gp, halo[1], stats_1, lat_low, own_s, own_d, lows_1, kp, lat[:2], (dq_0, *parts), *size
    )
    lat_back = [swap_lat(slot, lat_back[slot]) for slot in (1, 0)]
    outs = finish(dq, back, held(dk), dv, lat_back, *size)
    shape = (rows, cols, width)
    return tuple(x.reshape(shape) for x in outs)


def solution(mesh):
    spec = P("lat", "lon", None)
    return jax.shard_map(
        shards, mesh=mesh, in_specs=(spec,) * 4, out_specs=(spec,) * 3, check_vma=False
    )
```

```python
import math

import jax
import jax.numpy as jnp
from jax import lax
from jax.experimental import pallas as pl
from jax.experimental.pallas import tpu as pltpu
from jax.sharding import PartitionSpec as P

HEAD_DIM = 128
WINDOW = 13
RADIUS = WINDOW // 2
LANES = 128
MASKED = -1e30
LOG2E = math.log2(math.e)
VMEM_BYTES = 16 * 1024 * 1024


def split(index, width):
    if width & (width - 1) == 0:
        whole = index >> (width.bit_length() - 1)
    else:
        whole = (index * ((1 << 12) // width + 1)) >> 12
    return whole, index - whole * width


def odd(axis):
    return lax.axis_index(axis) & 1


def slot_side(axis, slot):
    parity = odd(axis)
    return parity if slot == (0 if axis == "lon" else 1) else 1 - parity


def own_query_cell(position, rows, cols):
    edge = rows * RADIUS
    group = position >> 7
    place = position & (LANES - 1)
    side = jnp.where(group == 0, slot_side("lon", 0), slot_side("lon", 1))
    row_a, col_a = split(place, RADIUS)
    inner = cols - 2 * RADIUS
    row_b, col_b = split(place - edge + (LANES - edge) * group, inner)
    at_edge = place < edge
    row = jnp.where(at_edge, row_a, row_b)
    col = jnp.where(at_edge, side * (cols - RADIUS) + col_a, RADIUS + col_b)
    return row, col


def halo_query_cell(position, rows, cols):
    edge = rows * RADIUS
    group = position >> 7
    place = position & (LANES - 1)
    side = jnp.where(group == 0, slot_side("lon", 0), slot_side("lon", 1))
    row, col = split(place, RADIUS)
    col = jnp.where(side == 1, cols, -RADIUS) + col
    col = jnp.where(place < edge, col, 1 << 12)
    return row, col


def lat_key_cell(slot, position, rows, cols):
    row, col = split(position, cols)
    return row + jnp.where(slot_side("lat", slot) == 1, rows, -RADIUS), col


def bias_of(key_cells, query_cells, rows):
    total_rows = rows * lax.axis_size("lat")
    first = rows * lax.axis_index("lat")
    key_row, key_col = key_cells
    query_row, query_col = query_cells
    start = jnp.clip(first + query_row - RADIUS, 0, total_rows - WINDOW)
    from_start = first + key_row - start
    inside = (from_start >= 0) & (from_start < WINDOW)
    inside = inside & (jnp.abs(key_col - query_col) <= RADIUS)
    return jnp.where(inside, 0.0, MASKED)


def down(count):
    return lax.broadcasted_iota(jnp.int32, (count, 1), 0)


def across(count, start=0):
    return lax.broadcasted_iota(jnp.int32, (1, count), 1) + start


def dot(a, b, contract):
    return lax.dot_general(a, b, ((contract[:1], contract[1:]), ((), ())), preferred_element_type=jnp.float32)


def call(kernel, name, operands, out_shapes, scratch=(), flops=0, aliases=None, outs=None, ins=None):
    return pl.pallas_call(
        kernel,
        name=name,
        in_specs=ins or [VMEM_SPEC] * len(operands),
        out_specs=outs or [VMEM_SPEC] * len(out_shapes),
        out_shape=out_shapes,
        scratch_shapes=scratch,
        input_output_aliases=aliases or {},
        compiler_params=pltpu.CompilerParams(vmem_limit_bytes=VMEM_BYTES),
        cost_estimate=pl.CostEstimate(flops=flops, bytes_accessed=0, transcendentals=0),
    )(*operands)


def low(*shape):
    return jax.ShapeDtypeStruct(shape, jnp.bfloat16)


def full(*shape):
    return jax.ShapeDtypeStruct(shape, jnp.float32)


def lanes_of(head, count=1):
    return slice(head * HEAD_DIM, (head + count) * HEAD_DIM)


def selection(row, col, rows, cols):
    source = across(rows * cols)
    return jnp.where(source == row * cols + col, 1.0, 0.0).astype(jnp.bfloat16)


HBM_SPEC, VMEM_SPEC = pl.BlockSpec(memory_space=pltpu.HBM), pl.BlockSpec(memory_space=pltpu.VMEM)
BLOCK = 2 * HEAD_DIM


def pack_queries(queries, out_grad, key_field, value_field, rows, cols, count):
    own, edge, width = rows * cols, rows * RADIUS, count * HEAD_DIM
    lat_edge = RADIUS * cols

    def kernel(
        q_hbm, g_hbm, k_hbm, v_hbm, qp_ref, gp_ref, send_0, send_1, k_ref, v_ref, k_0, k_1, v_0, v_1, q_ref, g_ref, sems
    ):
        copies = [
            pltpu.make_async_copy(src, dst, sems.at[i])
            for i, (src, dst) in enumerate(
                ((q_hbm, q_ref), (g_hbm, g_ref), (k_hbm, k_ref), (v_hbm, v_ref))
            )
        ]
        for copy in copies:
            copy.start()
        order = selection(*own_query_cell(down(own), rows, cols), rows, cols)
        for place, (src, dst) in enumerate(((q_ref, qp_ref), (g_ref, gp_ref))):
            copies[place].wait()
            for at in range(0, width, BLOCK):
                here = slice(at, at + BLOCK)
                moved = dot(order, src[:, here], (1, 0)).astype(jnp.bfloat16)
                dst[:, here] = moved
                for group, send in enumerate((send_0, send_1)):
                    send[place * edge : (place + 1) * edge, here] = moved[group * LANES : group * LANES + edge]
        for copy, src, sends in zip(copies[2:], (k_ref, v_ref), ((k_0, k_1), (v_0, v_1))):
            copy.wait()
            for slot, send in enumerate(sends):
                start = pl.multiple_of(slot_side("lat", slot) * (own - lat_edge), 16)
                send[...] = src[pl.ds(start, lat_edge), :]

    operands = [
        pltpu.with_memory_space_constraint(x, pltpu.HBM) for x in (queries, out_grad, key_field, value_field)
    ]
    return call(
        kernel, "pack_queries", operands,
        [low(own, width)] * 2 + [low(2 * edge, width)] * 2 + [low(own, width)] * 2 + [low(lat_edge, width)] * 4,
        [pltpu.VMEM((own, width), jnp.bfloat16)] * 2 + [pltpu.SemaphoreType.DMA((4,))],
        ins=[HBM_SPEC] * 4,
    )


def own_scores(qp, gp, key_field, value_field, rows, cols, count):
    own, width = rows * cols, key_field.shape[1]

    def kernel(q_ref, g_ref, k_ref, v_ref, kp_ref, vp_ref, out_0, out_1, s_ref, d_ref, bias):
        order = selection(*own_query_cell(down(own), rows, cols), rows, cols)
        for src, dst in ((k_ref, kp_ref), (v_ref, vp_ref)):
            for at in range(0, width, BLOCK):
                here = slice(at, at + BLOCK)
                dst[:, here] = dot(order, src[:, here], (1, 0)).astype(jnp.bfloat16)
        bias[...] = bias_of(
            own_query_cell(down(own), rows, cols), own_query_cell(across(own), rows, cols), rows
        )
        for out in (out_0, out_1):
            out[...] = jnp.zeros_like(out)
        for head in range(count):
            lanes = lanes_of(head)
            s_ref[head] = dot(kp_ref[:, lanes], q_ref[:, lanes], (1, 1)) * (SCORE_SCALE * LOG2E) + bias[...]
            d_ref[head] = dot(vp_ref[:, lanes], g_ref[:, lanes], (1, 1))
            put_stats((out_0, out_1), head, part_stats(s_ref[head], d_ref[head]), count)

    return call(
        kernel, "own_scores", (qp, gp, key_field, value_field),
        [low(own, width)] * 2 + [full(stat_rows(count), LANES)] * 2 + [full(count, own, own)] * 2,
        [pltpu.VMEM((own, own), jnp.float32)],
    )


def put_stats(outs, head, stats, count):
    for out, half in zip(outs, (LOW, HIGH)):
        for at, stat in zip((head, count + head), stats):
            out[at : at + 1, :] = stat[:, half]


def halo_head(ref, edge, part, head):
    rows = ref[part * edge : (part + 1) * edge, lanes_of(head)]
    return jnp.concatenate([rows, jnp.zeros((LANES - edge, HEAD_DIM), jnp.bfloat16)], axis=0)


def near_keys(group, own_ref, lat_refs, head):
    lanes, edge = lanes_of(head), lat_refs[0].shape[0]
    pieces = [own_ref[group * LANES : group * LANES + edge, lanes]]
    return jnp.concatenate(pieces + [ref[:, lanes] for ref in lat_refs], axis=0)


def every_key(own_ref, lat_refs, head):
    lanes = lanes_of(head)
    return jnp.concatenate([ref[:, lanes] for ref in (own_ref, *lat_refs)], axis=0)


def fill_bias(bias, own_position, queries, rows, cols):
    at, edge = own_position.shape[0], RADIUS * cols
    bias[:at, :] = bias_of(own_query_cell(own_position, rows, cols), queries, rows)
    for slot in (0, 1):
        here = slice(at + slot * edge, at + (slot + 1) * edge)
        bias[here, :] = bias_of(lat_key_cell(slot, down(edge), rows, cols), queries, rows)


LOW, HIGH = slice(0, LANES), slice(LANES, 2 * LANES)
SCORE_SCALE = 1.0 / math.sqrt(HEAD_DIM)


def part_stats(scores, weight_grad):
    peak = jnp.max(scores, axis=0, keepdims=True)
    weights = jnp.exp2(scores - peak)
    total = jnp.sum(weights, axis=0, keepdims=True)
    dotted = jnp.sum(weights * weight_grad, axis=0, keepdims=True)
    return peak + jnp.log(total) * LOG2E, dotted / total


def stat_rows(count):
    return -(-2 * count // 8) * 8


def lat_scores(qp, gp, lat, stats, rows, cols, count):
    own, lat_edge = rows * cols, RADIUS * cols

    def kernel(q_ref, g_ref, k_0, k_1, v_0, v_1, before_0, before_1, out_0, out_1, s_ref, d_ref, bias, part_0, part_1):
        queries = own_query_cell(across(own), rows, cols)
        for slot in (0, 1):
            cells = lat_key_cell(slot, down(lat_edge), rows, cols)
            bias[slot * lat_edge : (slot + 1) * lat_edge, :] = bias_of(cells, queries, rows)
        for head in range(count):
            lanes = lanes_of(head)
            key, value = (
                jnp.concatenate([ref[:, lanes] for ref in pair], axis=0) for pair in ((k_0, k_1), (v_0, v_1))
            )
            s_ref[head] = dot(key, q_ref[:, lanes], (1, 1)) * (SCORE_SCALE * LOG2E) + bias[...]
            d_ref[head] = dot(value, g_ref[:, lanes], (1, 1))
            put_stats((part_0, part_1), head, part_stats(s_ref[head], d_ref[head]), count)
        for out, part, before in ((out_0, part_0, before_0), (out_1, part_1, before_1)):
            out[...] = jnp.zeros_like(out)
            out[:count, :], out[count : 2 * count, :] = stats_of(part, before, count)

    return call(
        kernel, "lat_scores", (qp, gp, *lat, *stats),
        [full(stat_rows(count), LANES)] * 2 + [full(count, 2 * lat_edge, own)] * 2,
        [pltpu.VMEM((2 * lat_edge, own), jnp.float32)] + [pltpu.VMEM((stat_rows(count), LANES), jnp.float32)] * 2,
    )


def combined(mine, theirs):
    (a, delta_a), (b, delta_b) = mine, theirs
    peak = jnp.maximum(a, b)
    part_a, part_b = jnp.exp2(a - peak), jnp.exp2(b - peak)
    total = part_a + part_b
    return peak + jnp.log(total) * LOG2E, (part_a * delta_a + part_b * delta_b) / total


def halo_grads(group, halo, theirs, kp, vp, lat, rows, cols, count, pad=0):
    edge = RADIUS * rows
    near = edge + 2 * RADIUS * cols

    def kernel(halo_ref, stat, k_ref, v_ref, k_0, k_1, v_0, v_1, out, mine, p_ref, g_ref, bias, s_ref, d_ref):
        queries = halo_query_cell(across(LANES, group * LANES), rows, cols)
        fill_bias(bias, down(edge) + group * LANES, queries, rows, cols)
        mine[...] = jnp.zeros_like(mine)
        for head in range(count):
            key = near_keys(group, k_ref, (k_0, k_1), head)
            value = near_keys(group, v_ref, (v_0, v_1), head)
            s_ref[head] = dot(key, halo_head(halo_ref, edge, 0, head), (1, 1)) * (SCORE_SCALE * LOG2E) + bias[...]
            d_ref[head] = dot(value, halo_head(halo_ref, edge, 1, head), (1, 1))
            log_total, delta = part_stats(s_ref[head], d_ref[head])
            mine[head : head + 1, :] = log_total
            mine[count + head : count + head + 1, :] = delta
        log_total, delta = combined(*((x[:count, :], x[count : 2 * count, :]) for x in (mine, stat)))
        for head in range(count):
            row = slice(head, head + 1)
            p_ref[head], grad = gradients(s_ref[head], d_ref[head], log_total[row], delta[row])
            g_ref[head] = grad
            query_grad = dot(grad, near_keys(group, k_ref, (k_0, k_1), head), (0, 0)) * SCORE_SCALE
            out[:, lanes_of(head)] = query_grad[:edge].astype(jnp.bfloat16)

    return call(
        kernel, f"halo_grads_{group}", (halo, theirs, kp, vp, *lat),
        [pltpu.VMEM((edge, count * HEAD_DIM), jnp.bfloat16), full(stat_rows(count) + pad, LANES)]
        + [low(count, near, LANES)] * 2,
        [pltpu.VMEM((near, LANES), jnp.float32)] + [pltpu.VMEM((count, near, LANES), jnp.float32)] * 2,
    )


def halo_scores(group, halo, own_stat, kp, vp, lat, rows, cols, count):
    edge = RADIUS * rows
    near = edge + 2 * RADIUS * cols

    def kernel(halo_ref, stat, k_ref, v_ref, k_0, k_1, v_0, v_1, out, s_ref, d_ref, bias):
        queries = halo_query_cell(across(LANES, group * LANES), rows, cols)
        fill_bias(bias, down(edge) + group * LANES, queries, rows, cols)
        out[:, LOW] = stat[...]
        out[:, HIGH] = jnp.zeros((out.shape[0], LANES), jnp.float32)
        for head in range(count):
            key = near_keys(group, k_ref, (k_0, k_1), head)
            value = near_keys(group, v_ref, (v_0, v_1), head)
            s_ref[head] = dot(key, halo_head(halo_ref, edge, 0, head), (1, 1)) * (SCORE_SCALE * LOG2E) + bias[...]
            d_ref[head] = dot(value, halo_head(halo_ref, edge, 1, head), (1, 1))
            log_total, delta = part_stats(s_ref[head], d_ref[head])
            out[head : head + 1, HIGH] = log_total
            out[count + head : count + head + 1, HIGH] = delta

    return call(
        kernel, f"halo_scores_{group}", (halo, own_stat, kp, vp, *lat),
        [full(stat_rows(count), 2 * LANES)] + [full(count, near, LANES)] * 2,
        [pltpu.VMEM((near, LANES), jnp.float32)],
    )


def halo_finish(group, mine, theirs, scores, weight_grad, kp, lat, rows, cols, count):
    edge = RADIUS * rows

    def kernel(m, t, s_ref, d_ref, k_ref, k_0, k_1, out, final, p_ref, g_ref):
        final[...] = jnp.zeros_like(final)
        logs, deltas = combined(*((x[:count, half], x[count : 2 * count, half]) for x, half in ((m, LOW), (t, HIGH))))
        final[:count, :] = logs
        final[count : 2 * count, :] = deltas
        logs, deltas = combined(*((x[:count, half], x[count : 2 * count, half]) for x, half in ((m, HIGH), (t, LOW))))
        for head in range(count):
            row = slice(head, head + 1)
            p_ref[head], grad = gradients(s_ref[head], d_ref[head], logs[row], deltas[row])
            g_ref[head] = grad
            query_grad = dot(grad, near_keys(group, k_ref, (k_0, k_1), head), (0, 0)) * SCORE_SCALE
            out[:, lanes_of(head)] = query_grad[:edge].astype(jnp.bfloat16)

    return call(
        kernel, f"halo_finish_{group}", (mine, theirs, scores, weight_grad, kp, *lat),
        [low(edge, count * HEAD_DIM), full(stat_rows(count), LANES)] + [low(count, *scores.shape[1:])] * 2,
    )


def gradients(scores, weight_grad, log_total, delta):
    weights = jnp.exp2(scores - log_total)
    return weights.astype(jnp.bfloat16), (weights * (weight_grad - delta)).astype(jnp.bfloat16)


def stats_of(mine, theirs, count):
    return combined(*((x[:count, :], x[count : 2 * count, :]) for x in (mine, theirs)))


def lat_grads(qp, gp, halo, stats_0, mine, theirs, scores, weight_grad, lows, rows, cols, count):
    own, width, edge, lat_edge = rows * cols, count * HEAD_DIM, RADIUS * rows, RADIUS * cols

    def kernel(
        q_ref, g_ref, h_0, h_1, stat, m, t, s_ref, d_ref, p_0, l_0, p_1, l_1, out_0, out_1, final, lat_low
    ):
        final[...] = jnp.zeros_like(final)
        final[:count, :], final[count : 2 * count, :] = stats_of(m, t, count)
        for head in range(count):
            lanes = lanes_of(head)
            logs, deltas = (
                jnp.concatenate([ref[at : at + 1, :] for ref in (stat, final)], axis=1) for at in (head, count + head)
            )
            weights, grad = gradients(s_ref[head], d_ref[head], logs, deltas)
            lat_low[head] = grad
            sides = ((grad, (l_0, l_1), q_ref, SCORE_SCALE), (weights, (p_0, p_1), g_ref, 1.0))
            for part, (low_lat, low_halo, own_ref, scale) in enumerate(sides):
                every = [own_ref[:, lanes]] + [halo_head(h, edge, part, head) for h in (h_0, h_1)]
                met = jnp.concatenate([low_lat] + [x[head, edge:, :] for x in low_halo], axis=1)
                outside = (dot(met, jnp.concatenate(every, axis=0), (1, 0)) * scale).astype(jnp.bfloat16)
                for slot, out in enumerate((out_0, out_1)):
                    out[part * lat_edge : (part + 1) * lat_edge, lanes] = outside[
                        slot * lat_edge : (slot + 1) * lat_edge
                    ]

    return call(
        kernel, "lat_grads", (qp, gp, *halo, stats_0, mine, theirs, scores, weight_grad, *lows[0], *lows[1]),
        [low(2 * lat_edge, width)] * 2 + [full(stat_rows(count), LANES), low(count, 2 * lat_edge, own)],
    )


def own_grads(qp, gp, halo, stats, lat_low, scores, weight_grad, lows, kp, lat, rows, cols, count):
    own, width, edge = rows * cols, count * HEAD_DIM, RADIUS * rows

    def kernel(
        q_ref, g_ref, h_0, h_1, stat_0, stat_1, lat_ref, s_ref, d_ref, p_0, l_0, p_1, l_1, k_ref, k_0, k_1,
        dq_ref, dk_ref, dv_ref, sums,
    ):
        for head in range(count):
            lanes = lanes_of(head)
            logs, deltas = (
                jnp.concatenate([ref[at : at + 1, :] for ref in (stat_0, stat_1)], axis=1)
                for at in (head, count + head)
            )
            own_p, own_l = gradients(s_ref[head], d_ref[head], logs, deltas)
            every = jnp.concatenate([own_l, lat_ref[head]], axis=0)
            sums[0, :, lanes] = dot(every, every_key(k_ref, (k_0, k_1), head), (0, 0)) * SCORE_SCALE
            sides = ((own_l, (l_0, l_1), q_ref, SCORE_SCALE), (own_p, (p_0, p_1), g_ref, 1.0))
            for part, (low_own, low_halo, own_ref, scale) in enumerate(sides):
                inside = dot(low_own, own_ref[:, lanes], (1, 0))
                for group, (x, h) in enumerate(zip(low_halo, (h_0, h_1))):
                    at = group * LANES
                    near = inside[at : at + edge] + dot(x[head, :edge, :], halo_head(h, edge, part, head), (1, 0))
                    sums[1 + part, at : at + edge, lanes] = near * scale
                    sums[1 + part, at + edge : at + LANES, lanes] = inside[at + edge : at + LANES] * scale
        order = restore(rows, cols)
        twice = jnp.concatenate([order, order], axis=1)
        for place, result in enumerate((dq_ref, dk_ref, dv_ref)):
            for at in range(0, width, BLOCK):
                value = sums[place, :, at : at + BLOCK]
                high = value.astype(jnp.bfloat16)
                rest = (value - high.astype(jnp.float32)).astype(jnp.bfloat16)
                result[:, at : at + BLOCK] = dot(twice, jnp.concatenate([high, rest], axis=0), (1, 0))

    return call(
        kernel, "own_grads",
        (qp, gp, *halo, *stats, lat_low, scores, weight_grad, *lows[0], *lows[1], kp, *lat),
        [full(own, width)] * 3, [pltpu.VMEM((3, own, width), jnp.float32)],
    )


def restore(rows, cols):
    own = rows * cols
    row, col = own_query_cell(across(own), rows, cols)
    return jnp.where(down(own) == row * cols + col, 1.0, 0.0).astype(jnp.bfloat16)


def finish(query_grad, back, key_grad, value_grad, lat_back, rows, cols, count):
    own, width, edge, lat_edge = rows * cols, count * HEAD_DIM, RADIUS * rows, RADIUS * cols

    def kernel(dq_ref, b_0, b_1, dk_ref, dv_ref, a_1, a_0, out_q, out_k, out_v, done_q, done_k, done_v, sems):
        copies = []

        def write(done, out):
            copies.append(pltpu.make_async_copy(done, out, sems.at[len(copies)]))
            copies[-1].start()

        middle = slice(lat_edge, own - lat_edge)
        for part, (grad, done, out) in enumerate(((dk_ref, done_k, out_k), (dv_ref, done_v, out_v))):
            done[middle, :] = grad[middle, :].astype(jnp.bfloat16)
            for slot, arrived in enumerate((a_0, a_1)):
                start = pl.multiple_of(slot_side("lat", slot) * (own - lat_edge), 16)
                added = arrived[part * lat_edge : (part + 1) * lat_edge, :].astype(jnp.float32)
                done[pl.ds(start, lat_edge), :] = (grad[pl.ds(start, lat_edge), :] + added).astype(jnp.bfloat16)
            write(done, out)
        position = across(2 * edge)
        place = jnp.where(position < edge, position, position - edge + LANES)
        row, col = own_query_cell(place, rows, cols)
        spread = jnp.where(down(own) == row * cols + col, 1.0, 0.0).astype(jnp.bfloat16)
        for at in range(0, width, BLOCK):
            lanes = slice(at, at + BLOCK)
            arrived = jnp.concatenate([b_0[:, lanes], b_1[:, lanes]], axis=0)
            done_q[:, lanes] = (dq_ref[:, lanes] + dot(spread, arrived, (1, 0))).astype(jnp.bfloat16)
        write(done_q, out_q)
        for copy in copies:
            copy.wait()

    return call(
        kernel, "finish", (query_grad, *back, key_grad, value_grad, *lat_back), [low(own, width)] * 3,
        [pltpu.VMEM((own, width), jnp.bfloat16)] * 3 + [pltpu.SemaphoreType.DMA((3,))],
        outs=[HBM_SPEC] * 3,
    )


def swap(axis, slot, wrap, array):
    count = lax.axis_size(axis)
    pairs = []
    for lower in range(slot, count if wrap else count - 1, 2):
        upper = (lower + 1) % count
        pairs += [(lower, upper), (upper, lower)]
    return lax.ppermute(array, axis, pairs)


def swap_lon(slot, array):
    return swap("lon", 1 - slot, True, array)


def swap_lat(slot, array):
    return swap("lat", slot, False, array)


def after(value, *earlier):
    return lax.optimization_barrier((value, *earlier))[0]


def held(value, *earlier, flops=1 << 33):
    spec = pl.BlockSpec(memory_space=pl.ANY)
    return call(
        lambda *refs: None, "held", (value, *earlier), [jax.ShapeDtypeStruct(value.shape, value.dtype)],
        flops=flops, aliases={0: 0}, ins=[spec] * (1 + len(earlier)), outs=[spec],
    )[0]


def shards(queries, key_field, value_field, out_grad):
    rows, cols, width = queries.shape
    own = rows * cols
    flat = lambda x: x.reshape(own, width)
    queries, key_field, value_field, out_grad = map(flat, (queries, key_field, value_field, out_grad))
    size = (rows, cols, width // HEAD_DIM)

    qp, gp, *sends = pack_queries(queries, out_grad, key_field, value_field, *size)
    sends, (key_field, value_field), edges = sends[:2], sends[2:4], sends[4:]
    halo = [swap_lon(slot, send) for slot, send in enumerate(sends)]
    lat = [swap_lat(place & 1, edge) for place, edge in enumerate(edges)]
    kp, vp, *stats, own_s, own_d = own_scores(qp, gp, key_field, value_field, *size)
    *own_stat, lat_s, lat_d = lat_scores(qp, gp, lat, stats, *size)
    theirs_1 = swap_lon(1, own_stat[1])

    mine_0, *scores_0 = halo_scores(0, halo[0], own_stat[0], kp, vp, lat, *size)
    theirs_0 = swap_lon(0, mine_0)
    result_0, stats_0, *lows_0 = halo_finish(0, mine_0, theirs_0, *scores_0, kp, lat[:2], *size)
    halo[1] = after(halo[1], result_0)
    result_1, part_1, *lows_1 = halo_grads(1, halo[1], theirs_1, kp, vp, lat, *size)
    other_1 = held(swap_lon(1, part_1))
    result_1 = held(result_1, part_1, flops=1 << 29)
    result_0 = held(result_0, result_1, flops=1 << 29)
    back = [swap_lon(0, result_0), swap_lon(1, result_1)]
    *lat_back, stats_1, lat_low = lat_grads(
        qp, gp, halo, stats_0, own_stat[1], other_1, lat_s, lat_d, (lows_0, lows_1), *size
    )
    dq, dk, dv = own_grads(
        qp, gp, halo, (stats_0, stats_1), lat_low, own_s, own_d, (lows_0, lows_1), kp, lat[:2], *size
    )
    lat_back = [swap_lat(slot, lat_back[slot]) for slot in (1, 0)]
    outs = finish(dq, back, held(dk), dv, lat_back, *size)
    shape = (rows, cols, width)
    return tuple(x.reshape(shape) for x in outs)


def solution(mesh):
    spec = P("lat", "lon", None)
    return jax.shard_map(
        shards, mesh=mesh, in_specs=(spec,) * 4, out_specs=(spec,) * 3, check_vma=False
    )
```

```python
import math

import jax
import jax.numpy as jnp
from jax import lax
from jax.experimental import pallas as pl
from jax.experimental.pallas import tpu as pltpu
from jax.sharding import PartitionSpec as P

HEAD_DIM = 128
WINDOW = 13
RADIUS = WINDOW // 2
LANES = 128
MASKED = -1e30
LOG2E = math.log2(math.e)
VMEM_BYTES = 16 * 1024 * 1024


def split(index, width):
    if width & (width - 1) == 0:
        whole = index >> (width.bit_length() - 1)
    else:
        whole = (index * ((1 << 12) // width + 1)) >> 12
    return whole, index - whole * width


def odd(axis):
    return lax.axis_index(axis) & 1


def slot_side(axis, slot):
    parity = odd(axis)
    return parity if slot == (0 if axis == "lon" else 1) else 1 - parity


def own_query_cell(position, rows, cols):
    edge = rows * RADIUS
    group = position >> 7
    place = position & (LANES - 1)
    side = jnp.where(group == 0, slot_side("lon", 0), slot_side("lon", 1))
    row_a, col_a = split(place, RADIUS)
    inner = cols - 2 * RADIUS
    row_b, col_b = split(place - edge + (LANES - edge) * group, inner)
    at_edge = place < edge
    row = jnp.where(at_edge, row_a, row_b)
    col = jnp.where(at_edge, side * (cols - RADIUS) + col_a, RADIUS + col_b)
    return row, col


def halo_query_cell(position, rows, cols):
    edge = rows * RADIUS
    group = position >> 7
    place = position & (LANES - 1)
    side = jnp.where(group == 0, slot_side("lon", 0), slot_side("lon", 1))
    row, col = split(place, RADIUS)
    col = jnp.where(side == 1, cols, -RADIUS) + col
    col = jnp.where(place < edge, col, 1 << 12)
    return row, col


def lat_key_cell(slot, position, rows, cols):
    row, col = split(position, cols)
    return row + jnp.where(slot_side("lat", slot) == 1, rows, -RADIUS), col


def bias_of(key_cells, query_cells, rows):
    total_rows = rows * lax.axis_size("lat")
    first = rows * lax.axis_index("lat")
    key_row, key_col = key_cells
    query_row, query_col = query_cells
    start = jnp.clip(first + query_row - RADIUS, 0, total_rows - WINDOW)
    from_start = first + key_row - start
    inside = (from_start >= 0) & (from_start < WINDOW)
    inside = inside & (jnp.abs(key_col - query_col) <= RADIUS)
    return jnp.where(inside, 0.0, MASKED)


def down(count):
    return lax.broadcasted_iota(jnp.int32, (count, 1), 0)


def across(count, start=0):
    return lax.broadcasted_iota(jnp.int32, (1, count), 1) + start


def dot(a, b, contract):
    return lax.dot_general(a, b, ((contract[:1], contract[1:]), ((), ())), preferred_element_type=jnp.float32)


def call(kernel, name, operands, out_shapes, scratch=(), flops=0, aliases=None, outs=None, ins=None):
    return pl.pallas_call(
        kernel,
        name=name,
        in_specs=ins or [VMEM_SPEC] * len(operands),
        out_specs=outs or [VMEM_SPEC] * len(out_shapes),
        out_shape=out_shapes,
        scratch_shapes=scratch,
        input_output_aliases=aliases or {},
        compiler_params=pltpu.CompilerParams(vmem_limit_bytes=VMEM_BYTES),
        cost_estimate=pl.CostEstimate(flops=flops, bytes_accessed=0, transcendentals=0),
    )(*operands)


def low(*shape):
    return jax.ShapeDtypeStruct(shape, jnp.bfloat16)


def full(*shape):
    return jax.ShapeDtypeStruct(shape, jnp.float32)


def lanes_of(head, count=1):
    return slice(head * HEAD_DIM, (head + count) * HEAD_DIM)


def selection(row, col, rows, cols):
    source = across(rows * cols)
    return jnp.where(source == row * cols + col, 1.0, 0.0).astype(jnp.bfloat16)


HBM_SPEC, VMEM_SPEC = pl.BlockSpec(memory_space=pltpu.HBM), pl.BlockSpec(memory_space=pltpu.VMEM)
BLOCK = 2 * HEAD_DIM


def pack_queries(queries, out_grad, key_field, value_field, rows, cols, count):
    own, edge, width = rows * cols, rows * RADIUS, count * HEAD_DIM
    lat_edge = RADIUS * cols

    def kernel(
        q_hbm, g_hbm, k_hbm, v_hbm, qp_ref, gp_ref, send_0, send_1, k_ref, v_ref, k_0, k_1, v_0, v_1, q_ref, g_ref, sems
    ):
        copies = [
            pltpu.make_async_copy(src, dst, sems.at[i])
            for i, (src, dst) in enumerate(
                ((q_hbm, q_ref), (g_hbm, g_ref), (k_hbm, k_ref), (v_hbm, v_ref))
            )
        ]
        for copy in copies:
            copy.start()
        order = selection(*own_query_cell(down(own), rows, cols), rows, cols)
        for place, (src, dst) in enumerate(((q_ref, qp_ref), (g_ref, gp_ref))):
            copies[place].wait()
            for at in range(0, width, BLOCK):
                here = slice(at, at + BLOCK)
                moved = dot(order, src[:, here], (1, 0)).astype(jnp.bfloat16)
                dst[:, here] = moved
                for group, send in enumerate((send_0, send_1)):
                    send[place * edge : (place + 1) * edge, here] = moved[group * LANES : group * LANES + edge]
        for copy, src, sends in zip(copies[2:], (k_ref, v_ref), ((k_0, k_1), (v_0, v_1))):
            copy.wait()
            for slot, send in enumerate(sends):
                start = pl.multiple_of(slot_side("lat", slot) * (own - lat_edge), 16)
                send[...] = src[pl.ds(start, lat_edge), :]

    operands = [
        pltpu.with_memory_space_constraint(x, pltpu.HBM) for x in (queries, out_grad, key_field, value_field)
    ]
    return call(
        kernel, "pack_queries", operands,
        [low(own, width)] * 2 + [low(2 * edge, width), low(2 * edge + 16, width)] + [low(own, width)] * 2 + [low(lat_edge, width)] * 4,
        [pltpu.VMEM((own, width), jnp.bfloat16)] * 2 + [pltpu.SemaphoreType.DMA((4,))],
        ins=[HBM_SPEC] * 4,
    )


def own_scores(qp, gp, key_field, value_field, rows, cols, count):
    own, width = rows * cols, key_field.shape[1]

    def kernel(q_ref, g_ref, k_ref, v_ref, kp_ref, vp_ref, out_0, out_1, s_ref, d_ref, bias):
        order = selection(*own_query_cell(down(own), rows, cols), rows, cols)
        for src, dst in ((k_ref, kp_ref), (v_ref, vp_ref)):
            for at in range(0, width, BLOCK):
                here = slice(at, at + BLOCK)
                dst[:, here] = dot(order, src[:, here], (1, 0)).astype(jnp.bfloat16)
        bias[...] = bias_of(
            own_query_cell(down(own), rows, cols), own_query_cell(across(own), rows, cols), rows
        )
        for out in (out_0, out_1):
            out[...] = jnp.zeros_like(out)
        for head in range(count):
            lanes = lanes_of(head)
            s_ref[head] = dot(kp_ref[:, lanes], q_ref[:, lanes], (1, 1)) * (SCORE_SCALE * LOG2E) + bias[...]
            d_ref[head] = dot(vp_ref[:, lanes], g_ref[:, lanes], (1, 1))
            put_stats((out_0, out_1), head, part_stats(s_ref[head], d_ref[head]), count)

    return call(
        kernel, "own_scores", (qp, gp, key_field, value_field),
        [low(own, width)] * 2 + [full(stat_rows(count), LANES)] * 2 + [full(count, own, own)] * 2,
        [pltpu.VMEM((own, own), jnp.float32)],
    )


def put_stats(outs, head, stats, count):
    for out, half in zip(outs, (LOW, HIGH)):
        for at, stat in zip((head, count + head), stats):
            out[at : at + 1, :] = stat[:, half]


def halo_head(ref, edge, part, head):
    rows = ref[part * edge : (part + 1) * edge, lanes_of(head)]
    return jnp.concatenate([rows, jnp.zeros((LANES - edge, HEAD_DIM), jnp.bfloat16)], axis=0)


def near_keys(group, own_ref, lat_refs, head):
    lanes, edge = lanes_of(head), lat_refs[0].shape[0]
    pieces = [own_ref[group * LANES : group * LANES + edge, lanes]]
    return jnp.concatenate(pieces + [ref[:, lanes] for ref in lat_refs], axis=0)


def every_key(own_ref, lat_refs, head):
    lanes = lanes_of(head)
    return jnp.concatenate([ref[:, lanes] for ref in (own_ref, *lat_refs)], axis=0)


def fill_bias(bias, own_position, queries, rows, cols):
    at, edge = own_position.shape[0], RADIUS * cols
    bias[:at, :] = bias_of(own_query_cell(own_position, rows, cols), queries, rows)
    for slot in (0, 1):
        here = slice(at + slot * edge, at + (slot + 1) * edge)
        bias[here, :] = bias_of(lat_key_cell(slot, down(edge), rows, cols), queries, rows)


LOW, HIGH = slice(0, LANES), slice(LANES, 2 * LANES)
SCORE_SCALE = 1.0 / math.sqrt(HEAD_DIM)


def part_stats(scores, weight_grad):
    peak = jnp.max(scores, axis=0, keepdims=True)
    weights = jnp.exp2(scores - peak)
    total = jnp.sum(weights, axis=0, keepdims=True)
    dotted = jnp.sum(weights * weight_grad, axis=0, keepdims=True)
    return peak + jnp.log(total) * LOG2E, dotted / total


def stat_rows(count):
    return -(-2 * count // 8) * 8


def lat_scores(qp, gp, lat, stats, rows, cols, count):
    own, lat_edge = rows * cols, RADIUS * cols

    def kernel(q_ref, g_ref, k_0, k_1, v_0, v_1, before_0, before_1, out_0, out_1, s_ref, d_ref, bias, part_0, part_1):
        queries = own_query_cell(across(own), rows, cols)
        for slot in (0, 1):
            cells = lat_key_cell(slot, down(lat_edge), rows, cols)
            bias[slot * lat_edge : (slot + 1) * lat_edge, :] = bias_of(cells, queries, rows)
        for head in range(count):
            lanes = lanes_of(head)
            key, value = (
                jnp.concatenate([ref[:, lanes] for ref in pair], axis=0) for pair in ((k_0, k_1), (v_0, v_1))
            )
            s_ref[head] = dot(key, q_ref[:, lanes], (1, 1)) * (SCORE_SCALE * LOG2E) + bias[...]
            d_ref[head] = dot(value, g_ref[:, lanes], (1, 1))
            put_stats((part_0, part_1), head, part_stats(s_ref[head], d_ref[head]), count)
        for out, part, before in ((out_0, part_0, before_0), (out_1, part_1, before_1)):
            out[...] = jnp.zeros_like(out)
            out[:count, :], out[count : 2 * count, :] = stats_of(part, before, count)

    return call(
        kernel, "lat_scores", (qp, gp, *lat, *stats),
        [full(stat_rows(count), LANES)] * 2 + [full(count, 2 * lat_edge, own)] * 2,
        [pltpu.VMEM((2 * lat_edge, own), jnp.float32)] + [pltpu.VMEM((stat_rows(count), LANES), jnp.float32)] * 2,
    )


def combined(mine, theirs):
    (a, delta_a), (b, delta_b) = mine, theirs
    peak = jnp.maximum(a, b)
    part_a, part_b = jnp.exp2(a - peak), jnp.exp2(b - peak)
    total = part_a + part_b
    return peak + jnp.log(total) * LOG2E, (part_a * delta_a + part_b * delta_b) / total


def halo_part(group, halo, kp, vp, lat, rows, cols, count):
    edge = RADIUS * rows
    near = edge + 2 * RADIUS * cols

    def kernel(halo_ref, k_ref, v_ref, k_0, k_1, v_0, v_1, out, s_ref, d_ref, bias):
        queries = halo_query_cell(across(LANES, group * LANES), rows, cols)
        fill_bias(bias, down(edge) + group * LANES, queries, rows, cols)
        out[...] = jnp.zeros_like(out)
        for head in range(count):
            key = near_keys(group, k_ref, (k_0, k_1), head)
            value = near_keys(group, v_ref, (v_0, v_1), head)
            s_ref[head] = dot(key, halo_head(halo_ref, edge, 0, head), (1, 1)) * (SCORE_SCALE * LOG2E) + bias[...]
            d_ref[head] = dot(value, halo_head(halo_ref, edge, 1, head), (1, 1))
            log_total, delta = part_stats(s_ref[head], d_ref[head])
            out[head : head + 1, :] = log_total
            out[count + head : count + head + 1, :] = delta

    return call(
        kernel, f"halo_part_{group}", (halo, kp, vp, *lat),
        [full(stat_rows(count), LANES)] + [full(count, near, LANES)] * 2,
        [pltpu.VMEM((near, LANES), jnp.float32)],
    )


def halo_rest(group, mine, theirs, scores, weight_grad, kp, lat, rows, cols, count):
    edge = RADIUS * rows

    def kernel(m, t, s_ref, d_ref, k_ref, k_0, k_1, out, p_ref, g_ref):
        logs, deltas = stats_of(m, t, count)
        for head in range(count):
            row = slice(head, head + 1)
            p_ref[head], grad = gradients(s_ref[head], d_ref[head], logs[row], deltas[row])
            g_ref[head] = grad
            query_grad = dot(grad, near_keys(group, k_ref, (k_0, k_1), head), (0, 0)) * SCORE_SCALE
            out[:, lanes_of(head)] = query_grad[:edge].astype(jnp.bfloat16)

    return call(
        kernel, f"halo_rest_{group}", (mine, theirs, scores, weight_grad, kp, *lat),
        [low(edge, count * HEAD_DIM)] + [low(count, *scores.shape[1:])] * 2,
    )


def halo_scores(group, halo, own_stat, kp, vp, lat, rows, cols, count):
    edge = RADIUS * rows
    near = edge + 2 * RADIUS * cols

    def kernel(halo_ref, stat, k_ref, v_ref, k_0, k_1, v_0, v_1, out, s_ref, d_ref, bias):
        queries = halo_query_cell(across(LANES, group * LANES), rows, cols)
        fill_bias(bias, down(edge) + group * LANES, queries, rows, cols)
        out[:, LOW] = stat[...]
        out[:, HIGH] = jnp.zeros((out.shape[0], LANES), jnp.float32)
        for head in range(count):
            key = near_keys(group, k_ref, (k_0, k_1), head)
            value = near_keys(group, v_ref, (v_0, v_1), head)
            s_ref[head] = dot(key, halo_head(halo_ref, edge, 0, head), (1, 1)) * (SCORE_SCALE * LOG2E) + bias[...]
            d_ref[head] = dot(value, halo_head(halo_ref, edge, 1, head), (1, 1))
            log_total, delta = part_stats(s_ref[head], d_ref[head])
            out[head : head + 1, HIGH] = log_total
            out[count + head : count + head + 1, HIGH] = delta

    return call(
        kernel, f"halo_scores_{group}", (halo, own_stat, kp, vp, *lat),
        [full(stat_rows(count), 2 * LANES)] + [full(count, near, LANES)] * 2,
        [pltpu.VMEM((near, LANES), jnp.float32)],
    )


def halo_finish(group, mine, theirs, scores, weight_grad, kp, lat, rows, cols, count):
    edge = RADIUS * rows

    def kernel(m, t, s_ref, d_ref, k_ref, k_0, k_1, out, final, p_ref, g_ref):
        final[...] = jnp.zeros_like(final)
        logs, deltas = combined(*((x[:count, half], x[count : 2 * count, half]) for x, half in ((m, LOW), (t, HIGH))))
        final[:count, :] = logs
        final[count : 2 * count, :] = deltas
        logs, deltas = combined(*((x[:count, half], x[count : 2 * count, half]) for x, half in ((m, HIGH), (t, LOW))))
        for head in range(count):
            row = slice(head, head + 1)
            p_ref[head], grad = gradients(s_ref[head], d_ref[head], logs[row], deltas[row])
            g_ref[head] = grad
            query_grad = dot(grad, near_keys(group, k_ref, (k_0, k_1), head), (0, 0)) * SCORE_SCALE
            out[:, lanes_of(head)] = query_grad[:edge].astype(jnp.bfloat16)

    return call(
        kernel, f"halo_finish_{group}", (mine, theirs, scores, weight_grad, kp, *lat),
        [low(edge, count * HEAD_DIM), full(stat_rows(count), LANES)] + [low(count, *scores.shape[1:])] * 2,
    )


def gradients(scores, weight_grad, log_total, delta):
    weights = jnp.exp2(scores - log_total)
    return weights.astype(jnp.bfloat16), (weights * (weight_grad - delta)).astype(jnp.bfloat16)


def stats_of(mine, theirs, count):
    return combined(*((x[:count, :], x[count : 2 * count, :]) for x in (mine, theirs)))


def lat_grads(qp, gp, halo, stats_0, mine, theirs, scores, weight_grad, lows, rows, cols, count):
    own, width, edge, lat_edge = rows * cols, count * HEAD_DIM, RADIUS * rows, RADIUS * cols

    def kernel(
        q_ref, g_ref, h_0, h_1, stat, m, t, s_ref, d_ref, p_0, l_0, p_1, l_1, out_0, out_1, final, lat_low
    ):
        final[...] = jnp.zeros_like(final)
        final[:count, :], final[count : 2 * count, :] = stats_of(m, t, count)
        for head in range(count):
            lanes = lanes_of(head)
            logs, deltas = (
                jnp.concatenate([ref[at : at + 1, :] for ref in (stat, final)], axis=1) for at in (head, count + head)
            )
            weights, grad = gradients(s_ref[head], d_ref[head], logs, deltas)
            lat_low[head] = grad
            sides = ((grad, (l_0, l_1), q_ref, SCORE_SCALE), (weights, (p_0, p_1), g_ref, 1.0))
            for part, (low_lat, low_halo, own_ref, scale) in enumerate(sides):
                every = [own_ref[:, lanes]] + [halo_head(h, edge, part, head) for h in (h_0, h_1)]
                met = jnp.concatenate([low_lat] + [x[head, edge:, :] for x in low_halo], axis=1)
                outside = (dot(met, jnp.concatenate(every, axis=0), (1, 0)) * scale).astype(jnp.bfloat16)
                for slot, out in enumerate((out_0, out_1)):
                    out[part * lat_edge : (part + 1) * lat_edge, lanes] = outside[
                        slot * lat_edge : (slot + 1) * lat_edge
                    ]

    return call(
        kernel, "lat_grads", (qp, gp, *halo, stats_0, mine, theirs, scores, weight_grad, *lows[0], *lows[1]),
        [low(2 * lat_edge, width)] * 2 + [full(stat_rows(count), LANES), low(count, 2 * lat_edge, own)],
    )


def own_grads(qp, gp, halo, stats, lat_low, scores, weight_grad, lows, kp, lat, rows, cols, count):
    own, width, edge = rows * cols, count * HEAD_DIM, RADIUS * rows

    def kernel(
        q_ref, g_ref, h_0, h_1, stat_0, stat_1, lat_ref, s_ref, d_ref, p_0, l_0, p_1, l_1, k_ref, k_0, k_1,
        dq_ref, dk_ref, dv_ref, sums,
    ):
        for head in range(count):
            lanes = lanes_of(head)
            logs, deltas = (
                jnp.concatenate([ref[at : at + 1, :] for ref in (stat_0, stat_1)], axis=1)
                for at in (head, count + head)
            )
            own_p, own_l = gradients(s_ref[head], d_ref[head], logs, deltas)
            every = jnp.concatenate([own_l, lat_ref[head]], axis=0)
            sums[0, :, lanes] = dot(every, every_key(k_ref, (k_0, k_1), head), (0, 0)) * SCORE_SCALE
            sides = ((own_l, (l_0, l_1), q_ref, SCORE_SCALE), (own_p, (p_0, p_1), g_ref, 1.0))
            for part, (low_own, low_halo, own_ref, scale) in enumerate(sides):
                inside = dot(low_own, own_ref[:, lanes], (1, 0))
                for group, (x, h) in enumerate(zip(low_halo, (h_0, h_1))):
                    at = group * LANES
                    near = inside[at : at + edge] + dot(x[head, :edge, :], halo_head(h, edge, part, head), (1, 0))
                    sums[1 + part, at : at + edge, lanes] = near * scale
                    sums[1 + part, at + edge : at + LANES, lanes] = inside[at + edge : at + LANES] * scale
        order = restore(rows, cols)
        twice = jnp.concatenate([order, order], axis=1)
        for place, result in enumerate((dq_ref, dk_ref, dv_ref)):
            for at in range(0, width, BLOCK):
                value = sums[place, :, at : at + BLOCK]
                high = value.astype(jnp.bfloat16)
                rest = (value - high.astype(jnp.float32)).astype(jnp.bfloat16)
                result[:, at : at + BLOCK] = dot(twice, jnp.concatenate([high, rest], axis=0), (1, 0))

    return call(
        kernel, "own_grads",
        (qp, gp, *halo, *stats, lat_low, scores, weight_grad, *lows[0], *lows[1], kp, *lat),
        [full(own, width)] * 3, [pltpu.VMEM((3, own, width), jnp.float32)],
    )


def restore(rows, cols):
    own = rows * cols
    row, col = own_query_cell(across(own), rows, cols)
    return jnp.where(down(own) == row * cols + col, 1.0, 0.0).astype(jnp.bfloat16)


def finish(query_grad, back, key_grad, value_grad, lat_back, rows, cols, count):
    own, width, edge, lat_edge = rows * cols, count * HEAD_DIM, RADIUS * rows, RADIUS * cols

    def kernel(dq_ref, b_0, b_1, dk_ref, dv_ref, a_1, a_0, out_q, out_k, out_v, done_q, done_k, done_v, sems):
        copies = []

        def write(done, out):
            copies.append(pltpu.make_async_copy(done, out, sems.at[len(copies)]))
            copies[-1].start()

        middle = slice(lat_edge, own - lat_edge)
        for part, (grad, done, out) in enumerate(((dk_ref, done_k, out_k), (dv_ref, done_v, out_v))):
            done[middle, :] = grad[middle, :].astype(jnp.bfloat16)
            for slot, arrived in enumerate((a_0, a_1)):
                start = pl.multiple_of(slot_side("lat", slot) * (own - lat_edge), 16)
                added = arrived[part * lat_edge : (part + 1) * lat_edge, :].astype(jnp.float32)
                done[pl.ds(start, lat_edge), :] = (grad[pl.ds(start, lat_edge), :] + added).astype(jnp.bfloat16)
            write(done, out)
        position = across(2 * edge)
        place = jnp.where(position < edge, position, position - edge + LANES)
        row, col = own_query_cell(place, rows, cols)
        spread = jnp.where(down(own) == row * cols + col, 1.0, 0.0).astype(jnp.bfloat16)
        for at in range(0, width, BLOCK):
            lanes = slice(at, at + BLOCK)
            arrived = jnp.concatenate([b_0[:, lanes], b_1[:, lanes]], axis=0)
            done_q[:, lanes] = (dq_ref[:, lanes] + dot(spread, arrived, (1, 0))).astype(jnp.bfloat16)
        write(done_q, out_q)
        for copy in copies:
            copy.wait()

    return call(
        kernel, "finish", (query_grad, *back, key_grad, value_grad, *lat_back), [low(own, width)] * 3,
        [pltpu.VMEM((own, width), jnp.bfloat16)] * 3 + [pltpu.SemaphoreType.DMA((3,))],
        outs=[HBM_SPEC] * 3,
    )


def swap(axis, slot, wrap, array):
    count = lax.axis_size(axis)
    pairs = []
    for lower in range(slot, count if wrap else count - 1, 2):
        upper = (lower + 1) % count
        pairs += [(lower, upper), (upper, lower)]
    return lax.ppermute(array, axis, pairs)


def swap_lon(slot, array):
    return swap("lon", 1 - slot, True, array)


def swap_lat(slot, array):
    return swap("lat", slot, False, array)


def after(value, *earlier):
    return lax.optimization_barrier((value, *earlier))[0]


def held(value, *earlier, flops=1 << 33):
    spec = pl.BlockSpec(memory_space=pl.ANY)
    return call(
        lambda *refs: None, "held", (value, *earlier), [jax.ShapeDtypeStruct(value.shape, value.dtype)],
        flops=flops, aliases={0: 0}, ins=[spec] * (1 + len(earlier)), outs=[spec],
    )[0]


def shards(queries, key_field, value_field, out_grad):
    rows, cols, width = queries.shape
    own = rows * cols
    flat = lambda x: x.reshape(own, width)
    queries, key_field, value_field, out_grad = map(flat, (queries, key_field, value_field, out_grad))
    size = (rows, cols, width // HEAD_DIM)

    qp, gp, *sends = pack_queries(queries, out_grad, key_field, value_field, *size)
    sends, (key_field, value_field), edges = sends[:2], sends[2:4], sends[4:]
    halo = [swap_lon(slot, send) for slot, send in enumerate(sends)]
    lat = [swap_lat(place & 1, edge) for place, edge in enumerate(edges)]
    kp, vp, *stats, own_s, own_d = own_scores(qp, gp, key_field, value_field, *size)
    *own_stat, lat_s, lat_d = lat_scores(qp, gp, lat, stats, *size)
    theirs_1 = swap_lon(1, own_stat[1])

    mine_0, *scores_0 = halo_scores(0, halo[0], own_stat[0], kp, vp, lat, *size)
    theirs_0 = swap_lon(0, mine_0)
    part_1, *scores_1 = halo_part(1, after(halo[1], mine_0), kp, vp, lat, *size)
    other_1 = held(swap_lon(1, part_1))
    theirs_0 = held(theirs_0, part_1, flops=1 << 29)
    result_0, stats_0, *lows_0 = halo_finish(0, mine_0, theirs_0, *scores_0, kp, lat[:2], *size)
    theirs_1 = held(theirs_1, result_0, flops=1 << 29)
    result_1, *lows_1 = halo_rest(1, part_1, theirs_1, *scores_1, kp, lat[:2], *size)
    result_0 = held(result_0, result_1, flops=1 << 29)
    result_1 = held(result_1, result_0, flops=1 << 29)
    back = [swap_lon(0, result_0), swap_lon(1, result_1)]
    *lat_back, stats_1, lat_low = lat_grads(
        qp, gp, halo, stats_0, own_stat[1], other_1, lat_s, lat_d, (lows_0, lows_1), *size
    )
    dq, dk, dv = own_grads(
        qp, gp, halo, (stats_0, stats_1), lat_low, own_s, own_d, (lows_0, lows_1), kp, lat[:2], *size
    )
    lat_back = [swap_lat(slot, lat_back[slot]) for slot in (1, 0)]
    outs = finish(dq, back, held(dk), dv, lat_back, *size)
    shape = (rows, cols, width)
    return tuple(x.reshape(shape) for x in outs)


def solution(mesh):
    spec = P("lat", "lon", None)
    return jax.shard_map(
        shards, mesh=mesh, in_specs=(spec,) * 4, out_specs=(spec,) * 3, check_vma=False
    )
```

```python
import math

import jax
import jax.numpy as jnp
from jax import lax
from jax.experimental import pallas as pl
from jax.experimental.pallas import tpu as pltpu
from jax.sharding import PartitionSpec as P

HEAD_DIM = 128
WINDOW = 13
RADIUS = WINDOW // 2
LANES = 128
MASKED = -1e30
LOG2E = math.log2(math.e)
VMEM_BYTES = 16 * 1024 * 1024


def split(index, width):
    if width & (width - 1) == 0:
        whole = index >> (width.bit_length() - 1)
    else:
        whole = (index * ((1 << 12) // width + 1)) >> 12
    return whole, index - whole * width


def odd(axis):
    return lax.axis_index(axis) & 1


def slot_side(axis, slot):
    parity = odd(axis)
    return parity if slot == (0 if axis == "lon" else 1) else 1 - parity


def own_query_cell(position, rows, cols):
    edge = rows * RADIUS
    group = position >> 7
    place = position & (LANES - 1)
    side = jnp.where(group == 0, slot_side("lon", 0), slot_side("lon", 1))
    row_a, col_a = split(place, RADIUS)
    inner = cols - 2 * RADIUS
    row_b, col_b = split(place - edge + (LANES - edge) * group, inner)
    at_edge = place < edge
    row = jnp.where(at_edge, row_a, row_b)
    col = jnp.where(at_edge, side * (cols - RADIUS) + col_a, RADIUS + col_b)
    return row, col


def halo_query_cell(position, rows, cols):
    edge = rows * RADIUS
    group = position >> 7
    place = position & (LANES - 1)
    side = jnp.where(group == 0, slot_side("lon", 0), slot_side("lon", 1))
    row, col = split(place, RADIUS)
    col = jnp.where(side == 1, cols, -RADIUS) + col
    col = jnp.where(place < edge, col, 1 << 12)
    return row, col


def lat_key_cell(slot, position, rows, cols):
    row, col = split(position, cols)
    return row + jnp.where(slot_side("lat", slot) == 1, rows, -RADIUS), col


def bias_of(key_cells, query_cells, rows):
    total_rows = rows * lax.axis_size("lat")
    first = rows * lax.axis_index("lat")
    key_row, key_col = key_cells
    query_row, query_col = query_cells
    start = jnp.clip(first + query_row - RADIUS, 0, total_rows - WINDOW)
    from_start = first + key_row - start
    inside = (from_start >= 0) & (from_start < WINDOW)
    inside = inside & (jnp.abs(key_col - query_col) <= RADIUS)
    return jnp.where(inside, 0.0, MASKED)


def down(count):
    return lax.broadcasted_iota(jnp.int32, (count, 1), 0)


def across(count, start=0):
    return lax.broadcasted_iota(jnp.int32, (1, count), 1) + start


def dot(a, b, contract):
    return lax.dot_general(a, b, ((contract[:1], contract[1:]), ((), ())), preferred_element_type=jnp.float32)


def call(kernel, name, operands, out_shapes, scratch=(), flops=0, aliases=None, outs=None, ins=None):
    return pl.pallas_call(
        kernel,
        name=name,
        in_specs=ins or [VMEM_SPEC] * len(operands),
        out_specs=outs or [VMEM_SPEC] * len(out_shapes),
        out_shape=out_shapes,
        scratch_shapes=scratch,
        input_output_aliases=aliases or {},
        compiler_params=pltpu.CompilerParams(vmem_limit_bytes=VMEM_BYTES),
        cost_estimate=pl.CostEstimate(flops=flops, bytes_accessed=0, transcendentals=0),
    )(*operands)


def low(*shape):
    return jax.ShapeDtypeStruct(shape, jnp.bfloat16)


def full(*shape):
    return jax.ShapeDtypeStruct(shape, jnp.float32)


def lanes_of(head, count=1):
    return slice(head * HEAD_DIM, (head + count) * HEAD_DIM)


def selection(row, col, rows, cols):
    source = across(rows * cols)
    return jnp.where(source == row * cols + col, 1.0, 0.0).astype(jnp.bfloat16)


HBM_SPEC, VMEM_SPEC = pl.BlockSpec(memory_space=pltpu.HBM), pl.BlockSpec(memory_space=pltpu.VMEM)
BLOCK = 2 * HEAD_DIM


def pack_queries(queries, out_grad, key_field, value_field, rows, cols, count):
    own, edge, width = rows * cols, rows * RADIUS, count * HEAD_DIM
    lat_edge = RADIUS * cols

    def kernel(
        q_hbm, g_hbm, k_hbm, v_hbm, qp_ref, gp_ref, send_0, send_1, k_ref, v_ref, k_0, k_1, v_0, v_1, q_ref, g_ref, sems
    ):
        copies = [
            pltpu.make_async_copy(src, dst, sems.at[i])
            for i, (src, dst) in enumerate(
                ((q_hbm, q_ref), (g_hbm, g_ref), (k_hbm, k_ref), (v_hbm, v_ref))
            )
        ]
        for copy in copies:
            copy.start()
        order = selection(*own_query_cell(down(own), rows, cols), rows, cols)
        for place, (src, dst) in enumerate(((q_ref, qp_ref), (g_ref, gp_ref))):
            copies[place].wait()
            for at in range(0, width, BLOCK):
                here = slice(at, at + BLOCK)
                moved = dot(order, src[:, here], (1, 0)).astype(jnp.bfloat16)
                dst[:, here] = moved
                for group, send in enumerate((send_0, send_1)):
                    send[place * edge : (place + 1) * edge, here] = moved[group * LANES : group * LANES + edge]
        for copy, src, sends in zip(copies[2:], (k_ref, v_ref), ((k_0, k_1), (v_0, v_1))):
            copy.wait()
            for slot, send in enumerate(sends):
                start = pl.multiple_of(slot_side("lat", slot) * (own - lat_edge), 16)
                send[...] = src[pl.ds(start, lat_edge), :]

    operands = [
        pltpu.with_memory_space_constraint(x, pltpu.HBM) for x in (queries, out_grad, key_field, value_field)
    ]
    return call(
        kernel, "pack_queries", operands,
        [low(own, width)] * 2 + [low(2 * edge, width), low(2 * edge + 16, width)] + [low(own, width)] * 2 + [low(lat_edge, width)] * 4,
        [pltpu.VMEM((own, width), jnp.bfloat16)] * 2 + [pltpu.SemaphoreType.DMA((4,))],
        ins=[HBM_SPEC] * 4,
    )


def own_scores(qp, gp, key_field, value_field, rows, cols, count):
    own, width = rows * cols, key_field.shape[1]

    def kernel(q_ref, g_ref, k_ref, v_ref, kp_ref, vp_ref, out_0, out_1, s_ref, d_ref, bias):
        order = selection(*own_query_cell(down(own), rows, cols), rows, cols)
        for src, dst in ((k_ref, kp_ref), (v_ref, vp_ref)):
            for at in range(0, width, BLOCK):
                here = slice(at, at + BLOCK)
                dst[:, here] = dot(order, src[:, here], (1, 0)).astype(jnp.bfloat16)
        bias[...] = bias_of(
            own_query_cell(down(own), rows, cols), own_query_cell(across(own), rows, cols), rows
        )
        for out in (out_0, out_1):
            out[...] = jnp.zeros_like(out)
        for head in range(count):
            lanes = lanes_of(head)
            s_ref[head] = dot(kp_ref[:, lanes], q_ref[:, lanes], (1, 1)) * (SCORE_SCALE * LOG2E) + bias[...]
            d_ref[head] = dot(vp_ref[:, lanes], g_ref[:, lanes], (1, 1))
            put_stats((out_0, out_1), head, part_stats(s_ref[head], d_ref[head]), count)

    return call(
        kernel, "own_scores", (qp, gp, key_field, value_field),
        [low(own, width)] * 2 + [full(stat_rows(count), LANES)] * 2 + [full(count, own, own)] * 2,
        [pltpu.VMEM((own, own), jnp.float32)],
    )


def put_stats(outs, head, stats, count):
    for out, half in zip(outs, (LOW, HIGH)):
        for at, stat in zip((head, count + head), stats):
            out[at : at + 1, :] = stat[:, half]


def halo_head(ref, edge, part, head):
    rows = ref[part * edge : (part + 1) * edge, lanes_of(head)]
    return jnp.concatenate([rows, jnp.zeros((LANES - edge, HEAD_DIM), jnp.bfloat16)], axis=0)


def near_keys(group, own_ref, lat_refs, head):
    lanes, edge = lanes_of(head), lat_refs[0].shape[0]
    pieces = [own_ref[group * LANES : group * LANES + edge, lanes]]
    return jnp.concatenate(pieces + [ref[:, lanes] for ref in lat_refs], axis=0)


def every_key(own_ref, lat_refs, head):
    lanes = lanes_of(head)
    return jnp.concatenate([ref[:, lanes] for ref in (own_ref, *lat_refs)], axis=0)


def fill_bias(bias, own_position, queries, rows, cols):
    at, edge = own_position.shape[0], RADIUS * cols
    bias[:at, :] = bias_of(own_query_cell(own_position, rows, cols), queries, rows)
    for slot in (0, 1):
        here = slice(at + slot * edge, at + (slot + 1) * edge)
        bias[here, :] = bias_of(lat_key_cell(slot, down(edge), rows, cols), queries, rows)


LOW, HIGH = slice(0, LANES), slice(LANES, 2 * LANES)
SCORE_SCALE = 1.0 / math.sqrt(HEAD_DIM)


def part_stats(scores, weight_grad):
    peak = jnp.max(scores, axis=0, keepdims=True)
    weights = jnp.exp2(scores - peak)
    total = jnp.sum(weights, axis=0, keepdims=True)
    dotted = jnp.sum(weights * weight_grad, axis=0, keepdims=True)
    return peak + jnp.log(total) * LOG2E, dotted / total


def stat_rows(count):
    return -(-2 * count // 8) * 8


def lat_scores(qp, gp, lat, stats, rows, cols, count):
    own, lat_edge = rows * cols, RADIUS * cols

    def kernel(q_ref, g_ref, k_0, k_1, v_0, v_1, before_0, before_1, out_0, out_1, s_ref, d_ref, bias, part_0, part_1):
        queries = own_query_cell(across(own), rows, cols)
        for slot in (0, 1):
            cells = lat_key_cell(slot, down(lat_edge), rows, cols)
            bias[slot * lat_edge : (slot + 1) * lat_edge, :] = bias_of(cells, queries, rows)
        for head in range(count):
            lanes = lanes_of(head)
            key, value = (
                jnp.concatenate([ref[:, lanes] for ref in pair], axis=0) for pair in ((k_0, k_1), (v_0, v_1))
            )
            s_ref[head] = dot(key, q_ref[:, lanes], (1, 1)) * (SCORE_SCALE * LOG2E) + bias[...]
            d_ref[head] = dot(value, g_ref[:, lanes], (1, 1))
            put_stats((part_0, part_1), head, part_stats(s_ref[head], d_ref[head]), count)
        for out, part, before in ((out_0, part_0, before_0), (out_1, part_1, before_1)):
            out[...] = jnp.zeros_like(out)
            out[:count, :], out[count : 2 * count, :] = stats_of(part, before, count)

    return call(
        kernel, "lat_scores", (qp, gp, *lat, *stats),
        [full(stat_rows(count), LANES)] * 2 + [full(count, 2 * lat_edge, own)] * 2,
        [pltpu.VMEM((2 * lat_edge, own), jnp.float32)] + [pltpu.VMEM((stat_rows(count), LANES), jnp.float32)] * 2,
    )


def combined(mine, theirs):
    (a, delta_a), (b, delta_b) = mine, theirs
    peak = jnp.maximum(a, b)
    part_a, part_b = jnp.exp2(a - peak), jnp.exp2(b - peak)
    total = part_a + part_b
    return peak + jnp.log(total) * LOG2E, (part_a * delta_a + part_b * delta_b) / total


def halo_part(group, halo, kp, vp, lat, rows, cols, count):
    edge = RADIUS * rows
    near = edge + 2 * RADIUS * cols

    def kernel(halo_ref, k_ref, v_ref, k_0, k_1, v_0, v_1, out, s_ref, d_ref, bias):
        queries = halo_query_cell(across(LANES, group * LANES), rows, cols)
        fill_bias(bias, down(edge) + group * LANES, queries, rows, cols)
        out[...] = jnp.zeros_like(out)
        for head in range(count):
            key = near_keys(group, k_ref, (k_0, k_1), head)
            value = near_keys(group, v_ref, (v_0, v_1), head)
            s_ref[head] = dot(key, halo_head(halo_ref, edge, 0, head), (1, 1)) * (SCORE_SCALE * LOG2E) + bias[...]
            d_ref[head] = dot(value, halo_head(halo_ref, edge, 1, head), (1, 1))
            log_total, delta = part_stats(s_ref[head], d_ref[head])
            out[head : head + 1, :] = log_total
            out[count + head : count + head + 1, :] = delta

    return call(
        kernel, f"halo_part_{group}", (halo, kp, vp, *lat),
        [full(stat_rows(count), LANES)] + [full(count, near, LANES)] * 2,
        [pltpu.VMEM((near, LANES), jnp.float32)],
    )


def halo_rest(group, mine, theirs, scores, weight_grad, kp, lat, rows, cols, count):
    edge = RADIUS * rows

    def kernel(m, t, s_ref, d_ref, k_ref, k_0, k_1, out, p_ref, g_ref):
        logs, deltas = stats_of(m, t, count)
        for head in range(count):
            row = slice(head, head + 1)
            p_ref[head], grad = gradients(s_ref[head], d_ref[head], logs[row], deltas[row])
            g_ref[head] = grad
            query_grad = dot(grad, near_keys(group, k_ref, (k_0, k_1), head), (0, 0)) * SCORE_SCALE
            out[:, lanes_of(head)] = query_grad[:edge].astype(jnp.bfloat16)

    return call(
        kernel, f"halo_rest_{group}", (mine, theirs, scores, weight_grad, kp, *lat),
        [low(edge, count * HEAD_DIM)] + [low(count, *scores.shape[1:])] * 2,
    )


def halo_scores(group, halo, own_stat, kp, vp, lat, rows, cols, count):
    edge = RADIUS * rows
    near = edge + 2 * RADIUS * cols

    def kernel(halo_ref, stat, k_ref, v_ref, k_0, k_1, v_0, v_1, out, s_ref, d_ref, bias):
        queries = halo_query_cell(across(LANES, group * LANES), rows, cols)
        fill_bias(bias, down(edge) + group * LANES, queries, rows, cols)
        out[:, LOW] = stat[...]
        out[:, HIGH] = jnp.zeros((out.shape[0], LANES), jnp.float32)
        for head in range(count):
            key = near_keys(group, k_ref, (k_0, k_1), head)
            value = near_keys(group, v_ref, (v_0, v_1), head)
            s_ref[head] = dot(key, halo_head(halo_ref, edge, 0, head), (1, 1)) * (SCORE_SCALE * LOG2E) + bias[...]
            d_ref[head] = dot(value, halo_head(halo_ref, edge, 1, head), (1, 1))
            log_total, delta = part_stats(s_ref[head], d_ref[head])
            out[head : head + 1, HIGH] = log_total
            out[count + head : count + head + 1, HIGH] = delta

    return call(
        kernel, f"halo_scores_{group}", (halo, own_stat, kp, vp, *lat),
        [full(stat_rows(count), 2 * LANES)] + [full(count, near, LANES)] * 2,
        [pltpu.VMEM((near, LANES), jnp.float32)],
    )


def halo_finish(group, mine, theirs, scores, weight_grad, kp, lat, rows, cols, count):
    edge = RADIUS * rows

    def kernel(m, t, s_ref, d_ref, k_ref, k_0, k_1, out, final, p_ref, g_ref):
        final[...] = jnp.zeros_like(final)
        logs, deltas = combined(*((x[:count, half], x[count : 2 * count, half]) for x, half in ((m, LOW), (t, HIGH))))
        final[:count, :] = logs
        final[count : 2 * count, :] = deltas
        logs, deltas = combined(*((x[:count, half], x[count : 2 * count, half]) for x, half in ((m, HIGH), (t, LOW))))
        for head in range(count):
            row = slice(head, head + 1)
            p_ref[head], grad = gradients(s_ref[head], d_ref[head], logs[row], deltas[row])
            g_ref[head] = grad
            query_grad = dot(grad, near_keys(group, k_ref, (k_0, k_1), head), (0, 0)) * SCORE_SCALE
            out[:, lanes_of(head)] = query_grad[:edge].astype(jnp.bfloat16)

    return call(
        kernel, f"halo_finish_{group}", (mine, theirs, scores, weight_grad, kp, *lat),
        [low(edge, count * HEAD_DIM), full(stat_rows(count), LANES)] + [low(count, *scores.shape[1:])] * 2,
    )


def gradients(scores, weight_grad, log_total, delta):
    weights = jnp.exp2(scores - log_total)
    return weights.astype(jnp.bfloat16), (weights * (weight_grad - delta)).astype(jnp.bfloat16)


def stats_of(mine, theirs, count):
    return combined(*((x[:count, :], x[count : 2 * count, :]) for x in (mine, theirs)))


def lat_grads(qp, gp, halo, stats_0, mine, theirs, scores, weight_grad, lows, rows, cols, count):
    own, width, edge, lat_edge = rows * cols, count * HEAD_DIM, RADIUS * rows, RADIUS * cols

    def kernel(
        q_ref, g_ref, h_0, h_1, stat, m, t, s_ref, d_ref, p_0, l_0, p_1, l_1, out_0, out_1, final, lat_low
    ):
        final[...] = jnp.zeros_like(final)
        final[:count, :], final[count : 2 * count, :] = stats_of(m, t, count)
        for head in range(count):
            lanes = lanes_of(head)
            logs, deltas = (
                jnp.concatenate([ref[at : at + 1, :] for ref in (stat, final)], axis=1) for at in (head, count + head)
            )
            weights, grad = gradients(s_ref[head], d_ref[head], logs, deltas)
            lat_low[head] = grad
            sides = ((grad, (l_0, l_1), q_ref, SCORE_SCALE), (weights, (p_0, p_1), g_ref, 1.0))
            for part, (low_lat, low_halo, own_ref, scale) in enumerate(sides):
                every = [own_ref[:, lanes]] + [halo_head(h, edge, part, head) for h in (h_0, h_1)]
                met = jnp.concatenate([low_lat] + [x[head, edge:, :] for x in low_halo], axis=1)
                outside = (dot(met, jnp.concatenate(every, axis=0), (1, 0)) * scale).astype(jnp.bfloat16)
                for slot, out in enumerate((out_0, out_1)):
                    out[part * lat_edge : (part + 1) * lat_edge, lanes] = outside[
                        slot * lat_edge : (slot + 1) * lat_edge
                    ]

    return call(
        kernel, "lat_grads", (qp, gp, *halo, stats_0, mine, theirs, scores, weight_grad, *lows[0], *lows[1]),
        [low(2 * lat_edge, width)] * 2 + [full(stat_rows(count), LANES), low(count, 2 * lat_edge, own)],
    )


def own_grads(qp, gp, halo, stats, lat_low, scores, weight_grad, lows, kp, lat, rows, cols, count):
    own, width, edge = rows * cols, count * HEAD_DIM, RADIUS * rows

    def kernel(
        q_ref, g_ref, h_0, h_1, stat_0, stat_1, lat_ref, s_ref, d_ref, p_0, l_0, p_1, l_1, k_ref, k_0, k_1,
        dq_ref, dk_ref, dv_ref, sums,
    ):
        for head in range(count):
            lanes = lanes_of(head)
            logs, deltas = (
                jnp.concatenate([ref[at : at + 1, :] for ref in (stat_0, stat_1)], axis=1)
                for at in (head, count + head)
            )
            own_p, own_l = gradients(s_ref[head], d_ref[head], logs, deltas)
            every = jnp.concatenate([own_l, lat_ref[head]], axis=0)
            sums[0, :, lanes] = dot(every, every_key(k_ref, (k_0, k_1), head), (0, 0)) * SCORE_SCALE
            sides = ((own_l, (l_0, l_1), q_ref, SCORE_SCALE), (own_p, (p_0, p_1), g_ref, 1.0))
            for part, (low_own, low_halo, own_ref, scale) in enumerate(sides):
                inside = dot(low_own, own_ref[:, lanes], (1, 0))
                for group, (x, h) in enumerate(zip(low_halo, (h_0, h_1))):
                    at = group * LANES
                    near = inside[at : at + edge] + dot(x[head, :edge, :], halo_head(h, edge, part, head), (1, 0))
                    sums[1 + part, at : at + edge, lanes] = near * scale
                    sums[1 + part, at + edge : at + LANES, lanes] = inside[at + edge : at + LANES] * scale
        order = restore(rows, cols)
        twice = jnp.concatenate([order, order], axis=1)
        for place, result in enumerate((dq_ref, dk_ref, dv_ref)):
            for at in range(0, width, BLOCK):
                value = sums[place, :, at : at + BLOCK]
                high = value.astype(jnp.bfloat16)
                rest = (value - high.astype(jnp.float32)).astype(jnp.bfloat16)
                result[:, at : at + BLOCK] = dot(twice, jnp.concatenate([high, rest], axis=0), (1, 0))

    return call(
        kernel, "own_grads",
        (qp, gp, *halo, *stats, lat_low, scores, weight_grad, *lows[0], *lows[1], kp, *lat),
        [full(own, width)] * 3, [pltpu.VMEM((3, own, width), jnp.float32)],
    )


def restore(rows, cols):
    own = rows * cols
    row, col = own_query_cell(across(own), rows, cols)
    return jnp.where(down(own) == row * cols + col, 1.0, 0.0).astype(jnp.bfloat16)


def finish(query_grad, back, key_grad, value_grad, lat_back, rows, cols, count):
    own, width, edge, lat_edge = rows * cols, count * HEAD_DIM, RADIUS * rows, RADIUS * cols

    def kernel(dq_ref, b_0, b_1, dk_ref, dv_ref, a_1, a_0, out_q, out_k, out_v, done_q, done_k, done_v, sems):
        copies = []

        def write(done, out):
            copies.append(pltpu.make_async_copy(done, out, sems.at[len(copies)]))
            copies[-1].start()

        middle = slice(lat_edge, own - lat_edge)
        for part, (grad, done, out) in enumerate(((dk_ref, done_k, out_k), (dv_ref, done_v, out_v))):
            done[middle, :] = grad[middle, :].astype(jnp.bfloat16)
            for slot, arrived in enumerate((a_0, a_1)):
                start = pl.multiple_of(slot_side("lat", slot) * (own - lat_edge), 16)
                added = arrived[part * lat_edge : (part + 1) * lat_edge, :].astype(jnp.float32)
                done[pl.ds(start, lat_edge), :] = (grad[pl.ds(start, lat_edge), :] + added).astype(jnp.bfloat16)
            write(done, out)
        position = across(2 * edge)
        place = jnp.where(position < edge, position, position - edge + LANES)
        row, col = own_query_cell(place, rows, cols)
        spread = jnp.where(down(own) == row * cols + col, 1.0, 0.0).astype(jnp.bfloat16)
        for at in range(0, width, BLOCK):
            lanes = slice(at, at + BLOCK)
            arrived = jnp.concatenate([b_0[:, lanes], b_1[:, lanes]], axis=0)
            done_q[:, lanes] = (dq_ref[:, lanes] + dot(spread, arrived, (1, 0))).astype(jnp.bfloat16)
        write(done_q, out_q)
        for copy in copies:
            copy.wait()

    return call(
        kernel, "finish", (query_grad, *back, key_grad, value_grad, *lat_back), [low(own, width)] * 3,
        [pltpu.VMEM((own, width), jnp.bfloat16)] * 3 + [pltpu.SemaphoreType.DMA((3,))],
        outs=[HBM_SPEC] * 3,
    )


def swap(axis, slot, wrap, array):
    count = lax.axis_size(axis)
    pairs = []
    for lower in range(slot, count if wrap else count - 1, 2):
        upper = (lower + 1) % count
        pairs += [(lower, upper), (upper, lower)]
    return lax.ppermute(array, axis, pairs)


def swap_lon(slot, array):
    return swap("lon", 1 - slot, True, array)


def swap_lat(slot, array):
    return swap("lat", slot, False, array)


def after(value, *earlier):
    return lax.optimization_barrier((value, *earlier))[0]


def held(value, *earlier, flops=1 << 33):
    spec = pl.BlockSpec(memory_space=pl.ANY)
    return call(
        lambda *refs: None, "held", (value, *earlier), [jax.ShapeDtypeStruct(value.shape, value.dtype)],
        flops=flops, aliases={0: 0}, ins=[spec] * (1 + len(earlier)), outs=[spec],
    )[0]


def shards(queries, key_field, value_field, out_grad):
    rows, cols, width = queries.shape
    own = rows * cols
    flat = lambda x: x.reshape(own, width)
    queries, key_field, value_field, out_grad = map(flat, (queries, key_field, value_field, out_grad))
    size = (rows, cols, width // HEAD_DIM)

    qp, gp, *sends = pack_queries(queries, out_grad, key_field, value_field, *size)
    sends, (key_field, value_field), edges = sends[:2], sends[2:4], sends[4:]
    halo = [swap_lon(slot, send) for slot, send in enumerate(sends)]
    lat = [swap_lat(place & 1, edge) for place, edge in enumerate(edges)]
    kp, vp, *stats, own_s, own_d = own_scores(qp, gp, key_field, value_field, *size)
    *own_stat, lat_s, lat_d = lat_scores(qp, gp, lat, stats, *size)
    theirs_1 = swap_lon(1, own_stat[1])

    mine_0, *scores_0 = halo_scores(0, halo[0], own_stat[0], kp, vp, lat, *size)
    theirs_0 = swap_lon(0, mine_0)
    part_1, *scores_1 = halo_part(1, after(halo[1], mine_0), kp, vp, lat, *size)
    other_1 = held(swap_lon(1, part_1))
    theirs_0 = held(theirs_0, part_1, flops=1 << 29)
    result_0, stats_0, *lows_0 = halo_finish(0, mine_0, theirs_0, *scores_0, kp, lat[:2], *size)
    theirs_1 = held(theirs_1, result_0, flops=1 << 29)
    result_1, *lows_1 = halo_rest(1, part_1, theirs_1, *scores_1, kp, lat[:2], *size)
    back_1 = swap_lon(1, result_1)
    *lat_back, stats_1, lat_low = lat_grads(
        qp, gp, halo, stats_0, own_stat[1], other_1, lat_s, lat_d, (lows_0, lows_1), *size
    )
    dq, dk, dv = own_grads(
        qp, gp, halo, (stats_0, stats_1), lat_low, own_s, own_d, (lows_0, lows_1), kp, lat[:2], *size
    )
    back = [swap_lon(0, held(result_0, lat_back[1], flops=1 << 29)), back_1]
    lat_back = [swap_lat(slot, lat_back[slot]) for slot in (1, 0)]
    outs = finish(dq, back, held(dk), dv, lat_back, *size)
    shape = (rows, cols, width)
    return tuple(x.reshape(shape) for x in outs)


def solution(mesh):
    spec = P("lat", "lon", None)
    return jax.shard_map(
        shards, mesh=mesh, in_specs=(spec,) * 4, out_specs=(spec,) * 3, check_vma=False
    )
```

```python
import math

import jax
import jax.numpy as jnp
from jax import lax
from jax.experimental import pallas as pl
from jax.experimental.pallas import tpu as pltpu
from jax.sharding import PartitionSpec as P

HEAD_DIM = 128
WINDOW = 13
RADIUS = WINDOW // 2
LANES = 128
MASKED = -1e30
LOG2E = math.log2(math.e)
VMEM_BYTES = 16 * 1024 * 1024


def split(index, width):
    if width & (width - 1) == 0:
        whole = index >> (width.bit_length() - 1)
    else:
        whole = (index * ((1 << 12) // width + 1)) >> 12
    return whole, index - whole * width


def odd(axis):
    return lax.axis_index(axis) & 1


def slot_side(axis, slot):
    parity = odd(axis)
    return parity if slot == (0 if axis == "lon" else 1) else 1 - parity


def own_query_cell(position, rows, cols):
    edge = rows * RADIUS
    group = position >> 7
    place = position & (LANES - 1)
    side = jnp.where(group == 0, slot_side("lon", 0), slot_side("lon", 1))
    row_a, col_a = split(place, RADIUS)
    inner = cols - 2 * RADIUS
    row_b, col_b = split(place - edge + (LANES - edge) * group, inner)
    at_edge = place < edge
    row = jnp.where(at_edge, row_a, row_b)
    col = jnp.where(at_edge, side * (cols - RADIUS) + col_a, RADIUS + col_b)
    return row, col


def halo_query_cell(position, rows, cols):
    edge = rows * RADIUS
    group = position >> 7
    place = position & (LANES - 1)
    side = jnp.where(group == 0, slot_side("lon", 0), slot_side("lon", 1))
    row, col = split(place, RADIUS)
    col = jnp.where(side == 1, cols, -RADIUS) + col
    col = jnp.where(place < edge, col, 1 << 12)
    return row, col


def lat_key_cell(slot, position, rows, cols):
    row, col = split(position, cols)
    return row + jnp.where(slot_side("lat", slot) == 1, rows, -RADIUS), col


def bias_of(key_cells, query_cells, rows):
    total_rows = rows * lax.axis_size("lat")
    first = rows * lax.axis_index("lat")
    key_row, key_col = key_cells
    query_row, query_col = query_cells
    start = jnp.clip(first + query_row - RADIUS, 0, total_rows - WINDOW)
    from_start = first + key_row - start
    inside = (from_start >= 0) & (from_start < WINDOW)
    inside = inside & (jnp.abs(key_col - query_col) <= RADIUS)
    return jnp.where(inside, 0.0, MASKED)


def down(count):
    return lax.broadcasted_iota(jnp.int32, (count, 1), 0)


def across(count, start=0):
    return lax.broadcasted_iota(jnp.int32, (1, count), 1) + start


def dot(a, b, contract):
    return lax.dot_general(a, b, ((contract[:1], contract[1:]), ((), ())), preferred_element_type=jnp.float32)


def call(kernel, name, operands, out_shapes, scratch=(), flops=0, aliases=None, outs=None, ins=None):
    return pl.pallas_call(
        kernel,
        name=name,
        in_specs=ins or [VMEM_SPEC] * len(operands),
        out_specs=outs or [VMEM_SPEC] * len(out_shapes),
        out_shape=out_shapes,
        scratch_shapes=scratch,
        input_output_aliases=aliases or {},
        compiler_params=pltpu.CompilerParams(vmem_limit_bytes=VMEM_BYTES),
        cost_estimate=pl.CostEstimate(flops=flops, bytes_accessed=0, transcendentals=0),
    )(*operands)


def low(*shape):
    return jax.ShapeDtypeStruct(shape, jnp.bfloat16)


def full(*shape):
    return jax.ShapeDtypeStruct(shape, jnp.float32)


def lanes_of(head, count=1):
    return slice(head * HEAD_DIM, (head + count) * HEAD_DIM)


def selection(row, col, rows, cols):
    source = across(rows * cols)
    return jnp.where(source == row * cols + col, 1.0, 0.0).astype(jnp.bfloat16)


HBM_SPEC, VMEM_SPEC = pl.BlockSpec(memory_space=pltpu.HBM), pl.BlockSpec(memory_space=pltpu.VMEM)
BLOCK = 2 * HEAD_DIM


def pack_queries(queries, out_grad, key_field, value_field, rows, cols, count):
    own, edge, width = rows * cols, rows * RADIUS, count * HEAD_DIM
    lat_edge = RADIUS * cols

    def kernel(
        q_hbm, g_hbm, k_hbm, v_hbm, qp_ref, gp_ref, send_0, send_1, k_ref, v_ref, k_0, k_1, v_0, v_1, q_ref, g_ref, sems
    ):
        copies = [
            pltpu.make_async_copy(src, dst, sems.at[i])
            for i, (src, dst) in enumerate(
                ((q_hbm, q_ref), (g_hbm, g_ref), (k_hbm, k_ref), (v_hbm, v_ref))
            )
        ]
        for copy in copies:
            copy.start()
        order = selection(*own_query_cell(down(own), rows, cols), rows, cols)
        for place, (src, dst) in enumerate(((q_ref, qp_ref), (g_ref, gp_ref))):
            copies[place].wait()
            for at in range(0, width, BLOCK):
                here = slice(at, at + BLOCK)
                moved = dot(order, src[:, here], (1, 0)).astype(jnp.bfloat16)
                dst[:, here] = moved
                for group, send in enumerate((send_0, send_1)):
                    send[place * edge : (place + 1) * edge, here] = moved[group * LANES : group * LANES + edge]
        for copy, src, sends in zip(copies[2:], (k_ref, v_ref), ((k_0, k_1), (v_0, v_1))):
            copy.wait()
            for slot, send in enumerate(sends):
                start = pl.multiple_of(slot_side("lat", slot) * (own - lat_edge), 16)
                send[...] = src[pl.ds(start, lat_edge), :]

    operands = [
        pltpu.with_memory_space_constraint(x, pltpu.HBM) for x in (queries, out_grad, key_field, value_field)
    ]
    return call(
        kernel, "pack_queries", operands,
        [low(own, width)] * 2 + [low(2 * edge, width), low(2 * edge + 16, width)] + [low(own, width)] * 2 + [low(lat_edge, width)] * 4,
        [pltpu.VMEM((own, width), jnp.bfloat16)] * 2 + [pltpu.SemaphoreType.DMA((4,))],
        ins=[HBM_SPEC] * 4,
    )


def own_scores(qp, gp, key_field, value_field, rows, cols, count):
    own, width = rows * cols, key_field.shape[1]

    def kernel(q_ref, g_ref, k_ref, v_ref, kp_ref, vp_ref, out_0, out_1, s_ref, d_ref, bias):
        order = selection(*own_query_cell(down(own), rows, cols), rows, cols)
        for src, dst in ((k_ref, kp_ref), (v_ref, vp_ref)):
            for at in range(0, width, BLOCK):
                here = slice(at, at + BLOCK)
                dst[:, here] = dot(order, src[:, here], (1, 0)).astype(jnp.bfloat16)
        bias[...] = bias_of(
            own_query_cell(down(own), rows, cols), own_query_cell(across(own), rows, cols), rows
        )
        for out in (out_0, out_1):
            out[...] = jnp.zeros_like(out)
        for head in range(count):
            lanes = lanes_of(head)
            s_ref[head] = dot(kp_ref[:, lanes], q_ref[:, lanes], (1, 1)) * (SCORE_SCALE * LOG2E) + bias[...]
            d_ref[head] = dot(vp_ref[:, lanes], g_ref[:, lanes], (1, 1))
            put_stats((out_0, out_1), head, part_stats(s_ref[head], d_ref[head]), count)

    return call(
        kernel, "own_scores", (qp, gp, key_field, value_field),
        [low(own, width)] * 2 + [full(stat_rows(count), LANES)] * 2 + [full(count, own, own)] * 2,
        [pltpu.VMEM((own, own), jnp.float32)],
    )


def put_stats(outs, head, stats, count):
    for out, half in zip(outs, (LOW, HIGH)):
        for at, stat in zip((head, count + head), stats):
            out[at : at + 1, :] = stat[:, half]


def halo_head(ref, edge, part, head):
    rows = ref[part * edge : (part + 1) * edge, lanes_of(head)]
    return jnp.concatenate([rows, jnp.zeros((LANES - edge, HEAD_DIM), jnp.bfloat16)], axis=0)


def near_keys(group, own_ref, lat_refs, head):
    lanes, edge = lanes_of(head), lat_refs[0].shape[0]
    pieces = [own_ref[group * LANES : group * LANES + edge, lanes]]
    return jnp.concatenate(pieces + [ref[:, lanes] for ref in lat_refs], axis=0)


def every_key(own_ref, lat_refs, head):
    lanes = lanes_of(head)
    return jnp.concatenate([ref[:, lanes] for ref in (own_ref, *lat_refs)], axis=0)


def fill_bias(bias, own_position, queries, rows, cols):
    at, edge = own_position.shape[0], RADIUS * cols
    bias[:at, :] = bias_of(own_query_cell(own_position, rows, cols), queries, rows)
    for slot in (0, 1):
        here = slice(at + slot * edge, at + (slot + 1) * edge)
        bias[here, :] = bias_of(lat_key_cell(slot, down(edge), rows, cols), queries, rows)


LOW, HIGH = slice(0, LANES), slice(LANES, 2 * LANES)
SCORE_SCALE = 1.0 / math.sqrt(HEAD_DIM)


def part_stats(scores, weight_grad):
    peak = jnp.max(scores, axis=0, keepdims=True)
    weights = jnp.exp2(scores - peak)
    total = jnp.sum(weights, axis=0, keepdims=True)
    dotted = jnp.sum(weights * weight_grad, axis=0, keepdims=True)
    return peak + jnp.log(total) * LOG2E, dotted / total


def stat_rows(count):
    return -(-2 * count // 8) * 8


def lat_scores(qp, gp, lat, stats, rows, cols, count):
    own, lat_edge = rows * cols, RADIUS * cols

    def kernel(q_ref, g_ref, k_0, k_1, v_0, v_1, before_0, before_1, out_0, out_1, s_ref, d_ref, bias, part_0, part_1):
        queries = own_query_cell(across(own), rows, cols)
        for slot in (0, 1):
            cells = lat_key_cell(slot, down(lat_edge), rows, cols)
            bias[slot * lat_edge : (slot + 1) * lat_edge, :] = bias_of(cells, queries, rows)
        for head in range(count):
            lanes = lanes_of(head)
            key, value = (
                jnp.concatenate([ref[:, lanes] for ref in pair], axis=0) for pair in ((k_0, k_1), (v_0, v_1))
            )
            s_ref[head] = dot(key, q_ref[:, lanes], (1, 1)) * (SCORE_SCALE * LOG2E) + bias[...]
            d_ref[head] = dot(value, g_ref[:, lanes], (1, 1))
            put_stats((part_0, part_1), head, part_stats(s_ref[head], d_ref[head]), count)
        for out, part, before in ((out_0, part_0, before_0), (out_1, part_1, before_1)):
            out[...] = jnp.zeros_like(out)
            out[:count, :], out[count : 2 * count, :] = stats_of(part, before, count)

    return call(
        kernel, "lat_scores", (qp, gp, *lat, *stats),
        [full(stat_rows(count), LANES)] * 2 + [full(count, 2 * lat_edge, own)] * 2,
        [pltpu.VMEM((2 * lat_edge, own), jnp.float32)] + [pltpu.VMEM((stat_rows(count), LANES), jnp.float32)] * 2,
    )


def combined(mine, theirs):
    (a, delta_a), (b, delta_b) = mine, theirs
    peak = jnp.maximum(a, b)
    part_a, part_b = jnp.exp2(a - peak), jnp.exp2(b - peak)
    total = part_a + part_b
    return peak + jnp.log(total) * LOG2E, (part_a * delta_a + part_b * delta_b) / total


def halo_part(group, halo, mask, kp, vp, lat, rows, cols, count):
    edge = RADIUS * rows
    near = edge + 2 * RADIUS * cols

    def kernel(halo_ref, bias, k_ref, v_ref, k_0, k_1, v_0, v_1, out, s_ref, d_ref):
        out[...] = jnp.zeros_like(out)
        for head in range(count):
            key = near_keys(group, k_ref, (k_0, k_1), head)
            value = near_keys(group, v_ref, (v_0, v_1), head)
            s_ref[head] = dot(key, halo_head(halo_ref, edge, 0, head), (1, 1)) * (SCORE_SCALE * LOG2E) + bias[...]
            d_ref[head] = dot(value, halo_head(halo_ref, edge, 1, head), (1, 1))
            log_total, delta = part_stats(s_ref[head], d_ref[head])
            out[head : head + 1, :] = log_total
            out[count + head : count + head + 1, :] = delta

    return call(
        kernel, f"halo_part_{group}", (halo, mask, kp, vp, *lat),
        [full(stat_rows(count), LANES)] + [full(count, near, LANES)] * 2,
    )


def halo_rest(group, mine, theirs, scores, weight_grad, kp, lat, rows, cols, count):
    edge = RADIUS * rows

    def kernel(m, t, s_ref, d_ref, k_ref, k_0, k_1, out, p_ref, g_ref):
        logs, deltas = stats_of(m, t, count)
        for head in range(count):
            row = slice(head, head + 1)
            p_ref[head], grad = gradients(s_ref[head], d_ref[head], logs[row], deltas[row])
            g_ref[head] = grad
            query_grad = dot(grad, near_keys(group, k_ref, (k_0, k_1), head), (0, 0)) * SCORE_SCALE
            out[:, lanes_of(head)] = query_grad[:edge].astype(jnp.bfloat16)

    return call(
        kernel, f"halo_rest_{group}", (mine, theirs, scores, weight_grad, kp, *lat),
        [low(edge, count * HEAD_DIM)] + [low(count, *scores.shape[1:])] * 2,
    )


def halo_scores(group, halo, own_stat, kp, vp, lat, rows, cols, count):
    edge = RADIUS * rows
    near = edge + 2 * RADIUS * cols

    def kernel(halo_ref, stat, k_ref, v_ref, k_0, k_1, v_0, v_1, out, s_ref, d_ref, other, bias):
        queries = halo_query_cell(across(LANES, group * LANES), rows, cols)
        fill_bias(bias, down(edge) + group * LANES, queries, rows, cols)
        queries = halo_query_cell(across(LANES, (1 - group) * LANES), rows, cols)
        fill_bias(other, down(edge) + (1 - group) * LANES, queries, rows, cols)
        out[:, LOW] = stat[...]
        out[:, HIGH] = jnp.zeros((out.shape[0], LANES), jnp.float32)
        for head in range(count):
            key = near_keys(group, k_ref, (k_0, k_1), head)
            value = near_keys(group, v_ref, (v_0, v_1), head)
            s_ref[head] = dot(key, halo_head(halo_ref, edge, 0, head), (1, 1)) * (SCORE_SCALE * LOG2E) + bias[...]
            d_ref[head] = dot(value, halo_head(halo_ref, edge, 1, head), (1, 1))
            log_total, delta = part_stats(s_ref[head], d_ref[head])
            out[head : head + 1, HIGH] = log_total
            out[count + head : count + head + 1, HIGH] = delta

    return call(
        kernel, f"halo_scores_{group}", (halo, own_stat, kp, vp, *lat),
        [full(stat_rows(count), 2 * LANES)] + [full(count, near, LANES)] * 2 + [full(near, LANES)],
        [pltpu.VMEM((near, LANES), jnp.float32)],
    )


def halo_finish(group, mine, theirs, scores, weight_grad, kp, lat, rows, cols, count):
    edge = RADIUS * rows

    def kernel(m, t, s_ref, d_ref, k_ref, k_0, k_1, out, final, p_ref, g_ref):
        final[...] = jnp.zeros_like(final)
        logs, deltas = combined(*((x[:count, half], x[count : 2 * count, half]) for x, half in ((m, LOW), (t, HIGH))))
        final[:count, :] = logs
        final[count : 2 * count, :] = deltas
        logs, deltas = combined(*((x[:count, half], x[count : 2 * count, half]) for x, half in ((m, HIGH), (t, LOW))))
        for head in range(count):
            row = slice(head, head + 1)
            p_ref[head], grad = gradients(s_ref[head], d_ref[head], logs[row], deltas[row])
            g_ref[head] = grad
            query_grad = dot(grad, near_keys(group, k_ref, (k_0, k_1), head), (0, 0)) * SCORE_SCALE
            out[:, lanes_of(head)] = query_grad[:edge].astype(jnp.bfloat16)

    return call(
        kernel, f"halo_finish_{group}", (mine, theirs, scores, weight_grad, kp, *lat),
        [low(edge, count * HEAD_DIM), full(stat_rows(count), LANES)] + [low(count, *scores.shape[1:])] * 2,
    )


def gradients(scores, weight_grad, log_total, delta):
    weights = jnp.exp2(scores - log_total)
    return weights.astype(jnp.bfloat16), (weights * (weight_grad - delta)).astype(jnp.bfloat16)


def stats_of(mine, theirs, count):
    return combined(*((x[:count, :], x[count : 2 * count, :]) for x in (mine, theirs)))


def lat_grads(qp, gp, halo, stats_0, mine, theirs, scores, weight_grad, lows, rows, cols, count):
    own, width, edge, lat_edge = rows * cols, count * HEAD_DIM, RADIUS * rows, RADIUS * cols

    def kernel(
        q_ref, g_ref, h_0, h_1, stat, m, t, s_ref, d_ref, p_0, l_0, p_1, l_1, out_0, out_1, final, lat_low
    ):
        final[...] = jnp.zeros_like(final)
        final[:count, :], final[count : 2 * count, :] = stats_of(m, t, count)
        for head in range(count):
            lanes = lanes_of(head)
            logs, deltas = (
                jnp.concatenate([ref[at : at + 1, :] for ref in (stat, final)], axis=1) for at in (head, count + head)
            )
            weights, grad = gradients(s_ref[head], d_ref[head], logs, deltas)
            lat_low[head] = grad
            sides = ((grad, (l_0, l_1), q_ref, SCORE_SCALE), (weights, (p_0, p_1), g_ref, 1.0))
            for part, (low_lat, low_halo, own_ref, scale) in enumerate(sides):
                every = [own_ref[:, lanes]] + [halo_head(h, edge, part, head) for h in (h_0, h_1)]
                met = jnp.concatenate([low_lat] + [x[head, edge:, :] for x in low_halo], axis=1)
                outside = (dot(met, jnp.concatenate(every, axis=0), (1, 0)) * scale).astype(jnp.bfloat16)
                for slot, out in enumerate((out_0, out_1)):
                    out[part * lat_edge : (part + 1) * lat_edge, lanes] = outside[
                        slot * lat_edge : (slot + 1) * lat_edge
                    ]

    return call(
        kernel, "lat_grads", (qp, gp, *halo, stats_0, mine, theirs, scores, weight_grad, *lows[0], *lows[1]),
        [low(2 * lat_edge, width)] * 2 + [full(stat_rows(count), LANES), low(count, 2 * lat_edge, own)],
    )


def own_grads(qp, gp, halo, stats, lat_low, scores, weight_grad, lows, kp, lat, rows, cols, count):
    own, width, edge = rows * cols, count * HEAD_DIM, RADIUS * rows

    def kernel(
        q_ref, g_ref, h_0, h_1, stat_0, stat_1, lat_ref, s_ref, d_ref, p_0, l_0, p_1, l_1, k_ref, k_0, k_1,
        dq_ref, dk_ref, dv_ref, sums,
    ):
        for head in range(count):
            lanes = lanes_of(head)
            logs, deltas = (
                jnp.concatenate([ref[at : at + 1, :] for ref in (stat_0, stat_1)], axis=1)
                for at in (head, count + head)
            )
            own_p, own_l = gradients(s_ref[head], d_ref[head], logs, deltas)
            every = jnp.concatenate([own_l, lat_ref[head]], axis=0)
            sums[0, :, lanes] = dot(every, every_key(k_ref, (k_0, k_1), head), (0, 0)) * SCORE_SCALE
            sides = ((own_l, (l_0, l_1), q_ref, SCORE_SCALE), (own_p, (p_0, p_1), g_ref, 1.0))
            for part, (low_own, low_halo, own_ref, scale) in enumerate(sides):
                inside = dot(low_own, own_ref[:, lanes], (1, 0))
                for group, (x, h) in enumerate(zip(low_halo, (h_0, h_1))):
                    at = group * LANES
                    near = inside[at : at + edge] + dot(x[head, :edge, :], halo_head(h, edge, part, head), (1, 0))
                    sums[1 + part, at : at + edge, lanes] = near * scale
                    sums[1 + part, at + edge : at + LANES, lanes] = inside[at + edge : at + LANES] * scale
        order = restore(rows, cols)
        twice = jnp.concatenate([order, order], axis=1)
        for place, result in enumerate((dq_ref, dk_ref, dv_ref)):
            for at in range(0, width, BLOCK):
                value = sums[place, :, at : at + BLOCK]
                high = value.astype(jnp.bfloat16)
                rest = (value - high.astype(jnp.float32)).astype(jnp.bfloat16)
                result[:, at : at + BLOCK] = dot(twice, jnp.concatenate([high, rest], axis=0), (1, 0))

    return call(
        kernel, "own_grads",
        (qp, gp, *halo, *stats, lat_low, scores, weight_grad, *lows[0], *lows[1], kp, *lat),
        [full(own, width)] * 3, [pltpu.VMEM((3, own, width), jnp.float32)],
    )


def restore(rows, cols):
    own = rows * cols
    row, col = own_query_cell(across(own), rows, cols)
    return jnp.where(down(own) == row * cols + col, 1.0, 0.0).astype(jnp.bfloat16)


def finish(query_grad, back, key_grad, value_grad, lat_back, rows, cols, count):
    own, width, edge, lat_edge = rows * cols, count * HEAD_DIM, RADIUS * rows, RADIUS * cols

    def kernel(dq_ref, b_0, b_1, dk_ref, dv_ref, a_1, a_0, out_q, out_k, out_v, done_q, done_k, done_v, sems):
        copies = []

        def write(done, out):
            copies.append(pltpu.make_async_copy(done, out, sems.at[len(copies)]))
            copies[-1].start()

        middle = slice(lat_edge, own - lat_edge)
        for part, (grad, done, out) in enumerate(((dk_ref, done_k, out_k), (dv_ref, done_v, out_v))):
            done[middle, :] = grad[middle, :].astype(jnp.bfloat16)
            for slot, arrived in enumerate((a_0, a_1)):
                start = pl.multiple_of(slot_side("lat", slot) * (own - lat_edge), 16)
                added = arrived[part * lat_edge : (part + 1) * lat_edge, :].astype(jnp.float32)
                done[pl.ds(start, lat_edge), :] = (grad[pl.ds(start, lat_edge), :] + added).astype(jnp.bfloat16)
            write(done, out)
        position = across(2 * edge)
        place = jnp.where(position < edge, position, position - edge + LANES)
        row, col = own_query_cell(place, rows, cols)
        spread = jnp.where(down(own) == row * cols + col, 1.0, 0.0).astype(jnp.bfloat16)
        for at in range(0, width, BLOCK):
            lanes = slice(at, at + BLOCK)
            arrived = jnp.concatenate([b_0[:, lanes], b_1[:, lanes]], axis=0)
            done_q[:, lanes] = (dq_ref[:, lanes] + dot(spread, arrived, (1, 0))).astype(jnp.bfloat16)
        write(done_q, out_q)
        for copy in copies:
            copy.wait()

    return call(
        kernel, "finish", (query_grad, *back, key_grad, value_grad, *lat_back), [low(own, width)] * 3,
        [pltpu.VMEM((own, width), jnp.bfloat16)] * 3 + [pltpu.SemaphoreType.DMA((3,))],
        outs=[HBM_SPEC] * 3,
    )


def swap(axis, slot, wrap, array):
    count = lax.axis_size(axis)
    pairs = []
    for lower in range(slot, count if wrap else count - 1, 2):
        upper = (lower + 1) % count
        pairs += [(lower, upper), (upper, lower)]
    return lax.ppermute(array, axis, pairs)


def swap_lon(slot, array):
    return swap("lon", 1 - slot, True, array)


def swap_lat(slot, array):
    return swap("lat", slot, False, array)


def after(value, *earlier):
    return lax.optimization_barrier((value, *earlier))[0]


def held(value, *earlier, flops=1 << 33):
    spec = pl.BlockSpec(memory_space=pl.ANY)
    return call(
        lambda *refs: None, "held", (value, *earlier), [jax.ShapeDtypeStruct(value.shape, value.dtype)],
        flops=flops, aliases={0: 0}, ins=[spec] * (1 + len(earlier)), outs=[spec],
    )[0]


def shards(queries, key_field, value_field, out_grad):
    rows, cols, width = queries.shape
    own = rows * cols
    flat = lambda x: x.reshape(own, width)
    queries, key_field, value_field, out_grad = map(flat, (queries, key_field, value_field, out_grad))
    size = (rows, cols, width // HEAD_DIM)

    qp, gp, *sends = pack_queries(queries, out_grad, key_field, value_field, *size)
    sends, (key_field, value_field), edges = sends[:2], sends[2:4], sends[4:]
    halo = [swap_lon(slot, send) for slot, send in enumerate(sends)]
    lat = [swap_lat(place & 1, edge) for place, edge in enumerate(edges)]
    kp, vp, *stats, own_s, own_d = own_scores(qp, gp, key_field, value_field, *size)
    *own_stat, lat_s, lat_d = lat_scores(qp, gp, lat, stats, *size)
    theirs_1 = swap_lon(1, own_stat[1])

    mine_0, *scores_0, mask_1 = halo_scores(0, halo[0], own_stat[0], kp, vp, lat, *size)
    theirs_0 = swap_lon(0, mine_0)
    part_1, *scores_1 = halo_part(1, after(halo[1], mine_0), mask_1, kp, vp, lat, *size)
    other_1 = held(swap_lon(1, part_1))
    theirs_0 = held(theirs_0, part_1, flops=1 << 29)
    result_0, stats_0, *lows_0 = halo_finish(0, mine_0, theirs_0, *scores_0, kp, lat[:2], *size)
    theirs_1 = held(theirs_1, result_0, flops=1 << 29)
    result_1, *lows_1 = halo_rest(1, part_1, theirs_1, *scores_1, kp, lat[:2], *size)
    back_1 = swap_lon(1, result_1)
    *lat_back, stats_1, lat_low = lat_grads(
        qp, gp, halo, stats_0, own_stat[1], other_1, lat_s, lat_d, (lows_0, lows_1), *size
    )
    dq, dk, dv = own_grads(
        qp, gp, halo, (stats_0, stats_1), lat_low, own_s, own_d, (lows_0, lows_1), kp, lat[:2], *size
    )
    back = [swap_lon(0, held(result_0, lat_back[1], flops=1 << 29)), back_1]
    lat_back = [swap_lat(slot, lat_back[slot]) for slot in (1, 0)]
    outs = finish(dq, back, held(dk), dv, lat_back, *size)
    shape = (rows, cols, width)
    return tuple(x.reshape(shape) for x in outs)


def solution(mesh):
    spec = P("lat", "lon", None)
    return jax.shard_map(
        shards, mesh=mesh, in_specs=(spec,) * 4, out_specs=(spec,) * 3, check_vma=False
    )
```

```python
import math

import jax
import jax.numpy as jnp
from jax import lax
from jax.experimental import pallas as pl
from jax.experimental.pallas import tpu as pltpu
from jax.sharding import PartitionSpec as P

HEAD_DIM = 128
WINDOW = 13
RADIUS = WINDOW // 2
LANES = 128
MASKED = -1e30
LOG2E = math.log2(math.e)
VMEM_BYTES = 16 * 1024 * 1024


def split(index, width):
    if width & (width - 1) == 0:
        whole = index >> (width.bit_length() - 1)
    else:
        whole = (index * ((1 << 12) // width + 1)) >> 12
    return whole, index - whole * width


def odd(axis):
    return lax.axis_index(axis) & 1


def slot_side(axis, slot):
    parity = odd(axis)
    return parity if slot == (0 if axis == "lon" else 1) else 1 - parity


def own_query_cell(position, rows, cols):
    edge = rows * RADIUS
    group = position >> 7
    place = position & (LANES - 1)
    side = jnp.where(group == 0, slot_side("lon", 0), slot_side("lon", 1))
    row_a, col_a = split(place, RADIUS)
    inner = cols - 2 * RADIUS
    row_b, col_b = split(place - edge + (LANES - edge) * group, inner)
    at_edge = place < edge
    row = jnp.where(at_edge, row_a, row_b)
    col = jnp.where(at_edge, side * (cols - RADIUS) + col_a, RADIUS + col_b)
    return row, col


def halo_query_cell(position, rows, cols):
    edge = rows * RADIUS
    group = position >> 7
    place = position & (LANES - 1)
    side = jnp.where(group == 0, slot_side("lon", 0), slot_side("lon", 1))
    row, col = split(place, RADIUS)
    col = jnp.where(side == 1, cols, -RADIUS) + col
    col = jnp.where(place < edge, col, 1 << 12)
    return row, col


def lat_key_cell(slot, position, rows, cols):
    row, col = split(position, cols)
    return row + jnp.where(slot_side("lat", slot) == 1, rows, -RADIUS), col


def bias_of(key_cells, query_cells, rows):
    total_rows = rows * lax.axis_size("lat")
    first = rows * lax.axis_index("lat")
    key_row, key_col = key_cells
    query_row, query_col = query_cells
    start = jnp.clip(first + query_row - RADIUS, 0, total_rows - WINDOW)
    from_start = first + key_row - start
    inside = (from_start >= 0) & (from_start < WINDOW)
    inside = inside & (jnp.abs(key_col - query_col) <= RADIUS)
    return jnp.where(inside, 0.0, MASKED)


def down(count):
    return lax.broadcasted_iota(jnp.int32, (count, 1), 0)


def across(count, start=0):
    return lax.broadcasted_iota(jnp.int32, (1, count), 1) + start


def dot(a, b, contract):
    return lax.dot_general(a, b, ((contract[:1], contract[1:]), ((), ())), preferred_element_type=jnp.float32)


def call(kernel, name, operands, out_shapes, scratch=(), flops=0, aliases=None, outs=None, ins=None):
    return pl.pallas_call(
        kernel,
        name=name,
        in_specs=ins or [VMEM_SPEC] * len(operands),
        out_specs=outs or [VMEM_SPEC] * len(out_shapes),
        out_shape=out_shapes,
        scratch_shapes=scratch,
        input_output_aliases=aliases or {},
        compiler_params=pltpu.CompilerParams(vmem_limit_bytes=VMEM_BYTES),
        cost_estimate=pl.CostEstimate(flops=flops, bytes_accessed=0, transcendentals=0),
    )(*operands)


def low(*shape):
    return jax.ShapeDtypeStruct(shape, jnp.bfloat16)


def full(*shape):
    return jax.ShapeDtypeStruct(shape, jnp.float32)


def lanes_of(head, count=1):
    return slice(head * HEAD_DIM, (head + count) * HEAD_DIM)


def selection(row, col, rows, cols):
    source = across(rows * cols)
    return jnp.where(source == row * cols + col, 1.0, 0.0).astype(jnp.bfloat16)


HBM_SPEC, VMEM_SPEC = pl.BlockSpec(memory_space=pltpu.HBM), pl.BlockSpec(memory_space=pltpu.VMEM)
BLOCK = 2 * HEAD_DIM


def pack_queries(queries, out_grad, key_field, value_field, rows, cols, count):
    own, edge, width = rows * cols, rows * RADIUS, count * HEAD_DIM
    lat_edge = RADIUS * cols

    def kernel(
        q_hbm, g_hbm, k_hbm, v_hbm, qp_ref, gp_ref, send_0, send_1, k_ref, v_ref, k_0, k_1, v_0, v_1, q_ref, g_ref, sems
    ):
        copies = [
            pltpu.make_async_copy(src, dst, sems.at[i])
            for i, (src, dst) in enumerate(
                ((q_hbm, q_ref), (g_hbm, g_ref), (k_hbm, k_ref), (v_hbm, v_ref))
            )
        ]
        for copy in copies:
            copy.start()
        order = selection(*own_query_cell(down(own), rows, cols), rows, cols)
        for place, (src, dst) in enumerate(((q_ref, qp_ref), (g_ref, gp_ref))):
            copies[place].wait()
            for at in range(0, width, BLOCK):
                here = slice(at, at + BLOCK)
                moved = dot(order, src[:, here], (1, 0)).astype(jnp.bfloat16)
                dst[:, here] = moved
                for group, send in enumerate((send_0, send_1)):
                    send[place * edge : (place + 1) * edge, here] = moved[group * LANES : group * LANES + edge]
        for copy, src, sends in zip(copies[2:], (k_ref, v_ref), ((k_0, k_1), (v_0, v_1))):
            copy.wait()
            for slot, send in enumerate(sends):
                start = pl.multiple_of(slot_side("lat", slot) * (own - lat_edge), 16)
                send[...] = src[pl.ds(start, lat_edge), :]

    operands = [
        pltpu.with_memory_space_constraint(x, pltpu.HBM) for x in (queries, out_grad, key_field, value_field)
    ]
    return call(
        kernel, "pack_queries", operands,
        [low(own, width)] * 2 + [low(2 * edge, width), low(2 * edge + 16, width)] + [low(own, width)] * 2 + [low(lat_edge, width)] * 4,
        [pltpu.VMEM((own, width), jnp.bfloat16)] * 2 + [pltpu.SemaphoreType.DMA((4,))],
        ins=[HBM_SPEC] * 4,
    )


def own_scores(qp, gp, key_field, value_field, rows, cols, count):
    own, width = rows * cols, key_field.shape[1]

    def kernel(q_ref, g_ref, k_ref, v_ref, kp_ref, vp_ref, out_0, out_1, s_ref, d_ref, bias):
        order = selection(*own_query_cell(down(own), rows, cols), rows, cols)
        for src, dst in ((k_ref, kp_ref), (v_ref, vp_ref)):
            for at in range(0, width, BLOCK):
                here = slice(at, at + BLOCK)
                dst[:, here] = dot(order, src[:, here], (1, 0)).astype(jnp.bfloat16)
        bias[...] = bias_of(
            own_query_cell(down(own), rows, cols), own_query_cell(across(own), rows, cols), rows
        )
        for out in (out_0, out_1):
            out[...] = jnp.zeros_like(out)
        for head in range(count):
            lanes = lanes_of(head)
            s_ref[head] = dot(kp_ref[:, lanes], q_ref[:, lanes], (1, 1)) * (SCORE_SCALE * LOG2E) + bias[...]
            d_ref[head] = dot(vp_ref[:, lanes], g_ref[:, lanes], (1, 1))
            put_stats((out_0, out_1), head, part_stats(s_ref[head], d_ref[head]), count)

    return call(
        kernel, "own_scores", (qp, gp, key_field, value_field),
        [low(own, width)] * 2 + [full(stat_rows(count), LANES)] * 2 + [full(count, own, own)] * 2,
        [pltpu.VMEM((own, own), jnp.float32)],
    )


def put_stats(outs, head, stats, count):
    for out, half in zip(outs, (LOW, HIGH)):
        for at, stat in zip((head, count + head), stats):
            out[at : at + 1, :] = stat[:, half]


def halo_head(ref, edge, part, head):
    rows = ref[part * edge : (part + 1) * edge, lanes_of(head)]
    return jnp.concatenate([rows, jnp.zeros((LANES - edge, HEAD_DIM), jnp.bfloat16)], axis=0)


def near_keys(group, own_ref, lat_refs, head):
    lanes, edge = lanes_of(head), lat_refs[0].shape[0]
    pieces = [own_ref[group * LANES : group * LANES + edge, lanes]]
    return jnp.concatenate(pieces + [ref[:, lanes] for ref in lat_refs], axis=0)


def every_key(own_ref, lat_refs, head):
    lanes = lanes_of(head)
    return jnp.concatenate([ref[:, lanes] for ref in (own_ref, *lat_refs)], axis=0)


def fill_bias(bias, own_position, queries, rows, cols):
    at, edge = own_position.shape[0], RADIUS * cols
    bias[:at, :] = bias_of(own_query_cell(own_position, rows, cols), queries, rows)
    for slot in (0, 1):
        here = slice(at + slot * edge, at + (slot + 1) * edge)
        bias[here, :] = bias_of(lat_key_cell(slot, down(edge), rows, cols), queries, rows)


LOW, HIGH = slice(0, LANES), slice(LANES, 2 * LANES)
SCORE_SCALE = 1.0 / math.sqrt(HEAD_DIM)


def part_stats(scores, weight_grad):
    peak = jnp.max(scores, axis=0, keepdims=True)
    weights = jnp.exp2(scores - peak)
    total = jnp.sum(weights, axis=0, keepdims=True)
    dotted = jnp.sum(weights * weight_grad, axis=0, keepdims=True)
    return peak + jnp.log(total) * LOG2E, dotted / total


def stat_rows(count):
    return -(-2 * count // 8) * 8


def lat_scores(qp, gp, lat, stats, rows, cols, count):
    own, lat_edge = rows * cols, RADIUS * cols

    def kernel(q_ref, g_ref, k_0, k_1, v_0, v_1, before_0, before_1, out_0, out_1, s_ref, d_ref, bias, part_0, part_1):
        queries = own_query_cell(across(own), rows, cols)
        for slot in (0, 1):
            cells = lat_key_cell(slot, down(lat_edge), rows, cols)
            bias[slot * lat_edge : (slot + 1) * lat_edge, :] = bias_of(cells, queries, rows)
        for head in range(count):
            lanes = lanes_of(head)
            key, value = (
                jnp.concatenate([ref[:, lanes] for ref in pair], axis=0) for pair in ((k_0, k_1), (v_0, v_1))
            )
            s_ref[head] = dot(key, q_ref[:, lanes], (1, 1)) * (SCORE_SCALE * LOG2E) + bias[...]
            d_ref[head] = dot(value, g_ref[:, lanes], (1, 1))
            put_stats((part_0, part_1), head, part_stats(s_ref[head], d_ref[head]), count)
        for out, part, before in ((out_0, part_0, before_0), (out_1, part_1, before_1)):
            out[...] = jnp.zeros_like(out)
            out[:count, :], out[count : 2 * count, :] = stats_of(part, before, count)

    return call(
        kernel, "lat_scores", (qp, gp, *lat, *stats),
        [full(stat_rows(count), LANES)] * 2 + [full(count, 2 * lat_edge, own)] * 2,
        [pltpu.VMEM((2 * lat_edge, own), jnp.float32)] + [pltpu.VMEM((stat_rows(count), LANES), jnp.float32)] * 2,
    )


def combined(mine, theirs):
    (a, delta_a), (b, delta_b) = mine, theirs
    peak = jnp.maximum(a, b)
    part_a, part_b = jnp.exp2(a - peak), jnp.exp2(b - peak)
    total = part_a + part_b
    return peak + jnp.log(total) * LOG2E, (part_a * delta_a + part_b * delta_b) / total


def halo_part(group, halo, mask, kp, vp, lat, rows, cols, count):
    edge = RADIUS * rows
    near = edge + 2 * RADIUS * cols

    def kernel(halo_ref, bias, k_ref, v_ref, k_0, k_1, v_0, v_1, out, s_ref, d_ref):
        out[...] = jnp.zeros_like(out)
        for head in range(count):
            key = near_keys(group, k_ref, (k_0, k_1), head)
            value = near_keys(group, v_ref, (v_0, v_1), head)
            s_ref[head] = dot(key, halo_head(halo_ref, edge, 0, head), (1, 1)) * (SCORE_SCALE * LOG2E) + bias[...]
            d_ref[head] = dot(value, halo_head(halo_ref, edge, 1, head), (1, 1))
            log_total, delta = part_stats(s_ref[head], d_ref[head])
            out[head : head + 1, :] = log_total
            out[count + head : count + head + 1, :] = delta

    return call(
        kernel, f"halo_part_{group}", (halo, mask, kp, vp, *lat),
        [full(stat_rows(count), LANES)] + [full(count, near, LANES)] * 2,
    )


def halo_rest(group, mine, theirs, scores, weight_grad, kp, lat, rows, cols, count):
    edge = RADIUS * rows

    def kernel(m, t, s_ref, d_ref, k_ref, k_0, k_1, out, p_ref, g_ref):
        logs, deltas = stats_of(m, t, count)
        for head in range(count):
            row = slice(head, head + 1)
            p_ref[head], grad = gradients(s_ref[head], d_ref[head], logs[row], deltas[row])
            g_ref[head] = grad
            query_grad = dot(grad, near_keys(group, k_ref, (k_0, k_1), head), (0, 0)) * SCORE_SCALE
            out[:, lanes_of(head)] = query_grad[:edge].astype(jnp.bfloat16)

    return call(
        kernel, f"halo_rest_{group}", (mine, theirs, scores, weight_grad, kp, *lat),
        [low(edge, count * HEAD_DIM)] + [low(count, *scores.shape[1:])] * 2,
    )


def halo_scores(group, halo, own_stat, kp, vp, lat, rows, cols, count):
    edge = RADIUS * rows
    near = edge + 2 * RADIUS * cols

    def kernel(halo_ref, stat, k_ref, v_ref, k_0, k_1, v_0, v_1, out, s_ref, d_ref, other, bias):
        queries = halo_query_cell(across(LANES, group * LANES), rows, cols)
        fill_bias(bias, down(edge) + group * LANES, queries, rows, cols)
        queries = halo_query_cell(across(LANES, (1 - group) * LANES), rows, cols)
        fill_bias(other, down(edge) + (1 - group) * LANES, queries, rows, cols)
        out[:, LOW] = stat[...]
        out[:, HIGH] = jnp.zeros((out.shape[0], LANES), jnp.float32)
        for head in range(count):
            key = near_keys(group, k_ref, (k_0, k_1), head)
            value = near_keys(group, v_ref, (v_0, v_1), head)
            s_ref[head] = dot(key, halo_head(halo_ref, edge, 0, head), (1, 1)) * (SCORE_SCALE * LOG2E) + bias[...]
            d_ref[head] = dot(value, halo_head(halo_ref, edge, 1, head), (1, 1))
            log_total, delta = part_stats(s_ref[head], d_ref[head])
            out[head : head + 1, HIGH] = log_total
            out[count + head : count + head + 1, HIGH] = delta

    return call(
        kernel, f"halo_scores_{group}", (halo, own_stat, kp, vp, *lat),
        [full(stat_rows(count), 2 * LANES)] + [full(count, near, LANES)] * 2 + [full(near, LANES)],
        [pltpu.VMEM((near, LANES), jnp.float32)],
    )


def halo_finish(group, mine, theirs, scores, weight_grad, kp, lat, rows, cols, count):
    edge = RADIUS * rows

    def kernel(m, t, s_ref, d_ref, k_ref, k_0, k_1, out, final, p_ref, g_ref):
        final[...] = jnp.zeros_like(final)
        logs, deltas = combined(*((x[:count, half], x[count : 2 * count, half]) for x, half in ((m, LOW), (t, HIGH))))
        final[:count, :] = logs
        final[count : 2 * count, :] = deltas
        logs, deltas = combined(*((x[:count, half], x[count : 2 * count, half]) for x, half in ((m, HIGH), (t, LOW))))
        for head in range(count):
            row = slice(head, head + 1)
            p_ref[head], grad = gradients(s_ref[head], d_ref[head], logs[row], deltas[row])
            g_ref[head] = grad
            query_grad = dot(grad, near_keys(group, k_ref, (k_0, k_1), head), (0, 0)) * SCORE_SCALE
            out[:, lanes_of(head)] = query_grad[:edge].astype(jnp.bfloat16)

    return call(
        kernel, f"halo_finish_{group}", (mine, theirs, scores, weight_grad, kp, *lat),
        [low(edge, count * HEAD_DIM), full(stat_rows(count), LANES)] + [low(count, *scores.shape[1:])] * 2,
    )


def gradients(scores, weight_grad, log_total, delta):
    weights = jnp.exp2(scores - log_total)
    return weights.astype(jnp.bfloat16), (weights * (weight_grad - delta)).astype(jnp.bfloat16)


def stats_of(mine, theirs, count):
    return combined(*((x[:count, :], x[count : 2 * count, :]) for x in (mine, theirs)))


def lat_grads(qp, gp, halo, stats_0, mine, theirs, scores, weight_grad, lows, rows, cols, count):
    own, width, edge, lat_edge = rows * cols, count * HEAD_DIM, RADIUS * rows, RADIUS * cols

    def kernel(
        q_ref, g_ref, h_0, h_1, stat, m, t, s_ref, d_ref, p_0, l_0, p_1, l_1, out_0, out_1, final, lat_low
    ):
        final[...] = jnp.zeros_like(final)
        final[:count, :], final[count : 2 * count, :] = stats_of(m, t, count)
        for head in range(count):
            lanes = lanes_of(head)
            logs, deltas = (
                jnp.concatenate([ref[at : at + 1, :] for ref in (stat, final)], axis=1) for at in (head, count + head)
            )
            weights, grad = gradients(s_ref[head], d_ref[head], logs, deltas)
            lat_low[head] = grad
            sides = ((grad, (l_0, l_1), q_ref, SCORE_SCALE), (weights, (p_0, p_1), g_ref, 1.0))
            for part, (low_lat, low_halo, own_ref, scale) in enumerate(sides):
                every = [own_ref[:, lanes]] + [halo_head(h, edge, part, head) for h in (h_0, h_1)]
                met = jnp.concatenate([low_lat] + [x[head, edge:, :] for x in low_halo], axis=1)
                outside = (dot(met, jnp.concatenate(every, axis=0), (1, 0)) * scale).astype(jnp.bfloat16)
                for slot, out in enumerate((out_0, out_1)):
                    out[part * lat_edge : (part + 1) * lat_edge, lanes] = outside[
                        slot * lat_edge : (slot + 1) * lat_edge
                    ]

    return call(
        kernel, "lat_grads", (qp, gp, *halo, stats_0, mine, theirs, scores, weight_grad, *lows[0], *lows[1]),
        [low(2 * lat_edge, width)] * 2 + [full(stat_rows(count), LANES), low(count, 2 * lat_edge, own)],
    )


def own_grads(qp, gp, halo, stats, lat_low, scores, weight_grad, lows, kp, lat, rows, cols, count):
    own, width, edge = rows * cols, count * HEAD_DIM, RADIUS * rows

    def kernel(
        q_ref, g_ref, h_0, h_1, stat_0, stat_1, lat_ref, s_ref, d_ref, p_0, l_0, p_1, l_1, k_ref, k_0, k_1,
        dq_ref, dk_ref, dv_ref, spread, sums,
    ):
        for head in range(count):
            lanes = lanes_of(head)
            logs, deltas = (
                jnp.concatenate([ref[at : at + 1, :] for ref in (stat_0, stat_1)], axis=1)
                for at in (head, count + head)
            )
            own_p, own_l = gradients(s_ref[head], d_ref[head], logs, deltas)
            every = jnp.concatenate([own_l, lat_ref[head]], axis=0)
            sums[0, :, lanes] = dot(every, every_key(k_ref, (k_0, k_1), head), (0, 0)) * SCORE_SCALE
            sides = ((own_l, (l_0, l_1), q_ref, SCORE_SCALE), (own_p, (p_0, p_1), g_ref, 1.0))
            for part, (low_own, low_halo, own_ref, scale) in enumerate(sides):
                inside = dot(low_own, own_ref[:, lanes], (1, 0))
                for group, (x, h) in enumerate(zip(low_halo, (h_0, h_1))):
                    at = group * LANES
                    near = inside[at : at + edge] + dot(x[head, :edge, :], halo_head(h, edge, part, head), (1, 0))
                    sums[1 + part, at : at + edge, lanes] = near * scale
                    sums[1 + part, at + edge : at + LANES, lanes] = inside[at + edge : at + LANES] * scale
        position = across(2 * edge)
        place = jnp.where(position < edge, position, position - edge + LANES)
        row, col = own_query_cell(place, rows, cols)
        spread[...] = jnp.where(down(own) == row * cols + col, 1.0, 0.0).astype(jnp.bfloat16)
        order = restore(rows, cols)
        twice = jnp.concatenate([order, order], axis=1)
        for place, result in enumerate((dq_ref, dk_ref, dv_ref)):
            for at in range(0, width, BLOCK):
                value = sums[place, :, at : at + BLOCK]
                high = value.astype(jnp.bfloat16)
                rest = (value - high.astype(jnp.float32)).astype(jnp.bfloat16)
                result[:, at : at + BLOCK] = dot(twice, jnp.concatenate([high, rest], axis=0), (1, 0))

    return call(
        kernel, "own_grads",
        (qp, gp, *halo, *stats, lat_low, scores, weight_grad, *lows[0], *lows[1], kp, *lat),
        [full(own, width)] * 3 + [low(own, 2 * edge)], [pltpu.VMEM((3, own, width), jnp.float32)],
    )


def restore(rows, cols):
    own = rows * cols
    row, col = own_query_cell(across(own), rows, cols)
    return jnp.where(down(own) == row * cols + col, 1.0, 0.0).astype(jnp.bfloat16)


def finish(query_grad, spread, back, key_grad, value_grad, lat_back, rows, cols, count):
    own, width, edge, lat_edge = rows * cols, count * HEAD_DIM, RADIUS * rows, RADIUS * cols

    def kernel(dq_ref, spread, b_0, b_1, dk_ref, dv_ref, a_1, a_0, out_q, out_k, out_v, done_q, done_k, done_v, sems):
        copies = []

        def write(done, out):
            copies.append(pltpu.make_async_copy(done, out, sems.at[len(copies)]))
            copies[-1].start()

        middle = slice(lat_edge, own - lat_edge)
        for part, (grad, done, out) in enumerate(((dk_ref, done_k, out_k), (dv_ref, done_v, out_v))):
            done[middle, :] = grad[middle, :].astype(jnp.bfloat16)
            for slot, arrived in enumerate((a_0, a_1)):
                start = pl.multiple_of(slot_side("lat", slot) * (own - lat_edge), 16)
                added = arrived[part * lat_edge : (part + 1) * lat_edge, :].astype(jnp.float32)
                done[pl.ds(start, lat_edge), :] = (grad[pl.ds(start, lat_edge), :] + added).astype(jnp.bfloat16)
            write(done, out)
        for at in range(0, width, BLOCK):
            lanes = slice(at, at + BLOCK)
            arrived = jnp.concatenate([b_0[:, lanes], b_1[:, lanes]], axis=0)
            done_q[:, lanes] = (dq_ref[:, lanes] + dot(spread[...], arrived, (1, 0))).astype(jnp.bfloat16)
        write(done_q, out_q)
        for copy in copies:
            copy.wait()

    return call(
        kernel, "finish", (query_grad, spread, *back, key_grad, value_grad, *lat_back), [low(own, width)] * 3,
        [pltpu.VMEM((own, width), jnp.bfloat16)] * 3 + [pltpu.SemaphoreType.DMA((3,))],
        outs=[HBM_SPEC] * 3,
    )


def swap(axis, slot, wrap, array):
    count = lax.axis_size(axis)
    pairs = []
    for lower in range(slot, count if wrap else count - 1, 2):
        upper = (lower + 1) % count
        pairs += [(lower, upper), (upper, lower)]
    return lax.ppermute(array, axis, pairs)


def swap_lon(slot, array):
    return swap("lon", 1 - slot, True, array)


def swap_lat(slot, array):
    return swap("lat", slot, False, array)


def after(value, *earlier):
    return lax.optimization_barrier((value, *earlier))[0]


def held(value, *earlier, flops=1 << 33):
    spec = pl.BlockSpec(memory_space=pl.ANY)
    return call(
        lambda *refs: None, "held", (value, *earlier), [jax.ShapeDtypeStruct(value.shape, value.dtype)],
        flops=flops, aliases={0: 0}, ins=[spec] * (1 + len(earlier)), outs=[spec],
    )[0]


def shards(queries, key_field, value_field, out_grad):
    rows, cols, width = queries.shape
    own = rows * cols
    flat = lambda x: x.reshape(own, width)
    queries, key_field, value_field, out_grad = map(flat, (queries, key_field, value_field, out_grad))
    size = (rows, cols, width // HEAD_DIM)

    qp, gp, *sends = pack_queries(queries, out_grad, key_field, value_field, *size)
    sends, (key_field, value_field), edges = sends[:2], sends[2:4], sends[4:]
    halo = [swap_lon(slot, send) for slot, send in enumerate(sends)]
    lat = [swap_lat(place & 1, edge) for place, edge in enumerate(edges)]
    kp, vp, *stats, own_s, own_d = own_scores(qp, gp, key_field, value_field, *size)
    *own_stat, lat_s, lat_d = lat_scores(qp, gp, lat, stats, *size)
    theirs_1 = swap_lon(1, own_stat[1])

    mine_0, *scores_0, mask_1 = halo_scores(0, halo[0], own_stat[0], kp, vp, lat, *size)
    theirs_0 = swap_lon(0, mine_0)
    part_1, *scores_1 = halo_part(1, after(halo[1], mine_0), mask_1, kp, vp, lat, *size)
    other_1 = held(swap_lon(1, part_1))
    theirs_0 = held(theirs_0, part_1, flops=1 << 29)
    result_0, stats_0, *lows_0 = halo_finish(0, mine_0, theirs_0, *scores_0, kp, lat[:2], *size)
    theirs_1 = held(theirs_1, result_0, flops=1 << 29)
    result_1, *lows_1 = halo_rest(1, part_1, theirs_1, *scores_1, kp, lat[:2], *size)
    back_1 = swap_lon(1, result_1)
    *lat_back, stats_1, lat_low = lat_grads(
        qp, gp, halo, stats_0, own_stat[1], other_1, lat_s, lat_d, (lows_0, lows_1), *size
    )
    dq, dk, dv, spread = own_grads(
        qp, gp, halo, (stats_0, stats_1), lat_low, own_s, own_d, (lows_0, lows_1), kp, lat[:2], *size
    )
    back = [swap_lon(0, held(result_0, lat_back[1], flops=1 << 29)), back_1]
    lat_back = [swap_lat(slot, lat_back[slot]) for slot in (1, 0)]
    outs = finish(dq, spread, back, held(dk), dv, lat_back, *size)
    shape = (rows, cols, width)
    return tuple(x.reshape(shape) for x in outs)


def solution(mesh):
    spec = P("lat", "lon", None)
    return jax.shard_map(
        shards, mesh=mesh, in_specs=(spec,) * 4, out_specs=(spec,) * 3, check_vma=False
    )
```
